128 devices in a mesh: dp: 2 (over x_lo), ctx: 8 (over z, core), fsdp: 8 (over y, x_hi).
Axes of the slice: x: 4 (x_hi: 2, x_lo: 2; x = x_hi * 2 + x_lo), y: 4, z: 4, core: 2. Of those that a mesh axis runs over, the one named last changes fastest.
Arguments:
- hidden_in: bfloat16 [16, 1024, 1024], P(('dp', 'fsdp'), 'ctx'), may hold values from -6 to 6
- positions: int32 [16, 1024], P(('dp', 'fsdp')), may hold values from 0 to 1023, as said below
- cotangent: bfloat16 [16, 1024, 1024], P(('dp', 'fsdp'), 'ctx'), may hold values from -6 to 6
- attn_gain: float32 [1024], replicated, may hold values from 0.25 to 1.75
- w_query: bfloat16 [1024, 1024], P('fsdp'), may hold values from -0.1875 to 0.1875
- w_key: bfloat16 [1024, 512], P('fsdp'), may hold values from -0.1875 to 0.1875
- w_value: bfloat16 [1024, 512], P('fsdp'), may hold values from -0.1875 to 0.1875
- query_gain: float32 [64], replicated, may hold values from 0.25 to 1.75
- key_gain: float32 [64], replicated, may hold values from 0.25 to 1.75
- w_out: bfloat16 [1024, 1024], P('fsdp'), may hold values from -3 to 3
- ffn_gain: float32 [1024], replicated, may hold values from 0.25 to 1.75
- w_gate: bfloat16 [1024, 4608], P('fsdp'), may hold values from -0.1875 to 0.1875
- w_up: bfloat16 [1024, 4608], P('fsdp'), may hold values from -0.1875 to 0.1875
- w_down: bfloat16 [4608, 1024], P('fsdp'), may hold values from -0.09375 to 0.09375
Outputs:
- block_out: bfloat16 [16, 1024, 1024], P(('dp', 'fsdp'), 'ctx')
- grad_in: bfloat16 [16, 1024, 1024], P(('dp', 'fsdp'), 'ctx')
- grad_attn_gain: float32 [1024], replicated
- grad_w_query: float32 [1024, 1024], P('fsdp')
- grad_w_key: float32 [1024, 512], P('fsdp')
- grad_w_value: float32 [1024, 512], P('fsdp')
- grad_query_gain: float32 [64], replicated
- grad_key_gain: float32 [64], replicated
- grad_w_out: float32 [1024, 1024], P('fsdp')
- grad_ffn_gain: float32 [1024], replicated
- grad_w_gate: float32 [1024, 4608], P('fsdp')
- grad_w_up: float32 [1024, 4608], P('fsdp')
- grad_w_down: float32 [4608, 1024], P('fsdp')
The draws below stay inside these ranges and needn't reach their ends.
Inputs may be any that keep to these rules, and one draw needn't show every extreme that they name: Each row holds every position once. The 128 entries that start at each multiple of 128 are two blocks of 64 consecutive increasing positions: block b and block 15 - b, in either order, where block b holds positions b * 64 to (b + 1) * 64 - 1.
All inputs are finite; a program needn't handle non-finite values.
Results may differ from the reference program's by a relative error of at most 0.024.
Values may be sent and summed in bfloat16 or wider, within the bound.
No kernel may reach another device: no remote copies, remote signals or barrier semaphores. Data moves between devices by JAX's collectives and lax.ppermute only.
A program may use at most 192 MiB of HBM per device.

```python
import jax
import jax.numpy as jnp
from jax import lax

D = 1024
H = 16
KV = 8
HD = 64
FF = 4608
SEQ_LEN = 1024
SEQS = 16
TOK_DEV = 128
BLOCK = 64


def draw_positions(key, part):
    key = jax.random.fold_in(key, 11)
    pair_key, flip_key = jax.random.split(key)
    npairs = SEQ_LEN // TOK_DEV
    row_keys = jax.random.split(pair_key, SEQS)
    pair_ids = jax.vmap(lambda row_key: jax.random.permutation(row_key, npairs))(row_keys)
    flip_bits = jax.random.randint(flip_key, (SEQS, npairs), 0, 2)
    first_block = jnp.where(flip_bits == 0, pair_ids, 2 * npairs - 1 - pair_ids)
    second = 2 * npairs - 1 - first_block
    blocks = jnp.stack([first_block, second], axis=2).reshape(SEQS, 2 * npairs)
    offsets = jnp.arange(BLOCK, dtype=jnp.int32)
    return (blocks[:, :, None] * BLOCK + offsets[None, None, :]).reshape(SEQS, SEQ_LEN).astype(jnp.int32)


def steps_of(key, dims, cuts, low, high):
    def one(position, blocks):
        heights = jax.random.uniform(jax.random.fold_in(jax.random.fold_in(key, 6), position), (blocks,), jnp.float32, low / len(cuts), high / len(cuts))
        return jnp.repeat(jnp.exp(heights), dims[position] // blocks).reshape((-1,) + (1,) * (len(dims) - position - 1))

    factor_of = one(*cuts[0])
    for cut in cuts[1:]:
        factor_of = factor_of * one(*cut)
    return factor_of


def noise(rng, shape, spread, reach, shards=(), kind=jnp.bfloat16):
    values = spread * jax.random.normal(rng, shape, jnp.float32)
    if shards:
        values = values * steps_of(rng, shape, shards, -0.22, 0.18)
    return jnp.clip(values, -reach, reach).astype(kind)


def setup_inputs(seed: int = 0) -> dict:
    splits = jax.random.split(jax.random.key(seed), 15)
    return {
        "hidden_in": noise(splits[0], (SEQS, SEQ_LEN, D), 1.0, 6.0, ((0, 16), (1, 8))),
        "positions": draw_positions(jax.random.fold_in(splits[14], 71), 0),
        "cotangent": noise(splits[2], (SEQS, SEQ_LEN, D), 1.0, 6.0, ((0, 16), (1, 8))),
        "attn_gain": jnp.clip(1.0 + 0.15 * jax.random.normal(splits[3], (D,), jnp.float32), 0.25, 1.75),
        "w_query": noise(splits[4], (D, H * HD), D ** -0.5, 0.1875, ((0, 8),)),
        "w_key": noise(splits[5], (D, KV * HD), D ** -0.5, 0.1875, ((0, 8),)),
        "w_value": noise(splits[6], (D, KV * HD), D ** -0.5, 0.1875, ((0, 8),)),
        "query_gain": jnp.clip(1.0 + 0.15 * jax.random.normal(splits[7], (HD,), jnp.float32), 0.25, 1.75),
        "key_gain": jnp.clip(1.0 + 0.15 * jax.random.normal(splits[8], (HD,), jnp.float32), 0.25, 1.75),
        "w_out": noise(splits[9], (H * HD, D), (max(1, 4 * D // SEQ_LEN)) ** -0.5, 3.0, ((0, 8),)),
        "ffn_gain": jnp.clip(1.0 + 0.15 * jax.random.normal(splits[10], (D,), jnp.float32), 0.25, 1.75),
        "w_gate": noise(splits[11], (D, FF), D ** -0.5, 0.1875, ((0, 8),)),
        "w_up": noise(splits[12], (D, FF), D ** -0.5, 0.1875, ((0, 8),)),
        "w_down": noise(splits[13], (FF, D), FF ** -0.5, 0.09375, ((0, 8),)),
    }


NORM_EPSILON = 1e-05
ROPE_BASE = 1000000.0
MASKED_SCORE = -1e+30
HIGHEST_PRECISION = lax.Precision.HIGHEST

@jax.custom_vjp
def low(v):
    return lax.optimization_barrier(v.astype(jnp.bfloat16)).astype(jnp.float32)

@jax.custom_vjp
def low_back(v):
    return v

def low_keep(v):
    return (low(v), None)

def low_pass(kept, grad):
    return (grad,)

def back_keep(v):
    return (v, None)

def back_low(kept, grad):
    return (low(grad),)
low.defvjp(low_keep, low_pass)
low_back.defvjp(back_keep, back_low)

def matmul(left, right):
    return jnp.dot(left, right, preferred_element_type=jnp.float32, precision=HIGHEST_PRECISION)

def rms_scale(values):
    return lax.rsqrt(lax.optimization_barrier(jnp.mean(values * values, axis=-1, keepdims=True)) + NORM_EPSILON)

def rope_tables(places, head_size):
    half_width = head_size // 2
    pair_index = jnp.arange(half_width, dtype=jnp.float32)
    frequency = ROPE_BASE ** (-2.0 * pair_index / head_size)
    angles = places.astype(jnp.float32)[:, None] * frequency[None, :]
    return (jnp.cos(angles)[:, None, :], jnp.sin(angles)[:, None, :])

def rotate(values, cosine_table, sine_table):
    half_width = values.shape[-1] // 2
    front = values[..., :half_width]
    back_half = values[..., half_width:]
    return jnp.concatenate([front * cosine_table - back_half * sine_table, back_half * cosine_table + front * sine_table], axis=-1)

def forward(tokens, places, attn_gain, w_query, w_key, w_value, query_gain, key_gain, w_out, ffn_gain, w_gate, w_up, w_down):
    length = tokens.shape[0]
    head_size = query_gain.shape[0]
    query_heads = w_query.shape[1] // head_size
    key_heads = w_key.shape[1] // head_size
    group_size = query_heads // key_heads
    score_scale = head_size ** (-0.5)
    first_normed = low(tokens * rms_scale(tokens) * attn_gain)
    query_proj = low_back(matmul(first_normed, w_query)).reshape(length, query_heads, head_size)
    key_proj = low_back(matmul(first_normed, w_key)).reshape(length, key_heads, head_size)
    value_low = low(low_back(matmul(first_normed, w_value))).reshape(length, key_heads, head_size)
    cosine_table, sine_table = rope_tables(places, head_size)
    query_rot = low(rotate(query_proj * rms_scale(query_proj) * query_gain, cosine_table, sine_table))
    key_rot = low(rotate(key_proj * rms_scale(key_proj) * key_gain, cosine_table, sine_table))
    block_rows = min(512, length)
    block_count = length // block_rows
    query_blocks = query_rot.reshape(block_count, block_rows, key_heads, group_size, head_size)
    place_blocks = places.reshape(block_count, block_rows)

    def attend(block_args):
        query_block, place_block = block_args
        scores = low_back(score_scale * jnp.einsum('tkgd,lkd->kgtl', query_block, key_rot, precision=HIGHEST_PRECISION))
        allowed = places[None, None, None, :] <= place_block[None, None, :, None]
        scores = jnp.where(allowed, scores, MASKED_SCORE)
        row_max = lax.optimization_barrier(jnp.max(scores, axis=-1, keepdims=True))
        weights = jnp.exp(scores - row_max)
        attn_probs = low(weights / lax.optimization_barrier(jnp.sum(weights, axis=-1, keepdims=True)))
        return jnp.einsum('kgtl,lkd->tkgd', attn_probs, value_low, precision=HIGHEST_PRECISION)
    attn_mixed = lax.map(jax.checkpoint(attend), (query_blocks, place_blocks))
    attn_mixed = low_back(low(attn_mixed.reshape(length, query_heads * head_size)))
    residual = tokens + low_back(matmul(attn_mixed, w_out))
    second_normed = low(residual * rms_scale(residual) * ffn_gain)
    gate_pre = low_back(matmul(second_normed, w_gate))
    up_pre = low_back(matmul(second_normed, w_up))
    hidden = low(jax.nn.silu(gate_pre) * up_pre)
    return residual + matmul(hidden, w_down)

def reference(hidden_in, positions, cotangent, attn_gain, w_query, w_key, w_value, query_gain, key_gain, w_out, ffn_gain, w_gate, w_up, w_down):
    params = tuple((source_array.astype(jnp.float32) for source_array in (attn_gain, w_query, w_key, w_value, query_gain, key_gain, w_out, ffn_gain, w_gate, w_up, w_down)))

    def one_sequence(totals, inputs):
        tokens, places, seq_cotangent = inputs

        def forward_here(token_values, *weights):
            return forward(token_values, places, *weights)
        seq_out, pullback = jax.vjp(forward_here, tokens.astype(jnp.float32), *params)
        gradients = pullback(seq_cotangent.astype(jnp.float32))
        totals = tuple((total_part + grad_part for total_part, grad_part in zip(totals, gradients[1:])))
        return (totals, (seq_out.astype(jnp.bfloat16), gradients[0].astype(jnp.bfloat16)))
    zero_totals = tuple((jnp.zeros(param_array.shape, jnp.float32) for param_array in params))
    totals, (block_out, grad_in) = lax.scan(one_sequence, zero_totals, (hidden_in, positions, cotangent))
    return (block_out, grad_in, totals[0], totals[1], totals[2], totals[3], totals[4], totals[5], totals[6], totals[7], totals[8], totals[9], totals[10])
```

```python
import jax
import jax.numpy as jnp
from jax import lax
from jax.sharding import PartitionSpec as P

NORM_EPSILON = 1e-05
ROPE_BASE = 1000000.0
MASKED_SCORE = -1e30
BF16 = jnp.bfloat16
F32 = jnp.float32
STEPS = (0, -1, 1, 2)


def rms_scale(values):
    return lax.rsqrt(jnp.mean(values * values, axis=-1, keepdims=True) + NORM_EPSILON)


def rope_tables(places, head_size):
    half_width = head_size // 2
    pair_index = jnp.arange(half_width, dtype=F32)
    frequency = ROPE_BASE ** (-2.0 * pair_index / head_size)
    angles = places.astype(F32)[:, None] * frequency[None, :]
    return (jnp.cos(angles)[:, None, :], jnp.sin(angles)[:, None, :])


def rotate(values, cosine_table, sine_table):
    half_width = values.shape[-1] // 2
    front = values[..., :half_width]
    back_half = values[..., half_width:]
    return jnp.concatenate(
        [
            front * cosine_table - back_half * sine_table,
            back_half * cosine_table + front * sine_table,
        ],
        axis=-1,
    )


def unrotate(grads_in, cosine_table, sine_table):
    return rotate(grads_in, cosine_table, -sine_table)


def norm_back(d_normed, normed_hat, scale_values, gain_vector):
    scaled = d_normed * gain_vector
    inner = jnp.mean(normed_hat * scaled, axis=-1, keepdims=True)
    return (scale_values * (scaled - normed_hat * inner), d_normed * normed_hat)


def mm(left, right):
    return jnp.dot(left, right, preferred_element_type=F32)


def mm_t(left, right):
    return lax.dot_general(left, right, (((1,), (1,)), ((), ())), preferred_element_type=F32)


def outer_sum(left, right):
    return lax.dot_general(left, right, (((0,), (0,)), ((), ())), preferred_element_type=F32)


def swap_core(value):
    return lax.ppermute(value, "ctx", [(i, i ^ 1) for i in range(8)])


def move_z(value, step):
    return lax.ppermute(value, "ctx", [(i, (i + 2 * step) % 8) for i in range(8)])


def gather_ctx(block):
    groups = []
    for step in STEPS:
        mine = block if step == 0 else move_z(block, -step)
        groups.append(jnp.concatenate([mine, swap_core(mine)], axis=0))
    return groups


def scatter_ctx(groups):
    total = None
    sums = {}
    for step in (2, 1, -1, 0):
        part = groups[STEPS.index(step)]
        half = part.shape[0] // 2
        other = swap_core(part[half:].astype(BF16))
        sums[step] = part[:half] + other.astype(F32)
    total = sums[0]
    for step in (1, -1, 2):
        total = total + move_z(sums[step].astype(BF16), step).astype(F32)
    return total


def transpose_mesh(value, flip=0):
    pairs = [
        ((d * 8 + c) * 8 + f, ((d ^ flip) * 8 + f) * 8 + c) for d in range(2) for c in range(8) for f in range(8)
    ]
    return lax.ppermute(value, ("dp", "ctx", "fsdp"), pairs)


def swap_dp(value):
    return lax.ppermute(value, "dp", [(0, 1), (1, 0)])


def after(value, *others):
    return lax.optimization_barrier((value, *others))[0]


def gather_fsdp_rows(block):
    copies = jnp.broadcast_to(block[None], (8, *block.shape))
    return lax.all_to_all(copies, "fsdp", split_axis=0, concat_axis=0, tiled=True).reshape(-1, block.shape[1])


def sum_fsdp_rows(partial):
    parts = lax.all_to_all(partial.astype(BF16), "fsdp", split_axis=0, concat_axis=0, tiled=True)
    return jnp.sum(parts.reshape(8, -1, partial.shape[1]).astype(F32), axis=0).astype(BF16)


def sum_dp(low):
    return (low.astype(F32) + swap_dp(low).astype(F32)).astype(BF16)


def sum_dp_transposed(low):
    return (transpose_mesh(low).astype(F32) + transpose_mesh(low, 1).astype(F32)).astype(BF16)


def gather_ctx_parts(block):
    parts = []
    for step in STEPS:
        mine = block if step == 0 else move_z(block, -step)
        parts += [mine, swap_core(mine)]
    stacked = jnp.stack(parts)
    ctx = lax.axis_index("ctx")
    ordered = []
    for owner in range(8):
        away = (owner // 2 - ctx // 2) % 4
        slot = jnp.array([0, 2, 3, 1])[away] * 2 + (owner % 2 ^ ctx % 2)
        ordered.append(lax.dynamic_index_in_dim(stacked, slot, 0, keepdims=False))
    return ordered


def sum_all(value):
    total = value + swap_core(value)
    total = total + move_z(total, 1) + move_z(total, -1) + move_z(total, 2)
    total = total + swap_dp(total)
    for step in (1, 2, 4):
        total = total + lax.ppermute(total, "fsdp", [(i, i ^ step) for i in range(8)])
    return total


def own_columns(weight, width, index):
    return lax.dynamic_slice_in_dim(weight, index * width, width, 1)


def body(
    hidden_in,
    positions,
    cotangent,
    attn_gain,
    w_query,
    w_key,
    w_value,
    query_gain,
    key_gain,
    w_out,
    ffn_gain,
    w_gate,
    w_up,
    w_down,
):
    ctx = lax.axis_index("ctx")
    tokens = hidden_in[0].astype(F32)
    count, width = tokens.shape
    head_size = query_gain.shape[0]
    q_width = w_query.shape[1] // 8
    k_width = w_key.shape[1] // 8
    ff_width = w_gate.shape[1] // 8
    group_size = q_width // k_width
    score_scale = head_size ** (-0.5)

    w_qkv = gather_fsdp_rows(
        jnp.concatenate(
            [own_columns(w_query, q_width, ctx), own_columns(w_key, k_width, ctx), own_columns(w_value, k_width, ctx)],
            axis=1,
        )
    )
    out_rows = transpose_mesh(w_out)
    down_chunk = transpose_mesh(jnp.transpose(own_columns(w_down, width // 8, ctx)))
    ffn_block = jnp.concatenate(
        [own_columns(w_gate, ff_width, ctx), own_columns(w_up, ff_width, ctx), down_chunk], axis=1
    )
    ffn_rows = gather_fsdp_rows(after(ffn_block, w_qkv))
    gate_up, down_t = ffn_rows[:, : 2 * ff_width], ffn_rows[:, 2 * ff_width :]

    z_index, core = ctx // 2, ctx % 2
    owners = jnp.stack(
        [((z_index + step) % 4) * 2 + (core ^ flip) for step in STEPS for flip in (0, 1)]
    )
    places = positions[0].reshape(8, count)[owners].reshape(8 * count)
    cosine_table, sine_table = rope_tables(places, head_size)

    first_scale = rms_scale(tokens)
    first_hat = tokens * first_scale
    first_normed = (first_hat * attn_gain).astype(BF16)
    first_groups = gather_ctx(first_normed)
    cot_groups = gather_ctx(after(cotangent[0], *first_groups))

    qkv = jnp.concatenate([mm(group, w_qkv) for group in first_groups], axis=0)
    length = qkv.shape[0]
    query_split = qkv[:, :q_width].reshape(length, group_size, head_size)
    key_split = qkv[:, q_width : q_width + k_width].reshape(length, 1, head_size)
    value_low = qkv[:, q_width + k_width :].astype(BF16)
    query_scale = rms_scale(query_split)
    query_hat = query_split * query_scale
    query_rot = rotate(query_hat * query_gain, cosine_table, sine_table).astype(BF16)
    key_scale = rms_scale(key_split)
    key_hat = key_split * key_scale
    key_rot = rotate(key_hat * key_gain, cosine_table, sine_table).astype(BF16)[:, 0]

    allowed = places[None, None, :] <= places[None, :, None]
    scores = jnp.einsum("tgd,ld->gtl", query_rot, key_rot, preferred_element_type=F32) * score_scale
    scores = jnp.where(allowed, scores, MASKED_SCORE)
    row_max = jnp.max(scores, axis=-1, keepdims=True)
    weights = jnp.exp(scores - row_max)
    row_total = jnp.sum(weights, axis=-1, keepdims=True)
    probs = weights / row_total
    probs_low = probs.astype(BF16)
    mixed = jnp.einsum("gtl,ld->tgd", probs_low, value_low, preferred_element_type=F32)
    mixed = mixed.reshape(length, q_width).astype(BF16)
    rows = 2 * count
    attn_proj = scatter_ctx([mm(mixed[i * rows : (i + 1) * rows], out_rows) for i in range(4)])

    residual = tokens + attn_proj
    second_scale = rms_scale(residual)
    second_hat = residual * second_scale
    second_normed = (second_hat * ffn_gain).astype(BF16)
    second_groups = gather_ctx(second_normed)

    hidden_groups, d_ffn_groups, block_parts, d_second_parts = [], [], [], []
    for second_group, cot_group in zip(second_groups, cot_groups):
        both = mm(second_group, gate_up)
        gate_pre, up_pre = both[:, :ff_width], both[:, ff_width:]
        sigmoid_gate = jax.nn.sigmoid(gate_pre)
        gate_act = gate_pre * sigmoid_gate
        hidden = (gate_act * up_pre).astype(BF16)
        d_hidden = mm(cot_group, down_t)
        d_gate = (d_hidden * up_pre * sigmoid_gate * (1.0 + gate_pre * (1.0 - sigmoid_gate))).astype(BF16)
        d_up = (d_hidden * gate_act).astype(BF16)
        d_ffn = jnp.concatenate([d_gate, d_up], axis=1)
        hidden_groups.append(hidden)
        d_ffn_groups.append(d_ffn)
        d_second_parts.append(mm_t(d_ffn, gate_up))
        block_parts.append(mm_t(hidden, down_t))
    d_second = scatter_ctx(d_second_parts)
    block_out = (residual + scatter_ctx(block_parts)).astype(BF16)

    ffn_partial = jnp.concatenate(
        [
            outer_sum(jnp.concatenate(second_groups, axis=0), jnp.concatenate(d_ffn_groups, axis=0)).astype(BF16),
            outer_sum(jnp.concatenate(cot_groups, axis=0), jnp.concatenate(hidden_groups, axis=0)).astype(BF16),
        ],
        axis=1,
    )
    ffn_sum = sum_fsdp_rows(ffn_partial)

    d_from_second, ffn_gain_part = norm_back(d_second, second_hat, second_scale, ffn_gain)
    d_resid = cotangent[0].astype(F32) + d_from_second
    d_attn = d_resid.astype(BF16)
    d_attn_all = jnp.concatenate(gather_ctx(d_attn), axis=0)

    d_mixed = mm_t(d_attn_all, out_rows).astype(BF16)
    d_mixed_split = d_mixed.reshape(length, group_size, head_size)
    d_value = jnp.einsum("gtl,tgd->ld", probs_low, d_mixed_split, preferred_element_type=F32).astype(BF16)
    d_probs = jnp.einsum("tgd,ld->gtl", d_mixed_split, value_low, preferred_element_type=F32)
    d_scores = (probs * (d_probs - jnp.sum(probs * d_probs, axis=-1, keepdims=True))).astype(BF16)
    d_query_rot = jnp.einsum("gtl,ld->tgd", d_scores, key_rot, preferred_element_type=F32) * score_scale
    d_key_rot = jnp.einsum("gtl,tgd->ld", d_scores, query_rot, preferred_element_type=F32) * score_scale
    d_query_heads, query_gain_part = norm_back(
        unrotate(d_query_rot, cosine_table, sine_table), query_hat, query_scale, query_gain
    )
    d_key_heads, key_gain_part = norm_back(
        unrotate(d_key_rot[:, None], cosine_table, sine_table), key_hat, key_scale, key_gain
    )
    d_qkv = jnp.concatenate(
        [d_query_heads.reshape(length, q_width).astype(BF16), d_key_heads[:, 0].astype(BF16), d_value], axis=1
    )
    d_qkv, ffn_sum = lax.optimization_barrier((d_qkv, ffn_sum))
    d_first = scatter_ctx([mm_t(d_qkv[i * rows : (i + 1) * rows], w_qkv) for i in range(4)])
    d_from_first, attn_gain_part = norm_back(d_first, first_hat, first_scale, attn_gain)
    grad_in = (d_resid + d_from_first).astype(BF16)

    gains = sum_all(
        jnp.concatenate(
            [
                jnp.sum(attn_gain_part, axis=0),
                jnp.sum(ffn_gain_part, axis=0),
                jnp.sum(query_gain_part, axis=(0, 1)),
                jnp.sum(key_gain_part, axis=(0, 1)),
            ]
        )[None]
    )[0]
    grad_attn_gain = gains[:width]
    grad_ffn_gain = gains[width : 2 * width]
    grad_query_gain = gains[2 * width : 2 * width + head_size]
    grad_key_gain = gains[2 * width + head_size :]

    attn_partial = jnp.concatenate(
        [
            outer_sum(jnp.concatenate(first_groups, axis=0), d_qkv).astype(BF16),
            outer_sum(d_attn_all, mixed).astype(BF16),
        ],
        axis=1,
    )
    attn_sum = sum_fsdp_rows(attn_partial)
    qkv_width = q_width + 2 * k_width
    ffn_parts = gather_ctx_parts(
        jnp.concatenate([sum_dp(ffn_sum[:, : 2 * ff_width]), sum_dp_transposed(ffn_sum[:, 2 * ff_width :])], axis=1)
    )
    attn_parts = gather_ctx_parts(
        jnp.concatenate([sum_dp(attn_sum[:, :qkv_width]), sum_dp_transposed(attn_sum[:, qkv_width:])], axis=1)
    )

    def side_by_side(parts, low, high):
        return jnp.concatenate([part[:, low:high] for part in parts], axis=1).astype(F32)

    def stacked_rows(parts, low):
        return jnp.transpose(jnp.concatenate([part[:, low:] for part in parts], axis=0)).astype(F32)

    return (
        block_out[None],
        grad_in[None],
        grad_attn_gain,
        side_by_side(attn_parts, 0, q_width),
        side_by_side(attn_parts, q_width, q_width + k_width),
        side_by_side(attn_parts, q_width + k_width, qkv_width),
        grad_query_gain,
        grad_key_gain,
        stacked_rows(attn_parts, qkv_width),
        grad_ffn_gain,
        side_by_side(ffn_parts, 0, ff_width),
        side_by_side(ffn_parts, ff_width, 2 * ff_width),
        stacked_rows(ffn_parts, 2 * ff_width),
    )


def solution(mesh):
    in_specs = (
        P(("dp", "fsdp"), "ctx", None),
        P(("dp", "fsdp"), None),
        P(("dp", "fsdp"), "ctx", None),
        P(),
        P("fsdp", None),
        P("fsdp", None),
        P("fsdp", None),
        P(),
        P(),
        P("fsdp", None),
        P(),
        P("fsdp", None),
        P("fsdp", None),
        P("fsdp", None),
    )
    out_specs = (
        P(("dp", "fsdp"), "ctx", None),
        P(("dp", "fsdp"), "ctx", None),
        P(),
        P("fsdp", None),
        P("fsdp", None),
        P("fsdp", None),
        P(),
        P(),
        P("fsdp", None),
        P(),
        P("fsdp", None),
        P("fsdp", None),
        P("fsdp", None),
    )
    return jax.shard_map(body, mesh=mesh, in_specs=in_specs, out_specs=out_specs, check_vma=False)
```

```python
import math

import jax
import jax.numpy as jnp
from jax import lax
from jax.experimental import pallas as pl
from jax.experimental.pallas import tpu as pltpu
from jax.sharding import PartitionSpec as P

NORM_EPSILON = 1e-05
ROPE_BASE = 1000000.0
MASKED_SCORE = -1e30
BF16 = jnp.bfloat16
F32 = jnp.float32
STEPS = (0, -1, 1, 2)
Y_STEPS = (1, 3, 2, 0)


def rms_scale(values):
    return lax.rsqrt(jnp.mean(values * values, axis=-1, keepdims=True) + NORM_EPSILON)


def rope_tables(places, head_size):
    half_width = head_size // 2
    pair_index = jnp.arange(half_width, dtype=F32)
    frequency = ROPE_BASE ** (-2.0 * pair_index / head_size)
    angles = frequency[:, None] * places.astype(F32)[None, :]
    return jnp.cos(angles), jnp.sin(angles)


def call(kernel, out_shapes, args, flops, scratch=(), scalars=0):
    vmem = pl.BlockSpec(memory_space=pltpu.VMEM)
    smem = pl.BlockSpec(memory_space=pltpu.SMEM)
    out_bytes = sum(math.prod(o.shape) * o.dtype.itemsize for o in out_shapes)
    in_bytes = sum(math.prod(a.shape) * a.dtype.itemsize for a in args)
    return pl.pallas_call(
        kernel,
        out_shape=out_shapes,
        in_specs=[smem] * scalars + [vmem] * (len(args) - scalars),
        out_specs=[vmem] * len(out_shapes),
        scratch_shapes=list(scratch),
        compiler_params=pltpu.CompilerParams(vmem_limit_bytes=40 * 2**20),
        cost_estimate=pl.CostEstimate(flops=flops, bytes_accessed=in_bytes + out_bytes, transcendentals=0),
    )(*args)


def shape(dims, kind):
    return jax.ShapeDtypeStruct(dims, kind)


def head_forward(values, gain, cosine, sine):
    scale = lax.rsqrt(jnp.mean(values * values, axis=0, keepdims=True) + NORM_EPSILON)
    hat = values * scale
    normed = hat * gain
    half = values.shape[0] // 2
    front, back = normed[:half], normed[half:]
    rotated = jnp.concatenate([front * cosine - back * sine, back * cosine + front * sine], axis=0)
    return scale, hat, rotated


def head_backward(grads, hat, scale, gain, cosine, sine):
    half = grads.shape[0] // 2
    front, back = grads[:half], grads[half:]
    d_normed = jnp.concatenate([front * cosine + back * sine, back * cosine - front * sine], axis=0)
    scaled = d_normed * gain
    inner = jnp.mean(hat * scaled, axis=0, keepdims=True)
    return scale * (scaled - hat * inner), jnp.sum(d_normed * hat, axis=1, keepdims=True)


def attend_forward(*refs):
    pieces, refs = refs[:8], refs[8:]
    w_qkv, out_rows, cos_ref, sin_ref, column_ref, row_ref, q_gain, k_gain = refs[:8]
    mixed_ref, qkv_ref, lse_ref, send_ref, *mine_refs = refs[8:]
    length = qkv_ref.shape[1]
    head = q_gain.shape[0]
    for pair in range(4):
        x = jnp.concatenate([pieces[2 * pair][...], pieces[2 * pair + 1][...]], axis=0)
        qkv_ref[:, pair * 256 : (pair + 1) * 256] = jnp.transpose(mm(x, w_qkv[...]))
    cosine, sine = cos_ref[...], sin_ref[...]
    queries = [
        (head_forward(qkv_ref[h * head : (h + 1) * head], q_gain[...], cosine, sine)[2]).astype(BF16) * BF16(head**-0.5)
        for h in range(2)
    ]
    key = jnp.transpose(head_forward(qkv_ref[2 * head : 3 * head], k_gain[...], cosine, sine)[2]).astype(BF16)
    value = qkv_ref[3 * head :].astype(BF16)
    width = column_ref.shape[1]
    for tile in range(length // width):
        lanes = slice(tile * width, (tile + 1) * width)
        allowed = column_ref[...] <= row_ref[:, lanes]
        outs = []
        for h in range(2):
            scores = jnp.where(allowed, mm(key, queries[h][:, lanes]), MASKED_SCORE)
            top = jnp.max(scores, axis=0, keepdims=True)
            weights = jnp.exp(scores - top)
            total = jnp.sum(weights, axis=0, keepdims=True)
            lse_ref[h : h + 1, lanes] = top + jnp.log(total)
            outs.append(mm(value, (weights * (1.0 / total)).astype(BF16)))
        mixed = jnp.transpose(jnp.concatenate(outs, axis=0)).astype(BF16)
        mixed_ref[lanes] = mixed
        proj = mm(mixed, out_rows[...])
        mine_refs[tile][...] = proj[: width // 2]
        send_ref[tile] = proj[width // 2 :].astype(BF16)


def attend_backward(*refs):
    place, pieces, d_pieces, refs = refs[0], refs[1:9], refs[9:17], refs[17:]
    w_qkv, out_rows, cos_ref, sin_ref, column_ref, row_ref, q_gain, k_gain, mixed_ref, qkv_ref, lse_ref = refs[:11]
    q_gain_ref, k_gain_ref, attn_gain_ref, send_ref = refs[11:15]
    mine_refs, part_refs = refs[15:19], refs[19:27]
    d_attn_ref, x_ref, d_qkv_ref, grads_ref = refs[27:]
    length = qkv_ref.shape[1]
    head = q_gain.shape[0]
    count = pieces[0].shape[0]
    for i in range(8):
        d_attn_ref[i * count : (i + 1) * count] = d_pieces[i][...]
        x_ref[i * count : (i + 1) * count] = pieces[i][...]
    cosine, sine = cos_ref[...], sin_ref[...]
    scales, hats, queries = [], [], []
    for h in range(2):
        scale, hat, rotated = head_forward(qkv_ref[h * head : (h + 1) * head], q_gain[...], cosine, sine)
        scales.append(scale)
        hats.append(hat)
        queries.append(rotated.astype(BF16) * BF16(head**-0.5))
    k_scale, k_hat, rotated = head_forward(qkv_ref[2 * head : 3 * head], k_gain[...], cosine, sine)
    key_rows = rotated.astype(BF16)
    key = jnp.transpose(rotated).astype(BF16)
    value = jnp.transpose(qkv_ref[3 * head :]).astype(BF16)
    width = column_ref.shape[1]
    d_key = jnp.zeros((length, head), F32)
    d_value = jnp.zeros((length, head), F32)
    for tile in range(length // width):
        lanes = slice(tile * width, (tile + 1) * width)
        allowed = column_ref[...] <= row_ref[:, lanes]
        d_mixed = jnp.transpose(mm_t(d_attn_ref[lanes], out_rows[...])).astype(BF16)
        for h in range(2):
            rows = slice(h * head, (h + 1) * head)
            query = queries[h][:, lanes]
            probs = jnp.where(allowed, jnp.exp(mm(key, query) - lse_ref[h : h + 1, lanes]), 0.0)
            d_probs = mm(value, d_mixed[rows])
            inner = jnp.sum(probs * d_probs, axis=0, keepdims=True)
            d_scores = (probs * (d_probs - inner)).astype(BF16)
            d_value += mm_t(probs.astype(BF16), d_mixed[rows])
            d_key += mm_t(d_scores, query)
            d_qkv_ref[rows, lanes] = mm(key_rows, d_scores) * head**-0.5
    for h in range(2):
        rows = slice(h * head, (h + 1) * head)
        d_query, gain_part = head_backward(d_qkv_ref[rows], hats[h], scales[h], q_gain[...], cosine, sine)
        d_qkv_ref[rows] = d_query
        if h == 0:
            q_gain_ref[...] = gain_part
        else:
            q_gain_ref[...] += gain_part
    d_keys, gain_part = head_backward(jnp.transpose(d_key), k_hat, k_scale, k_gain[...], cosine, sine)
    k_gain_ref[...] = gain_part
    d_qkv_ref[2 * head : 3 * head] = d_keys
    d_qkv_ref[3 * head :] = jnp.transpose(d_value)
    for tile in range(4):
        lanes = slice(tile * 2 * count, (tile + 1) * 2 * count)
        d_qkv = jnp.transpose(d_qkv_ref[:, lanes]).astype(BF16)
        d_first = mm_t(d_qkv, w_qkv[...])
        mine_refs[tile][...] = d_first[:count]
        send_ref[tile] = d_first[count:].astype(BF16)
    grad_qkv = jnp.transpose(mm(d_qkv_ref[...].astype(BF16), x_ref[...]))
    attn_gain_ref[...] = jnp.sum(grad_qkv * w_qkv[...].astype(F32), axis=1, keepdims=True)
    grads_ref[:, : 4 * head] = grad_qkv.astype(BF16)
    grads_ref[:, 4 * head :] = jnp.transpose(
        lax.dot_general(mixed_ref[...], d_attn_ref[...], (((0,), (0,)), ((), ())), preferred_element_type=F32)
    ).astype(BF16)
    for i, step in enumerate(Y_STEPS):
        for flip in (0, 1):
            owner = (place[0] + step) % 4 * 2 + (place[1] ^ flip)
            part_refs[2 * i + flip][...] = grads_ref[pl.ds(pl.multiple_of(owner * count, count), count)]


def ffn_group(first, second, cot_first, cot_second, weights, hidden_ref, d_ffn_ref, d_mine, d_send, mine, send):
    width = hidden_ref.shape[1]
    count = first.shape[0]
    x = jnp.concatenate([first[...], second[...]], axis=0)
    cot = jnp.concatenate([cot_first[...], cot_second[...]], axis=0)
    both = mm(x, weights[:, : 2 * width])
    gate, up = both[:, :width], both[:, width:]
    sigmoid = 1.0 / (1.0 + jnp.exp(-gate))
    act = gate * sigmoid
    hidden = (act * up).astype(BF16)
    hidden_ref[...] = hidden
    d_hidden = mm(cot, weights[:, 2 * width :])
    d_gate = d_hidden * up * sigmoid * (1.0 + gate * (1.0 - sigmoid))
    d_ffn = jnp.concatenate([d_gate, d_hidden * act], axis=1).astype(BF16)
    d_ffn_ref[...] = d_ffn
    d_second = mm_t(d_ffn, weights[:, : 2 * width])
    d_mine[...] = d_second[:count]
    d_send[...] = d_second[count:].astype(BF16)
    out = mm_t(hidden, weights[:, 2 * width :])
    mine[...] = out[:count]
    send[...] = out[count:].astype(BF16)


def ffn_weights(*refs):
    place, seconds, cots, hiddens, d_ffns = refs[0], refs[1:9], refs[9:17], refs[17:21], refs[21:25]
    part_refs, x_ref, h_ref = refs[25:33], refs[33], refs[34]
    count = seconds[0].shape[0]
    for pieces, others, columns in ((seconds, d_ffns, 0), (cots, hiddens, d_ffns[0].shape[1])):
        for i in range(8):
            x_ref[i * count : (i + 1) * count] = pieces[i][...]
        width = others[0].shape[1]
        for i in range(4):
            h_ref[2 * i * count : 2 * (i + 1) * count, :width] = others[i][...]
        for i, step in enumerate(Y_STEPS):
            rows = pl.ds(pl.multiple_of((place[0] + step) % 4 * (2 * count), 2 * count), 2 * count)
            both = outer_sum(x_ref[:, rows], h_ref[:, :width])
            low, high = both[:count], both[count:]
            first = place[1] == 0
            part_refs[2 * i][:, columns : columns + width] = jnp.where(first, low, high).astype(BF16)
            part_refs[2 * i + 1][:, columns : columns + width] = jnp.where(first, high, low).astype(BF16)


def assemble_ffn(*refs):
    order, pieces, (gate_ref, up_ref, down_ref, held) = refs[0], refs[1:9], refs[9:]
    width = down_ref.shape[0]
    count = pieces[0].shape[0]
    for i in range(8):
        held[order[i]] = pieces[i][...]
    for owner in range(8):
        columns = slice(owner * width, (owner + 1) * width)
        gate_ref[:, columns] = held[owner, :, :width].astype(F32)
        up_ref[:, columns] = held[owner, :, width : 2 * width].astype(F32)
        down = held[owner, :, 2 * width :].astype(F32)
        down_ref[:, owner * count : (owner + 1) * count] = jnp.transpose(down)


def assemble_attn(*refs):
    order, pieces, (query_ref, key_ref, value_ref, out_ref, held) = refs[0], refs[1:9], refs[9:]
    count = pieces[0].shape[0]
    half = count // 2
    for i in range(8):
        held[order[i]] = pieces[i][...]
    for owner in range(8):
        columns = slice(owner * count, (owner + 1) * count)
        narrow = slice(owner * half, (owner + 1) * half)
        part = held[owner].astype(F32)
        query_ref[:, columns] = part[:, :count]
        key_ref[:, narrow] = part[:, count : count + half]
        value_ref[:, narrow] = part[:, count + half : 2 * count]
        out_ref[:, columns] = jnp.transpose(part[:, 2 * count :])


def norm_back(d_normed, normed_hat, scale_values, gain_vector):
    scaled = d_normed * gain_vector
    inner = jnp.mean(normed_hat * scaled, axis=-1, keepdims=True)
    return (scale_values * (scaled - normed_hat * inner), d_normed * normed_hat)


def mm(left, right):
    return jnp.dot(left, right, preferred_element_type=F32)


def mm_t(left, right):
    return lax.dot_general(left, right, (((1,), (1,)), ((), ())), preferred_element_type=F32)


def outer_sum(left, right):
    return lax.dot_general(left, right, (((0,), (0,)), ((), ())), preferred_element_type=F32)


def swap_core(value):
    return lax.ppermute(value, "ctx", [(i, i ^ 1) for i in range(8)])


def move_z(value, step):
    return lax.ppermute(value, "ctx", [(i, (i + 2 * step) % 8) for i in range(8)])


def gather_ctx(block):
    pieces = []
    for step in STEPS:
        mine = block if step == 0 else move_z(block, -step)
        pieces += [mine, swap_core(mine)]
    return pieces


def start_scatter_ctx(mine, received):
    sums = [own + other.astype(F32) for own, other in zip(mine, received)]
    return [sums[0]] + [move_z(sums[slot].astype(BF16), STEPS[slot]) for slot in (3, 1, 2)]


def end_scatter(moves):
    return sum(move.astype(F32) for move in moves)


def scatter_ctx(mine, received):
    return end_scatter(start_scatter_ctx(mine, received))


def transpose_mesh(value, flip=0):
    pairs = [
        ((d * 8 + c) * 8 + f, ((d ^ flip) * 8 + f) * 8 + c) for d in range(2) for c in range(8) for f in range(8)
    ]
    return lax.ppermute(value, ("dp", "ctx", "fsdp"), pairs)


def swap_dp(value):
    return lax.ppermute(value, "dp", [(0, 1), (1, 0)])


def after(value, *others):
    return lax.optimization_barrier((value, *others))[0]


def move_y(value, step, flip=0):
    pairs = [(y * 2 + x, (y + step) % 4 * 2 + (x ^ flip)) for y in range(4) for x in range(2)]
    return lax.ppermute(value, "fsdp", pairs)


def gather_fsdp_rows(block):
    me = lax.axis_index("fsdp")
    rows = block.shape[0]
    whole = jnp.zeros((8 * rows, block.shape[1]), block.dtype)
    for flip, held in ((0, block), (1, move_y(block, 0, 1))):
        for step in (0, 1, 3, 2):
            piece = move_y(held, step) if step else held
            owner = (me // 2 - step) % 4 * 2 + (me % 2 ^ flip)
            whole = lax.dynamic_update_slice_in_dim(whole, piece, owner * rows, 0)
    return whole


def start_sum_fsdp(pieces):
    return [
        [pieces[2 * i + flip] if step == 0 else move_y(pieces[2 * i + flip], step) for flip in (1, 0)]
        for i, step in enumerate(Y_STEPS)
    ]


def end_sum_fsdp(moved):
    other, own = (sum(pair[i].astype(F32) for pair in moved) for i in (0, 1))
    return (own + move_y(other.astype(BF16), 0, 1).astype(F32)).astype(BF16)


def sum_dp(low):
    return (low.astype(F32) + swap_dp(low).astype(F32)).astype(BF16)


def sum_dp_transposed(low):
    return (transpose_mesh(low).astype(F32) + transpose_mesh(low, 1).astype(F32)).astype(BF16)


def sum_all(value):
    total = value + swap_core(value)
    total = total + move_z(total, 1) + move_z(total, -1) + move_z(total, 2)
    total = total + move_y(total, 1) + move_y(total, 3) + move_y(total, 2)
    total = total + swap_dp(total)
    return total + move_y(total, 0, 1)


def own_columns(weight, width, index):
    return lax.dynamic_slice_in_dim(weight, index * width, width, 1)


def body(
    hidden_in,
    positions,
    cotangent,
    attn_gain,
    w_query,
    w_key,
    w_value,
    query_gain,
    key_gain,
    w_out,
    ffn_gain,
    w_gate,
    w_up,
    w_down,
):
    ctx = lax.axis_index("ctx")
    tokens = hidden_in[0].astype(F32)
    count, width = tokens.shape
    head_size = query_gain.shape[0]
    q_width = w_query.shape[1] // 8
    k_width = w_key.shape[1] // 8
    ff_width = w_gate.shape[1] // 8

    w_qkv = gather_fsdp_rows(
        jnp.concatenate(
            [own_columns(w_query, q_width, ctx), own_columns(w_key, k_width, ctx), own_columns(w_value, k_width, ctx)],
            axis=1,
        )
    )
    out_rows = transpose_mesh(w_out)
    down_chunk = transpose_mesh(jnp.transpose(own_columns(w_down, width // 8, ctx)))
    ffn_block = jnp.concatenate(
        [own_columns(w_gate, ff_width, ctx), own_columns(w_up, ff_width, ctx), down_chunk], axis=1
    )
    ffn_rows = gather_fsdp_rows(after(ffn_block, w_qkv))
    place = jnp.stack([lax.axis_index("fsdp") // 2, lax.axis_index("fsdp") % 2])

    z_index, core = ctx // 2, ctx % 2
    owners = jnp.stack(
        [((z_index + step) % 4) * 2 + (core ^ flip) for step in STEPS for flip in (0, 1)]
    )
    places = positions[0].reshape(8, count)[owners].reshape(8 * count)
    length = 8 * count
    cosine_table, sine_table = rope_tables(places, head_size)
    column = jnp.broadcast_to(places[:, None], (length, 2 * count))
    row = places[None]
    gains = (query_gain[:, None], key_gain[:, None])

    first_scale = rms_scale(tokens)
    first_hat = tokens * first_scale
    first_normed = (first_hat * attn_gain).astype(BF16)
    first_pieces = gather_ctx(first_normed)
    cot_pieces = gather_ctx(after(cotangent[0], *first_pieces))

    mixed, qkv, lse, send, *mine = call(
        attend_forward,
        [
            shape((length, q_width), BF16),
            shape((4 * head_size, length), F32),
            shape((8, length), F32),
            shape((4, count, width), BF16),
        ]
        + [shape((count, width), F32)] * 4,
        (*first_pieces, w_qkv, out_rows, cosine_table, sine_table, column, row, *gains),
        4 * 10**9,
    )
    received = swap_core(send)
    residual = tokens + scatter_ctx(mine, received)
    second_scale = rms_scale(residual)
    second_hat = residual * second_scale
    second_normed = (second_hat * ffn_gain).astype(BF16)
    second_pieces = gather_ctx(second_normed)

    hiddens, d_ffns, d_mine, d_received, mine, received = [], [], [], [], [], []
    for group in range(4):
        pair = slice(2 * group, 2 * group + 2)
        hidden, d_ffn, own, other, block_own, block_other = call(
            ffn_group,
            [
                shape((2 * count, ff_width), BF16),
                shape((2 * count, 2 * ff_width), BF16),
                shape((count, width), F32),
                shape((count, width), BF16),
                shape((count, width), F32),
                shape((count, width), BF16),
            ],
            (*second_pieces[pair], *cot_pieces[pair], ffn_rows),
            2 * 10**9,
        )
        hiddens.append(hidden)
        d_ffns.append(d_ffn)
        d_mine.append(own)
        d_received.append(swap_core(other))
        mine.append(block_own)
        received.append(block_other)
    ffn_partial = call(
        ffn_weights,
        [shape((count, 3 * ff_width), BF16)] * 8,
        (place, *second_pieces, *cot_pieces, *hiddens, *d_ffns),
        4 * 10**9,
        [pltpu.VMEM((length, width), BF16), pltpu.VMEM((length, 2 * ff_width), BF16)],
        1,
    )
    d_moves = start_scatter_ctx(d_mine, d_received)
    d_moves, ffn_partial = lax.optimization_barrier((d_moves, ffn_partial))
    d_second = end_scatter(d_moves)
    ffn_moved = start_sum_fsdp(ffn_partial)

    d_from_second, ffn_gain_part = norm_back(d_second, second_hat, second_scale, ffn_gain)
    d_resid = cotangent[0].astype(F32) + d_from_second
    d_attn = d_resid.astype(BF16)
    d_pieces = gather_ctx(d_attn)
    received = [swap_core(part) for part in after(received, *d_pieces)]
    block_moves = start_scatter_ctx(mine, received)
    d_pieces, ffn_moved = lax.optimization_barrier((d_pieces, ffn_moved))
    ffn_sum = end_sum_fsdp(ffn_moved)
    ffn_gate_up, ffn_down = ffn_sum[:, : 2 * ff_width], ffn_sum[:, 2 * ff_width :]
    ffn_steps = [ffn_gate_up, swap_dp(ffn_gate_up), transpose_mesh(ffn_down), transpose_mesh(ffn_down, 1)]

    qkv_width = q_width + 2 * k_width
    q_gain_part, k_gain_part, attn_gain_part, send, *parts = call(
        attend_backward,
        [
            shape((head_size, 1), F32),
            shape((head_size, 1), F32),
            shape((width, 1), F32),
            shape((4, count, width), BF16),
        ]
        + [shape((count, width), F32)] * 4
        + [shape((count, qkv_width + q_width), BF16)] * 8,
        (place, *first_pieces, *d_pieces, w_qkv, out_rows, cosine_table, sine_table, column, row, *gains, mixed, qkv, lse),
        8 * 10**9,
        [
            pltpu.VMEM((length, width), BF16),
            pltpu.VMEM((length, width), BF16),
            pltpu.VMEM((qkv_width, length), F32),
            pltpu.VMEM((width, qkv_width + q_width), BF16),
        ],
        1,
    )
    mine, attn_partial = parts[:4], parts[4:]
    send, attn_partial, block_moves, ffn_steps = lax.optimization_barrier((send, attn_partial, block_moves, ffn_steps))
    block_out = (residual + end_scatter(block_moves)).astype(BF16)
    d_first = scatter_ctx(mine, swap_core(send))
    d_from_first, _ = norm_back(d_first, first_hat, first_scale, attn_gain)
    grad_in = (d_resid + d_from_first).astype(BF16)

    totals = sum_all(
        jnp.concatenate(
            [
                attn_gain_part[:, 0] / attn_gain,
                jnp.sum(ffn_gain_part, axis=0),
                q_gain_part[:, 0],
                k_gain_part[:, 0],
            ]
        ).reshape(-1, 128)
    ).reshape(-1)
    grad_attn_gain = totals[:width]
    grad_ffn_gain = totals[width : 2 * width]
    grad_query_gain = totals[2 * width : 2 * width + head_size]
    grad_key_gain = totals[2 * width + head_size :]

    ffn_steps = [step.astype(F32) for step in ffn_steps]
    ffn_parts = gather_ctx(
        jnp.concatenate([ffn_steps[0] + ffn_steps[1], ffn_steps[2] + ffn_steps[3]], axis=1).astype(BF16)
    )
    attn_sum = end_sum_fsdp(start_sum_fsdp(attn_partial))
    attn_parts = gather_ctx(
        jnp.concatenate([sum_dp(attn_sum[:, :qkv_width]), sum_dp_transposed(attn_sum[:, qkv_width:])], axis=1)
    )
    grad_gate, grad_up, grad_down = call(
        assemble_ffn,
        [shape((count, 8 * ff_width), F32)] * 2 + [shape((ff_width, width), F32)],
        (owners, *ffn_parts),
        10**6,
        [pltpu.VMEM((8, count, 3 * ff_width), BF16)],
        1,
    )
    grad_query, grad_key, grad_value, grad_out = call(
        assemble_attn,
        [shape((count, width), F32)] + [shape((count, 8 * k_width), F32)] * 2 + [shape((q_width, width), F32)],
        (owners, *attn_parts),
        10**6,
        [pltpu.VMEM((8, count, qkv_width + q_width), BF16)],
        1,
    )
    return (
        block_out[None],
        grad_in[None],
        grad_attn_gain,
        grad_query,
        grad_key,
        grad_value,
        grad_query_gain,
        grad_key_gain,
        grad_out,
        grad_ffn_gain,
        grad_gate,
        grad_up,
        grad_down,
    )


def solution(mesh):
    in_specs = (
        P(("dp", "fsdp"), "ctx", None),
        P(("dp", "fsdp"), None),
        P(("dp", "fsdp"), "ctx", None),
        P(),
        P("fsdp", None),
        P("fsdp", None),
        P("fsdp", None),
        P(),
        P(),
        P("fsdp", None),
        P(),
        P("fsdp", None),
        P("fsdp", None),
        P("fsdp", None),
    )
    out_specs = (
        P(("dp", "fsdp"), "ctx", None),
        P(("dp", "fsdp"), "ctx", None),
        P(),
        P("fsdp", None),
        P("fsdp", None),
        P("fsdp", None),
        P(),
        P(),
        P("fsdp", None),
        P(),
        P("fsdp", None),
        P("fsdp", None),
        P("fsdp", None),
    )
    return jax.shard_map(body, mesh=mesh, in_specs=in_specs, out_specs=out_specs, check_vma=False)
```

```python
import math

import jax
import jax.numpy as jnp
from jax import lax
from jax.experimental import pallas as pl
from jax.experimental.pallas import tpu as pltpu
from jax.sharding import PartitionSpec as P

NORM_EPSILON = 1e-05
ROPE_BASE = 1000000.0
MASKED_SCORE = -1e30
BF16 = jnp.bfloat16
F32 = jnp.float32
STEPS = (0, -1, 1, 2)
Y_STEPS = (1, 3, 2, 0)


def rms_scale(values):
    return lax.rsqrt(jnp.mean(values * values, axis=-1, keepdims=True) + NORM_EPSILON)


def rope_tables(places, head_size):
    half_width = head_size // 2
    pair_index = jnp.arange(half_width, dtype=F32)
    frequency = ROPE_BASE ** (-2.0 * pair_index / head_size)
    angles = frequency[:, None] * places.astype(F32)[None, :]
    return jnp.cos(angles), jnp.sin(angles)


def call(kernel, out_shapes, args, flops, scratch=(), scalars=0):
    vmem = pl.BlockSpec(memory_space=pltpu.VMEM)
    smem = pl.BlockSpec(memory_space=pltpu.SMEM)
    out_bytes = sum(math.prod(o.shape) * o.dtype.itemsize for o in out_shapes)
    in_bytes = sum(math.prod(a.shape) * a.dtype.itemsize for a in args)
    return pl.pallas_call(
        kernel,
        out_shape=out_shapes,
        in_specs=[smem] * scalars + [vmem] * (len(args) - scalars),
        out_specs=[vmem] * len(out_shapes),
        scratch_shapes=list(scratch),
        compiler_params=pltpu.CompilerParams(vmem_limit_bytes=40 * 2**20),
        cost_estimate=pl.CostEstimate(flops=flops, bytes_accessed=in_bytes + out_bytes, transcendentals=0),
    )(*args)


def shape(dims, kind):
    return jax.ShapeDtypeStruct(dims, kind)


def head_forward(values, gain, cosine, sine):
    scale = lax.rsqrt(jnp.mean(values * values, axis=0, keepdims=True) + NORM_EPSILON)
    hat = values * scale
    normed = hat * gain
    half = values.shape[0] // 2
    front, back = normed[:half], normed[half:]
    rotated = jnp.concatenate([front * cosine - back * sine, back * cosine + front * sine], axis=0)
    return scale, hat, rotated


def head_backward(grads, hat, scale, gain, cosine, sine):
    half = grads.shape[0] // 2
    front, back = grads[:half], grads[half:]
    d_normed = jnp.concatenate([front * cosine + back * sine, back * cosine - front * sine], axis=0)
    scaled = d_normed * gain
    inner = jnp.mean(hat * scaled, axis=0, keepdims=True)
    return scale * (scaled - hat * inner), jnp.sum(d_normed * hat, axis=1, keepdims=True)


def attend_forward(*refs):
    pieces, refs = refs[:8], refs[8:]
    w_qkv, cos_ref, sin_ref, column_ref, row_ref, q_gain, k_gain = refs[:7]
    qkv_ref, lse_ref, *mixed_refs = refs[7:]
    length = qkv_ref.shape[1]
    count = length // 8
    head = q_gain.shape[0]
    for pair in range(4):
        x = jnp.concatenate([pieces[2 * pair][...], pieces[2 * pair + 1][...]], axis=0)
        qkv_ref[:, pair * 2 * count : (pair + 1) * 2 * count] = jnp.transpose(mm(x, w_qkv[...]))
    cosine, sine = cos_ref[...], sin_ref[...]
    queries = [
        head_forward(qkv_ref[h * head : (h + 1) * head], q_gain[...], cosine, sine)[2].astype(BF16) * BF16(head**-0.5)
        for h in range(2)
    ]
    key = jnp.transpose(head_forward(qkv_ref[2 * head : 3 * head], k_gain[...], cosine, sine)[2]).astype(BF16)
    value = qkv_ref[3 * head :].astype(BF16)
    width = column_ref.shape[1]
    for tile in range(length // width):
        lanes = slice(tile * width, (tile + 1) * width)
        allowed = column_ref[...] <= row_ref[:, lanes]
        outs = []
        for h in range(2):
            scores = jnp.where(allowed, mm(key, queries[h][:, lanes]), MASKED_SCORE)
            top = jnp.max(scores, axis=0, keepdims=True)
            weights = jnp.exp(scores - top)
            total = jnp.sum(weights, axis=0, keepdims=True)
            lse_ref[h : h + 1, lanes] = top + jnp.log(total)
            outs.append(mm(value, (weights * (1.0 / total)).astype(BF16)))
        mixed = jnp.transpose(jnp.concatenate(outs, axis=0)).astype(BF16)
        mixed_refs[2 * tile][...] = mixed[:count]
        mixed_refs[2 * tile + 1][...] = mixed[count:]


def out_project(order, *refs):
    blocks, (w_out, tokens, gain, resid_ref, normed_ref, mixed_ref) = refs[:8], refs[8:]
    count = blocks[0].shape[1]
    for i in range(8):
        mixed_ref[:, pl.ds(pl.multiple_of(order[i] * count, count), count)] = blocks[i][...]
    resid = tokens[...].astype(F32) + mm(mixed_ref[...], w_out[...])
    resid_ref[...] = resid
    normed_ref[...] = (resid * rms_scale(resid) * gain[...]).astype(BF16)


def resid_backward(order, *refs):
    total, move_a, move_b, move_c, resid_ref, cot_ref, gain_ref, w_out = refs[:8]
    d_resid_ref, d_attn_ref, gain_part_ref = refs[8:11]
    block_refs, d_mixed_ref = refs[11:19], refs[19]
    d_second = total[...] + move_a[...].astype(F32) + move_b[...].astype(F32) + move_c[...].astype(F32)
    resid = resid_ref[...]
    scale = rms_scale(resid)
    d_from, gain_part = norm_back(d_second, resid * scale, scale, gain_ref[...])
    gain_part_ref[...] = jnp.sum(gain_part, axis=0, keepdims=True)
    d_resid = cot_ref[...].astype(F32) + d_from
    d_resid_ref[...] = d_resid
    d_attn = d_resid.astype(BF16)
    d_attn_ref[...] = d_attn
    d_mixed_ref[...] = mm_t(d_attn, w_out[...]).astype(BF16)
    count = block_refs[0].shape[1]
    for i in range(8):
        block_refs[i][...] = d_mixed_ref[:, pl.ds(pl.multiple_of(order[i] * count, count), count)]


def attend_backward(*refs):
    d_blocks, refs = refs[:8], refs[8:]
    w_qkv, cos_ref, sin_ref, column_ref, row_ref, q_gain, k_gain, qkv_ref, lse_ref = refs[:9]
    q_gain_ref, k_gain_ref, d_low_ref, send_ref = refs[9:13]
    mine_refs, d_qkv_ref = refs[13:17], refs[17]
    length = qkv_ref.shape[1]
    head = q_gain.shape[0]
    count = length // 8
    cosine, sine = cos_ref[...], sin_ref[...]
    scales, hats, queries = [], [], []
    for h in range(2):
        scale, hat, rotated = head_forward(qkv_ref[h * head : (h + 1) * head], q_gain[...], cosine, sine)
        scales.append(scale)
        hats.append(hat)
        queries.append(rotated.astype(BF16) * BF16(head**-0.5))
    k_scale, k_hat, rotated = head_forward(qkv_ref[2 * head : 3 * head], k_gain[...], cosine, sine)
    key_rows = rotated.astype(BF16)
    key = jnp.transpose(rotated).astype(BF16)
    value = jnp.transpose(qkv_ref[3 * head :]).astype(BF16)
    width = column_ref.shape[1]
    d_key = jnp.zeros((length, head), F32)
    d_value = jnp.zeros((length, head), F32)
    for tile in range(length // width):
        lanes = slice(tile * width, (tile + 1) * width)
        allowed = column_ref[...] <= row_ref[:, lanes]
        d_mixed = jnp.concatenate([d_blocks[2 * tile][...], d_blocks[2 * tile + 1][...]], axis=0)
        d_mixed = jnp.transpose(d_mixed.astype(F32)).astype(BF16)
        for h in range(2):
            rows = slice(h * head, (h + 1) * head)
            query = queries[h][:, lanes]
            probs = jnp.where(allowed, jnp.exp(mm(key, query) - lse_ref[h : h + 1, lanes]), 0.0)
            d_probs = mm(value, d_mixed[rows])
            inner = jnp.sum(probs * d_probs, axis=0, keepdims=True)
            d_scores = (probs * (d_probs - inner)).astype(BF16)
            d_value += mm_t(probs.astype(BF16), d_mixed[rows])
            d_key += mm_t(d_scores, query)
            d_qkv_ref[rows, lanes] = mm(key_rows, d_scores) * head**-0.5
    for h in range(2):
        rows = slice(h * head, (h + 1) * head)
        d_query, gain_part = head_backward(d_qkv_ref[rows], hats[h], scales[h], q_gain[...], cosine, sine)
        d_qkv_ref[rows] = d_query
        if h == 0:
            q_gain_ref[...] = gain_part
        else:
            q_gain_ref[...] += gain_part
    d_keys, gain_part = head_backward(jnp.transpose(d_key), k_hat, k_scale, k_gain[...], cosine, sine)
    k_gain_ref[...] = gain_part
    d_qkv_ref[2 * head : 3 * head] = d_keys
    d_qkv_ref[3 * head :] = jnp.transpose(d_value)
    for tile in range(4):
        lanes = slice(tile * 2 * count, (tile + 1) * 2 * count)
        d_qkv = jnp.transpose(d_qkv_ref[:, lanes]).astype(BF16)
        d_low_ref[lanes] = d_qkv
        d_first = mm_t(d_qkv, w_qkv[...])
        mine_refs[tile][...] = d_first[:count]
        send_ref[tile] = d_first[count:].astype(BF16)


def attend_weights(*refs):
    place, pieces, d_pieces, blocks = refs[0], refs[1:9], refs[9:17], refs[17:25]
    d_low_ref, w_qkv, attn_gain_ref = refs[25:28]
    part_refs, x_ref, mixed_ref, grads_ref = refs[28:36], refs[36], refs[37], refs[38]
    count = pieces[0].shape[0]
    width = d_low_ref.shape[1]
    for i in range(8):
        x_ref[i * count : (i + 1) * count] = pieces[i][...]
        mixed_ref[i * count : (i + 1) * count] = blocks[i][...]
    grad_qkv = outer_sum(d_low_ref[...], x_ref[...])
    attn_gain_ref[...] = jnp.sum(grad_qkv * jnp.transpose(w_qkv[...].astype(F32)), axis=0, keepdims=True)
    grads_ref[:, :width] = jnp.transpose(grad_qkv).astype(BF16)
    for i in range(8):
        x_ref[i * count : (i + 1) * count] = d_pieces[i][...]
    grads_ref[:, width:] = jnp.transpose(outer_sum(mixed_ref[...], x_ref[...])).astype(BF16)
    for i, step in enumerate(Y_STEPS):
        for flip in (0, 1):
            owner = (place[0] + step) % 4 * 2 + (place[1] ^ flip)
            part_refs[2 * i + flip][...] = grads_ref[pl.ds(pl.multiple_of(owner * count, count), count)]


def ffn(*refs):
    seconds, cots, weights = refs[:8], refs[8:16], refs[16]
    hidden_ref, d_ffn_ref, d_send, send = refs[17:21]
    d_mine, mine = refs[21:25], refs[25:29]
    width = hidden_ref.shape[1]
    count = seconds[0].shape[0]
    for group in (3, 1, 2, 0):
        rows = slice(2 * group * count, 2 * (group + 1) * count)
        x = jnp.concatenate([seconds[2 * group][...], seconds[2 * group + 1][...]], axis=0)
        cot = jnp.concatenate([cots[2 * group][...], cots[2 * group + 1][...]], axis=0)
        both = mm(x, weights[:, : 2 * width])
        gate, up = both[:, :width], both[:, width:]
        sigmoid = 1.0 / (1.0 + jnp.exp(-gate))
        act = gate * sigmoid
        hidden = (act * up).astype(BF16)
        hidden_ref[rows] = hidden
        d_hidden = mm(cot, weights[:, 2 * width :])
        d_gate = d_hidden * up * sigmoid * (1.0 + gate * (1.0 - sigmoid))
        d_ffn = jnp.concatenate([d_gate, d_hidden * act], axis=1).astype(BF16)
        d_ffn_ref[rows] = d_ffn
        d_second = mm_t(d_ffn, weights[:, : 2 * width])
        d_mine[group][...] = d_second[:count]
        d_send[group] = d_second[count:].astype(BF16)
        out = mm_t(hidden, weights[:, 2 * width :])
        mine[group][...] = out[:count]
        send[group] = out[count:].astype(BF16)


def ffn_weights(*refs):
    place, seconds, cots, hidden_ref, d_ffn_ref = refs[0], refs[1:9], refs[9:17], refs[17], refs[18]
    part_refs, x_ref = refs[19:27], refs[27]
    count = seconds[0].shape[0]
    for pieces, other_ref, columns in ((seconds, d_ffn_ref, 0), (cots, hidden_ref, d_ffn_ref.shape[1])):
        for i in range(8):
            x_ref[i * count : (i + 1) * count] = pieces[i][...]
        width = other_ref.shape[1]
        for i, step in enumerate(Y_STEPS):
            rows = pl.ds(pl.multiple_of((place[0] + step) % 4 * (2 * count), 2 * count), 2 * count)
            both = outer_sum(x_ref[:, rows], other_ref[...])
            low, high = both[:count], both[count:]
            first = place[1] == 0
            part_refs[2 * i][:, columns : columns + width] = jnp.where(first, low, high).astype(BF16)
            part_refs[2 * i + 1][:, columns : columns + width] = jnp.where(first, high, low).astype(BF16)


def assemble_ffn(*refs):
    order, pieces, (gate_ref, up_ref, down_ref, held) = refs[0], refs[1:9], refs[9:]
    width = down_ref.shape[0]
    count = pieces[0].shape[0]
    for i in range(8):
        held[order[i]] = pieces[i][...]
    for owner in range(8):
        columns = slice(owner * width, (owner + 1) * width)
        gate_ref[:, columns] = held[owner, :, :width].astype(F32)
        up_ref[:, columns] = held[owner, :, width : 2 * width].astype(F32)
        down = held[owner, :, 2 * width :].astype(F32)
        down_ref[:, owner * count : (owner + 1) * count] = jnp.transpose(down)


def assemble_attn(*refs):
    order, pieces, (query_ref, key_ref, value_ref, out_ref, held) = refs[0], refs[1:9], refs[9:]
    count = pieces[0].shape[0]
    half = count // 2
    for i in range(8):
        held[order[i]] = pieces[i][...]
    for owner in range(8):
        columns = slice(owner * count, (owner + 1) * count)
        narrow = slice(owner * half, (owner + 1) * half)
        part = held[owner].astype(F32)
        query_ref[:, columns] = part[:, :count]
        key_ref[:, narrow] = part[:, count : count + half]
        value_ref[:, narrow] = part[:, count + half : 2 * count]
        out_ref[:, columns] = jnp.transpose(part[:, 2 * count :])


def norm_back(d_normed, normed_hat, scale_values, gain_vector):
    scaled = d_normed * gain_vector
    inner = jnp.mean(normed_hat * scaled, axis=-1, keepdims=True)
    return (scale_values * (scaled - normed_hat * inner), d_normed * normed_hat)


def mm(left, right):
    return jnp.dot(left, right, preferred_element_type=F32)


def mm_t(left, right):
    return lax.dot_general(left, right, (((1,), (1,)), ((), ())), preferred_element_type=F32)


def outer_sum(left, right):
    return lax.dot_general(left, right, (((0,), (0,)), ((), ())), preferred_element_type=F32)


def swap_core(value):
    return lax.ppermute(value, "ctx", [(i, i ^ 1) for i in range(8)])


def move_z(value, step):
    return lax.ppermute(value, "ctx", [(i, (i + 2 * step) % 8) for i in range(8)])


def gather_ctx(block):
    pieces = []
    for step in STEPS:
        mine = block if step == 0 else move_z(block, -step)
        pieces += [mine, swap_core(mine)]
    return pieces


def start_scatter_ctx(mine, received):
    sums = [own + other.astype(F32) for own, other in zip(mine, received)]
    return [sums[0]] + [move_z(sums[slot].astype(BF16), STEPS[slot]) for slot in (3, 1, 2)]


def end_scatter(moves):
    return sum(move.astype(F32) for move in moves)


def scatter_ctx(mine, received):
    return end_scatter(start_scatter_ctx(mine, received))


def exchange_ctx(blocks):
    out = [None] * 8
    for i, step in enumerate(STEPS):
        back = (0, 2, 1, 3)[i]
        for flip in (0, 1):
            pairs = [(c, (c // 2 + step) % 4 * 2 + (c % 2 ^ flip)) for c in range(8)]
            block = blocks[2 * i + flip]
            out[2 * back + flip] = lax.ppermute(block, "ctx", pairs) if step or flip else block
    return out


def stage(*values):
    return lax.optimization_barrier(values)


def swap_pieces(moved):
    pieces = []
    for piece in moved:
        pieces += [piece, swap_core(piece)]
    return pieces


def transpose_mesh(value, flip=0):
    pairs = [
        ((d * 8 + c) * 8 + f, ((d ^ flip) * 8 + f) * 8 + c) for d in range(2) for c in range(8) for f in range(8)
    ]
    return lax.ppermute(value, ("dp", "ctx", "fsdp"), pairs)


def swap_dp(value):
    return lax.ppermute(value, "dp", [(0, 1), (1, 0)])


def after(value, *others):
    return lax.optimization_barrier((value, *others))[0]


def move_y(value, step, flip=0):
    pairs = [(y * 2 + x, (y + step) % 4 * 2 + (x ^ flip)) for y in range(4) for x in range(2)]
    return lax.ppermute(value, "fsdp", pairs)


def spread_y(held):
    return [move_y(held, step) if step else held for step in (0, 1, 3, 2)]


def join_fsdp(own_side, other_side):
    me = lax.axis_index("fsdp")
    rows, columns = own_side[0].shape
    whole = jnp.zeros((8 * rows, columns), BF16)
    for flip, side in ((0, own_side), (1, other_side)):
        for step, piece in zip((0, 1, 3, 2), side):
            owner = (me // 2 - step) % 4 * 2 + (me % 2 ^ flip)
            whole = lax.dynamic_update_slice_in_dim(whole, piece, owner * rows, 0)
    return whole


def start_sum_fsdp(pieces):
    return [
        [pieces[2 * i + flip] if step == 0 else move_y(pieces[2 * i + flip], step) for flip in (1, 0)]
        for i, step in enumerate(Y_STEPS)
    ]


def end_sum_fsdp(moved):
    other, own = (sum(pair[i].astype(F32) for pair in moved) for i in (0, 1))
    return (own + move_y(other.astype(BF16), 0, 1).astype(F32)).astype(BF16)


def sum_dp(low):
    return (low.astype(F32) + swap_dp(low).astype(F32)).astype(BF16)


def sum_dp_transposed(low):
    return (transpose_mesh(low).astype(F32) + transpose_mesh(low, 1).astype(F32)).astype(BF16)


def sum_all(value):
    total = value + swap_core(value)
    total = total + move_z(total, 1) + move_z(total, -1) + move_z(total, 2)
    total = total + move_y(total, 1) + move_y(total, 3) + move_y(total, 2)
    total = total + swap_dp(total)
    return total + move_y(total, 0, 1)


def own_columns(weight, width, index):
    return lax.dynamic_slice_in_dim(weight, index * width, width, 1)


def body(
    hidden_in,
    positions,
    cotangent,
    attn_gain,
    w_query,
    w_key,
    w_value,
    query_gain,
    key_gain,
    w_out,
    ffn_gain,
    w_gate,
    w_up,
    w_down,
):
    ctx = lax.axis_index("ctx")
    tokens = hidden_in[0].astype(F32)
    count, width = tokens.shape
    head_size = query_gain.shape[0]
    q_width = w_query.shape[1] // 8
    k_width = w_key.shape[1] // 8
    ff_width = w_gate.shape[1] // 8

    z_index, core = ctx // 2, ctx % 2
    owners = jnp.stack(
        [((z_index + step) % 4) * 2 + (core ^ flip) for step in STEPS for flip in (0, 1)]
    )
    place = jnp.stack([lax.axis_index("fsdp") // 2, lax.axis_index("fsdp") % 2])
    places = positions[0].reshape(8, count)[owners].reshape(8 * count)
    length = 8 * count
    cosine_table, sine_table = rope_tables(places, head_size)
    column = jnp.broadcast_to(places[:, None], (length, 2 * count))
    row = places[None]
    gains = (query_gain[:, None], key_gain[:, None])
    tables = (cosine_table, sine_table, column, row)
    block = shape((count, q_width), BF16)
    low_rows, rows = shape((count, width), BF16), shape((count, width), F32)
    qkv_width = q_width + 2 * k_width

    first_scale = rms_scale(tokens)
    first_hat = tokens * first_scale
    first_normed = (first_hat * attn_gain).astype(BF16)
    first_pieces = gather_ctx(first_normed)
    qkv_block = jnp.concatenate(
        [own_columns(w_query, q_width, ctx), own_columns(w_key, k_width, ctx), own_columns(w_value, k_width, ctx)],
        axis=1,
    )
    w_qkv = join_fsdp(spread_y(qkv_block), spread_y(move_y(qkv_block, 0, 1)))
    out_other = move_y(w_out, 0, 1)
    down_chunk = transpose_mesh(jnp.transpose(own_columns(w_down, width // 8, ctx)))
    ffn_block = jnp.concatenate(
        [own_columns(w_gate, ff_width, ctx), own_columns(w_up, ff_width, ctx), down_chunk], axis=1
    )
    first_pieces, w_qkv, tables, w_out, out_other, ffn_block, cot = stage(
        first_pieces, w_qkv, tables, w_out, out_other, ffn_block, cotangent[0]
    )

    out_sides = (spread_y(w_out), spread_y(out_other))
    cot_near = [move_z(cot, 1), move_z(cot, -1)]
    qkv, lse, *mixed_blocks = call(
        attend_forward,
        [shape((qkv_width, length), F32), shape((8, length), F32)] + [block] * 8,
        (*first_pieces, w_qkv, *tables, *gains),
        4 * 10**9,
    )
    mixed_blocks, out_sides, cot_near, ffn_block = stage(mixed_blocks, out_sides, cot_near, ffn_block)

    ffn_other = move_y(ffn_block, 0, 1)
    ffn_own = spread_y(ffn_block)
    w_out_whole = join_fsdp(*out_sides)
    own_blocks = exchange_ctx(mixed_blocks)
    own_blocks, w_out_whole, ffn_other, cot = stage(own_blocks, w_out_whole, ffn_other, cot)
    residual, second_normed = call(
        out_project,
        [rows, low_rows],
        (owners, *own_blocks, w_out_whole, hidden_in[0], ffn_gain[None]),
        3 * 10**8,
        [pltpu.VMEM((count, width), BF16)],
        1,
    )

    second_pieces = gather_ctx(second_normed)
    ffn_sides = (ffn_own, spread_y(ffn_other))
    cot_pieces = swap_pieces([cot, *cot_near, move_z(cot, 2)])
    second_pieces, ffn_sides, cot_pieces = stage(second_pieces, ffn_sides, cot_pieces)
    hidden, d_ffn, d_send, send, *parts = call(
        ffn,
        [
            shape((length, ff_width), BF16),
            shape((length, 2 * ff_width), BF16),
            shape((4, count, width), BF16),
            shape((4, count, width), BF16),
        ]
        + [rows] * 8,
        (*second_pieces, *cot_pieces, join_fsdp(*ffn_sides)),
        8 * 10**9,
    )

    d_mine, mine = parts[:4], parts[4:]
    d_moves = start_scatter_ctx(d_mine, swap_core(d_send))
    ffn_partial = call(
        ffn_weights,
        [shape((count, 3 * ff_width), BF16)] * 8,
        (place, *second_pieces, *cot_pieces, hidden, d_ffn),
        4 * 10**9,
        [pltpu.VMEM((length, width), BF16)],
        1,
    )
    d_moves, ffn_partial, send = stage(d_moves, ffn_partial, send)
    d_resid, d_attn, ffn_gain_part, *d_blocks = call(
        resid_backward,
        [rows, low_rows, shape((1, width), F32)] + [block] * 8,
        (owners, *d_moves, residual, cot, ffn_gain[None], w_out_whole),
        3 * 10**8,
        [pltpu.VMEM((count, width), BF16)],
        1,
    )

    ffn_moved = start_sum_fsdp(ffn_partial)
    received = swap_core(send)
    d_blocks = exchange_ctx(d_blocks)
    d_blocks, ffn_moved, received, d_attn = stage(d_blocks, ffn_moved, received, d_attn)

    d_near = [move_z(d_attn, 1), move_z(d_attn, -1)]
    ffn_sum = end_sum_fsdp(ffn_moved)
    q_gain_part, k_gain_part, d_qkv, send, *d_first_mine = call(
        attend_backward,
        [
            shape((head_size, 1), F32),
            shape((head_size, 1), F32),
            shape((length, qkv_width), BF16),
            shape((4, count, width), BF16),
        ]
        + [rows] * 4,
        (*d_blocks, w_qkv, *tables, *gains, qkv, lse),
        8 * 10**9,
        [pltpu.VMEM((qkv_width, length), F32)],
    )
    d_qkv, send, d_first_mine, d_near, ffn_sum, d_attn = stage(d_qkv, send, d_first_mine, d_near, ffn_sum, d_attn)

    d_pieces = swap_pieces([d_attn, *d_near, move_z(d_attn, 2)])
    ffn_gate_up, ffn_down = ffn_sum[:, : 2 * ff_width], ffn_sum[:, 2 * ff_width :]
    ffn_steps = [ffn_gate_up, swap_dp(ffn_gate_up), transpose_mesh(ffn_down), transpose_mesh(ffn_down, 1)]
    d_first_moves = start_scatter_ctx(d_first_mine, swap_core(send))
    attn_gain_part, *attn_partial = call(
        attend_weights,
        [shape((1, width), F32)] + [shape((count, qkv_width + q_width), BF16)] * 8,
        (place, *first_pieces, *d_pieces, *mixed_blocks, d_qkv, w_qkv),
        10**9,
        [
            pltpu.VMEM((length, width), BF16),
            pltpu.VMEM((length, q_width), BF16),
            pltpu.VMEM((width, qkv_width + q_width), BF16),
        ],
        1,
    )
    attn_partial, attn_gain_part, ffn_steps, mine = stage(attn_partial, attn_gain_part, ffn_steps, mine)

    totals = sum_all(
        jnp.concatenate(
            [attn_gain_part[0] / attn_gain, ffn_gain_part[0], q_gain_part[:, 0], k_gain_part[:, 0]]
        ).reshape(-1, 128)
    ).reshape(-1)
    grad_attn_gain = totals[:width]
    grad_ffn_gain = totals[width : 2 * width]
    grad_query_gain = totals[2 * width : 2 * width + head_size]
    grad_key_gain = totals[2 * width + head_size :]
    attn_moved = start_sum_fsdp(attn_partial)
    ffn_steps = [step.astype(F32) for step in ffn_steps]
    ffn_parts = gather_ctx(
        jnp.concatenate([ffn_steps[0] + ffn_steps[1], ffn_steps[2] + ffn_steps[3]], axis=1).astype(BF16)
    )
    attn_sum = end_sum_fsdp(attn_moved)
    d_from_first, _ = norm_back(end_scatter(d_first_moves), first_hat, first_scale, attn_gain)
    grad_in = (d_resid + d_from_first).astype(BF16)
    block_out = (residual + scatter_ctx(mine, received)).astype(BF16)
    attn_parts = gather_ctx(
        jnp.concatenate([sum_dp(attn_sum[:, :qkv_width]), sum_dp_transposed(attn_sum[:, qkv_width:])], axis=1)
    )
    grad_gate, grad_up, grad_down = call(
        assemble_ffn,
        [shape((count, 8 * ff_width), F32)] * 2 + [shape((ff_width, width), F32)],
        (owners, *ffn_parts),
        10**6,
        [pltpu.VMEM((8, count, 3 * ff_width), BF16)],
        1,
    )
    grad_query, grad_key, grad_value, grad_out = call(
        assemble_attn,
        [shape((count, width), F32)] + [shape((count, 8 * k_width), F32)] * 2 + [shape((q_width, width), F32)],
        (owners, *attn_parts),
        10**6,
        [pltpu.VMEM((8, count, qkv_width + q_width), BF16)],
        1,
    )
    return (
        block_out[None],
        grad_in[None],
        grad_attn_gain,
        grad_query,
        grad_key,
        grad_value,
        grad_query_gain,
        grad_key_gain,
        grad_out,
        grad_ffn_gain,
        grad_gate,
        grad_up,
        grad_down,
    )


def solution(mesh):
    in_specs = (
        P(("dp", "fsdp"), "ctx", None),
        P(("dp", "fsdp"), None),
        P(("dp", "fsdp"), "ctx", None),
        P(),
        P("fsdp", None),
        P("fsdp", None),
        P("fsdp", None),
        P(),
        P(),
        P("fsdp", None),
        P(),
        P("fsdp", None),
        P("fsdp", None),
        P("fsdp", None),
    )
    out_specs = (
        P(("dp", "fsdp"), "ctx", None),
        P(("dp", "fsdp"), "ctx", None),
        P(),
        P("fsdp", None),
        P("fsdp", None),
        P("fsdp", None),
        P(),
        P(),
        P("fsdp", None),
        P(),
        P("fsdp", None),
        P("fsdp", None),
        P("fsdp", None),
    )
    return jax.shard_map(body, mesh=mesh, in_specs=in_specs, out_specs=out_specs, check_vma=False)
```

```python
import math

import jax
import jax.numpy as jnp
from jax import lax
from jax.experimental import pallas as pl
from jax.experimental.pallas import tpu as pltpu
from jax.sharding import PartitionSpec as P

NORM_EPSILON = 1e-05
ROPE_BASE = 1000000.0
MASKED_SCORE = -1e30
BF16 = jnp.bfloat16
F32 = jnp.float32
STEPS = (0, -1, 1, 2)


def rms_scale(values):
    return lax.rsqrt(jnp.mean(values * values, axis=-1, keepdims=True) + NORM_EPSILON)


def rope_tables(places, head_size):
    half_width = head_size // 2
    pair_index = jnp.arange(half_width, dtype=F32)
    frequency = ROPE_BASE ** (-2.0 * pair_index / head_size)
    angles = frequency[:, None] * places.astype(F32)[None, :]
    return jnp.cos(angles), jnp.sin(angles)


def call(kernel, out_shapes, args, flops, scratch=(), scalars=0):
    vmem = pl.BlockSpec(memory_space=pltpu.VMEM)
    smem = pl.BlockSpec(memory_space=pltpu.SMEM)
    out_bytes = sum(math.prod(o.shape) * o.dtype.itemsize for o in out_shapes)
    in_bytes = sum(math.prod(a.shape) * a.dtype.itemsize for a in args)
    return pl.pallas_call(
        kernel,
        out_shape=out_shapes,
        in_specs=[smem] * scalars + [vmem] * (len(args) - scalars),
        out_specs=[vmem] * len(out_shapes),
        scratch_shapes=list(scratch),
        compiler_params=pltpu.CompilerParams(vmem_limit_bytes=40 * 2**20),
        cost_estimate=pl.CostEstimate(flops=flops, bytes_accessed=in_bytes + out_bytes, transcendentals=0),
    )(*args)


def shape(dims, kind):
    return jax.ShapeDtypeStruct(dims, kind)


def head_forward(values, gain, cosine, sine):
    scale = lax.rsqrt(jnp.mean(values * values, axis=0, keepdims=True) + NORM_EPSILON)
    hat = values * scale
    normed = hat * gain
    half = values.shape[0] // 2
    front, back = normed[:half], normed[half:]
    rotated = jnp.concatenate([front * cosine - back * sine, back * cosine + front * sine], axis=0)
    return scale, hat, rotated


def head_backward(grads, hat, scale, gain, cosine, sine):
    half = grads.shape[0] // 2
    front, back = grads[:half], grads[half:]
    d_normed = jnp.concatenate([front * cosine + back * sine, back * cosine - front * sine], axis=0)
    scaled = d_normed * gain
    inner = jnp.mean(hat * scaled, axis=0, keepdims=True)
    return scale * (scaled - hat * inner), jnp.sum(d_normed * hat, axis=1, keepdims=True)


def norm_back(d_normed, normed_hat, scale_values, gain_vector):
    scaled = d_normed * gain_vector
    inner = jnp.mean(normed_hat * scaled, axis=-1, keepdims=True)
    return (scale_values * (scaled - normed_hat * inner), d_normed * normed_hat)


def mm(left, right):
    return jnp.dot(left, right, preferred_element_type=F32)


def mm_t(left, right):
    return lax.dot_general(left, right, (((1,), (1,)), ((), ())), preferred_element_type=F32)


def outer_sum(left, right):
    return lax.dot_general(left, right, (((0,), (0,)), ((), ())), preferred_element_type=F32)


def swap_core(value):
    return lax.ppermute(value, "ctx", [(i, i ^ 1) for i in range(8)])


def move_z(value, step):
    return lax.ppermute(value, "ctx", [(i, (i + 2 * step) % 8) for i in range(8)])


def gather_ctx(block):
    pieces = []
    for step in STEPS:
        mine = block if step == 0 else move_z(block, -step)
        pieces += [mine, swap_core(mine)]
    return pieces


def start_scatter_ctx(mine, received):
    sums = [own + other.astype(F32) for own, other in zip(mine, received)]
    return [sums[0]] + [move_z(sums[slot].astype(BF16), STEPS[slot]) for slot in (3, 1, 2)]


def exchange_ctx(blocks):
    out = [None] * 8
    for i, step in enumerate(STEPS):
        back = (0, 2, 1, 3)[i]
        for flip in (0, 1):
            pairs = [(c, (c // 2 + step) % 4 * 2 + (c % 2 ^ flip)) for c in range(8)]
            block = blocks[2 * i + flip]
            out[2 * back + flip] = lax.ppermute(block, "ctx", pairs) if step or flip else block
    return out


def stage(*values):
    return lax.optimization_barrier(values)


def transpose_mesh(value, flip=0):
    pairs = [
        ((d * 8 + c) * 8 + f, ((d ^ flip) * 8 + f) * 8 + c) for d in range(2) for c in range(8) for f in range(8)
    ]
    return lax.ppermute(value, ("dp", "ctx", "fsdp"), pairs)


def swap_dp(value):
    return lax.ppermute(value, "dp", [(0, 1), (1, 0)])


def move_y(value, step, flip=0):
    pairs = [(y * 2 + x, (y + step) % 4 * 2 + (x ^ flip)) for y in range(4) for x in range(2)]
    return lax.ppermute(value, "fsdp", pairs)


def pair_x(block):
    other = move_y(block, 0, 1)
    first = lax.axis_index("fsdp") % 2 == 0
    return jnp.concatenate([jnp.where(first, block, other), jnp.where(first, other, block)], axis=0)


def spread_y(pair):
    return [pair] + [move_y(pair, step) for step in (1, 3, 2)]


def join_y(pairs):
    y = lax.axis_index("fsdp") // 2
    rows, columns = pairs[0].shape
    whole = jnp.zeros((4 * rows, columns), BF16)
    for step, pair in zip((0, 1, 3, 2), pairs):
        whole = lax.dynamic_update_slice_in_dim(whole, pair, (y - step) % 4 * rows, 0)
    return whole


def all_to_all(blocks, axis):
    return lax.all_to_all(blocks, axis, split_axis=0, concat_axis=0, tiled=True)


def own_columns(weight, width, index):
    return lax.dynamic_slice_in_dim(weight, index * width, width, 1)


def attend_forward(*refs):
    pieces, refs = refs[:8], refs[8:]
    w_qkv, cos_ref, sin_ref, column_ref, row_ref, q_gain, k_gain = refs[:7]
    qkv_ref, lse_ref, *mixed_refs = refs[7:]
    length = qkv_ref.shape[1]
    count = length // 8
    head = q_gain.shape[0]
    for pair in range(4):
        x = jnp.concatenate([pieces[2 * pair][...], pieces[2 * pair + 1][...]], axis=0)
        qkv_ref[:, pair * 2 * count : (pair + 1) * 2 * count] = jnp.transpose(mm(x, w_qkv[...]))
    cosine, sine = cos_ref[...], sin_ref[...]
    queries = [
        head_forward(qkv_ref[h * head : (h + 1) * head], q_gain[...], cosine, sine)[2].astype(BF16) * BF16(head**-0.5)
        for h in range(2)
    ]
    key = jnp.transpose(head_forward(qkv_ref[2 * head : 3 * head], k_gain[...], cosine, sine)[2]).astype(BF16)
    value = qkv_ref[3 * head :].astype(BF16)
    width = column_ref.shape[1]
    for tile in range(length // width):
        lanes = slice(tile * width, (tile + 1) * width)
        allowed = column_ref[...] <= row_ref[:, lanes]
        outs = []
        for h in range(2):
            scores = jnp.where(allowed, mm(key, queries[h][:, lanes]), MASKED_SCORE)
            top = jnp.max(scores, axis=0, keepdims=True)
            weights = jnp.exp(scores - top)
            total = jnp.sum(weights, axis=0, keepdims=True)
            lse_ref[h : h + 1, lanes] = top + jnp.log(total)
            outs.append(mm(value, (weights * (1.0 / total)).astype(BF16)))
        mixed = jnp.transpose(jnp.concatenate(outs, axis=0)).astype(BF16)
        mixed_refs[2 * tile][...] = mixed[:count]
        mixed_refs[2 * tile + 1][...] = mixed[count:]


def out_project(order, *refs):
    blocks, (w_out, tokens, gain, resid_ref, normed_ref, mixed_ref) = refs[:8], refs[8:]
    count = blocks[0].shape[1]
    for i in range(8):
        mixed_ref[:, pl.ds(pl.multiple_of(order[i] * count, count), count)] = blocks[i][...]
    resid = tokens[...].astype(F32) + mm(mixed_ref[...], w_out[...])
    resid_ref[...] = resid
    normed_ref[...] = (resid * rms_scale(resid) * gain[...]).astype(BF16)


def resid_backward(order, *refs):
    total, move_a, move_b, move_c, resid_ref, cot_ref, gain_ref, w_out = refs[:8]
    d_resid_ref, d_attn_ref, gain_part_ref = refs[8:11]
    block_refs, d_mixed_ref = refs[11:19], refs[19]
    d_second = total[...] + move_a[...].astype(F32) + move_b[...].astype(F32) + move_c[...].astype(F32)
    resid = resid_ref[...]
    scale = rms_scale(resid)
    d_from, gain_part = norm_back(d_second, resid * scale, scale, gain_ref[...])
    gain_part_ref[...] = jnp.sum(gain_part, axis=0, keepdims=True)
    d_resid = cot_ref[...].astype(F32) + d_from
    d_resid_ref[...] = d_resid
    d_attn = d_resid.astype(BF16)
    d_attn_ref[...] = d_attn
    d_mixed_ref[...] = mm_t(d_attn, w_out[...]).astype(BF16)
    count = block_refs[0].shape[1]
    for i in range(8):
        block_refs[i][...] = d_mixed_ref[:, pl.ds(pl.multiple_of(order[i] * count, count), count)]


def attend_backward(*refs):
    order, d_blocks, refs = refs[0], refs[1:9], refs[9:]
    w_qkv, cos_ref, sin_ref, column_ref, row_ref, q_gain, k_gain, qkv_ref, lse_ref = refs[:9]
    q_gain_ref, k_gain_ref, d_low_ref, d_first_ref, d_qkv_ref = refs[9:]
    length = qkv_ref.shape[1]
    head = q_gain.shape[0]
    count = length // 8
    cosine, sine = cos_ref[...], sin_ref[...]
    scales, hats, queries = [], [], []
    for h in range(2):
        scale, hat, rotated = head_forward(qkv_ref[h * head : (h + 1) * head], q_gain[...], cosine, sine)
        scales.append(scale)
        hats.append(hat)
        queries.append(rotated.astype(BF16) * BF16(head**-0.5))
    k_scale, k_hat, rotated = head_forward(qkv_ref[2 * head : 3 * head], k_gain[...], cosine, sine)
    key_rows = rotated.astype(BF16)
    key = jnp.transpose(rotated).astype(BF16)
    value = jnp.transpose(qkv_ref[3 * head :]).astype(BF16)
    width = column_ref.shape[1]
    d_key = jnp.zeros((length, head), F32)
    d_value = jnp.zeros((length, head), F32)
    for tile in range(length // width):
        lanes = slice(tile * width, (tile + 1) * width)
        allowed = column_ref[...] <= row_ref[:, lanes]
        d_mixed = jnp.concatenate([d_blocks[2 * tile][...], d_blocks[2 * tile + 1][...]], axis=0)
        d_mixed = jnp.transpose(d_mixed.astype(F32)).astype(BF16)
        for h in range(2):
            rows = slice(h * head, (h + 1) * head)
            query = queries[h][:, lanes]
            probs = jnp.where(allowed, jnp.exp(mm(key, query) - lse_ref[h : h + 1, lanes]), 0.0)
            d_probs = mm(value, d_mixed[rows])
            inner = jnp.sum(probs * d_probs, axis=0, keepdims=True)
            d_scores = (probs * (d_probs - inner)).astype(BF16)
            d_value += mm_t(probs.astype(BF16), d_mixed[rows])
            d_key += mm_t(d_scores, query)
            d_qkv_ref[rows, lanes] = mm(key_rows, d_scores) * head**-0.5
    for h in range(2):
        rows = slice(h * head, (h + 1) * head)
        d_query, gain_part = head_backward(d_qkv_ref[rows], hats[h], scales[h], q_gain[...], cosine, sine)
        d_qkv_ref[rows] = d_query
        if h == 0:
            q_gain_ref[...] = gain_part
        else:
            q_gain_ref[...] += gain_part
    d_keys, gain_part = head_backward(jnp.transpose(d_key), k_hat, k_scale, k_gain[...], cosine, sine)
    k_gain_ref[...] = gain_part
    d_qkv_ref[2 * head : 3 * head] = d_keys
    d_qkv_ref[3 * head :] = jnp.transpose(d_value)
    for tile in range(4):
        lanes = slice(tile * 2 * count, (tile + 1) * 2 * count)
        d_qkv = jnp.transpose(d_qkv_ref[:, lanes]).astype(BF16)
        d_low_ref[lanes] = d_qkv
        d_first = mm_t(d_qkv, w_qkv[...])
        d_first_ref[order[2 * tile]] = d_first[:count].astype(BF16)
        d_first_ref[order[2 * tile + 1]] = d_first[count:].astype(BF16)


def attend_weights(*refs):
    pieces, d_pieces, blocks = refs[:8], refs[8:16], refs[16:24]
    d_low_ref, w_qkv, attn_gain, ffn_part, q_part, k_part = refs[24:30]
    out_ref, x_ref, mixed_ref = refs[30:]
    count = pieces[0].shape[0]
    width = d_low_ref.shape[1]
    for i in range(8):
        x_ref[i * count : (i + 1) * count] = pieces[i][...]
        mixed_ref[i * count : (i + 1) * count] = blocks[i][...]
    grad_qkv = outer_sum(d_low_ref[...], x_ref[...])
    attn_part = jnp.sum(grad_qkv * jnp.transpose(w_qkv[...].astype(F32)), axis=0, keepdims=True) / attn_gain[...]
    grad_qkv = jnp.transpose(grad_qkv).astype(BF16)
    for i in range(8):
        x_ref[i * count : (i + 1) * count] = d_pieces[i][...]
    grad_out = jnp.transpose(outer_sum(mixed_ref[...], x_ref[...])).astype(BF16)
    lines = [part[:, i * 128 : (i + 1) * 128] for part in (attn_part, ffn_part[...]) for i in range(8)]
    lines.append(jnp.concatenate([jnp.transpose(q_part[...]), jnp.transpose(k_part[...])], axis=1))
    gains = jnp.concatenate(lines + [jnp.zeros((7, 128), F32)], axis=0)
    high = gains.astype(BF16)
    low = (gains - high.astype(F32)).astype(BF16)
    gains = jnp.concatenate([high, low, jnp.zeros((count - 48, 128), BF16)], axis=0)
    for i in range(8):
        rows = slice(i * count, (i + 1) * count)
        out_ref[i, :, :width] = grad_qkv[rows]
        out_ref[i, :, width : width + 128] = gains
        out_ref[i, :, width + 128 :] = grad_out[rows]


def ffn(*refs):
    order, seconds, cots, gate_up, down = refs[0], refs[1:9], refs[9], refs[10], refs[11]
    hidden_ref, d_ffn_ref, block_ref, d_send = refs[12:16]
    d_mine = refs[16:20]
    width = hidden_ref.shape[1]
    count = seconds[0].shape[0]
    for group in (3, 1, 2, 0):
        rows = slice(2 * group * count, 2 * (group + 1) * count)
        x = jnp.concatenate([seconds[2 * group][...], seconds[2 * group + 1][...]], axis=0)
        cot = jnp.concatenate([cots[order[2 * group]], cots[order[2 * group + 1]]], axis=0)
        both = mm(x, gate_up[...])
        gate, up = both[:, :width], both[:, width:]
        sigmoid = 1.0 / (1.0 + jnp.exp(-gate))
        act = gate * sigmoid
        hidden = (act * up).astype(BF16)
        hidden_ref[rows] = hidden
        d_hidden = mm(cot, down[...])
        d_gate = d_hidden * up * sigmoid * (1.0 + gate * (1.0 - sigmoid))
        d_ffn = jnp.concatenate([d_gate, d_hidden * act], axis=1).astype(BF16)
        d_ffn_ref[rows] = d_ffn
        d_second = mm_t(d_ffn, gate_up[...])
        d_mine[group][...] = d_second[:count]
        d_send[group] = d_second[count:].astype(BF16)
        out = mm_t(hidden, down[...])
        block_ref[order[2 * group]] = out[:count].astype(BF16)
        block_ref[order[2 * group + 1]] = out[count:].astype(BF16)


def ffn_weights(*refs):
    order, seconds, cots, hidden_ref, d_ffn_ref, out_ref, x_ref = refs[0], refs[1:9], *refs[9:]
    count = seconds[0].shape[0]
    for lhs, other_ref, columns in ((0, d_ffn_ref, 0), (1, hidden_ref, d_ffn_ref.shape[1])):
        for i in range(8):
            x_ref[i * count : (i + 1) * count] = cots[order[i]] if lhs else seconds[i][...]
        width = other_ref.shape[1]
        for pair in range(4):
            both = outer_sum(x_ref[:, 2 * pair * count : 2 * (pair + 1) * count], other_ref[...]).astype(BF16)
            out_ref[2 * pair, :, columns : columns + width] = both[:count]
            out_ref[2 * pair + 1, :, columns : columns + width] = both[count:]
    used = d_ffn_ref.shape[1] + hidden_ref.shape[1]
    out_ref[:, :, used:] = jnp.zeros((8, count, out_ref.shape[2] - used), BF16)


def sum_ffn(parts, gate_up_ref, down_ref):
    width = gate_up_ref.shape[1]
    total = sum(parts[i].astype(F32) for i in range(8)).astype(BF16)
    gate_up_ref[...] = total[:, :width]
    down_ref[...] = total[:, width : width + down_ref.shape[1]]


def sum_attn(parts, first_ref, out_ref):
    count = out_ref.shape[0]
    width = first_ref.shape[1] - 128
    total = sum(parts[i].astype(F32) for i in range(8))
    first_ref[:, :width] = total[:, :width].astype(BF16)
    pack_gains(first_ref, width, total[:24, width : width + 128] + total[24:48, width : width + 128])
    out_ref[...] = total[:, width + 128 :].astype(BF16)


def pack_gains(ref, width, gains):
    high = gains.astype(BF16)
    low = (gains - high.astype(F32)).astype(BF16)
    rest = jnp.zeros((ref.shape[0] - 48, 128), BF16)
    ref[:, width : width + 128] = jnp.concatenate([high, low, rest], axis=0)


def join_ffn(own, other, down, down_other, out_ref):
    width = own.shape[1]
    out_ref[:, :width] = (own[...].astype(F32) + other[...].astype(F32)).astype(BF16)
    out_ref[:, width:] = (down[...].astype(F32) + down_other[...].astype(F32)).astype(BF16)


def join_attn(own, other, out, out_other, out_ref):
    width = own.shape[1] - 128
    total = own[...].astype(F32) + other[...].astype(F32)
    out_ref[:, :width] = total[:, :width].astype(BF16)
    pack_gains(out_ref, width, total[:24, width:] + total[24:48, width:])
    out_ref[:, width + 128 :] = (out[...].astype(F32) + out_other[...].astype(F32)).astype(BF16)


def assemble_ffn(*refs):
    order, pieces, (gate_ref, up_ref, down_ref, held) = refs[0], refs[1:9], refs[9:]
    width = down_ref.shape[0]
    count = pieces[0].shape[0]
    for i in range(8):
        held[order[i]] = pieces[i][...]
    for owner in range(8):
        columns = slice(owner * width, (owner + 1) * width)
        gate_ref[:, columns] = held[owner, :, :width].astype(F32)
        up_ref[:, columns] = held[owner, :, width : 2 * width].astype(F32)
        down = held[owner, :, 2 * width :].astype(F32)
        down_ref[:, owner * count : (owner + 1) * count] = jnp.transpose(down)


def assemble_attn(*refs):
    order, pieces, (query_ref, key_ref, value_ref, out_ref, gains_ref, held) = refs[0], refs[1:9], refs[9:]
    count = pieces[0].shape[0]
    half = count // 2
    for i in range(8):
        held[order[i]] = pieces[i][...]
    gains = jnp.zeros(gains_ref.shape, F32)
    for owner in range(8):
        columns = slice(owner * count, (owner + 1) * count)
        narrow = slice(owner * half, (owner + 1) * half)
        part = held[owner].astype(F32)
        query_ref[:, columns] = part[:, :count]
        key_ref[:, narrow] = part[:, count : count + half]
        value_ref[:, narrow] = part[:, count + half : 2 * count]
        out_ref[:, columns] = jnp.transpose(part[:, 3 * count :])
        gains += part[:24, 2 * count : 3 * count] + part[24:48, 2 * count : 3 * count]
    gains_ref[...] = gains


def body(
    hidden_in,
    positions,
    cotangent,
    attn_gain,
    w_query,
    w_key,
    w_value,
    query_gain,
    key_gain,
    w_out,
    ffn_gain,
    w_gate,
    w_up,
    w_down,
):
    ctx = lax.axis_index("ctx")
    tokens = hidden_in[0].astype(F32)
    count, width = tokens.shape
    head_size = query_gain.shape[0]
    q_width = w_query.shape[1] // 8
    k_width = w_key.shape[1] // 8
    ff_width = w_gate.shape[1] // 8

    z_index, core = ctx // 2, ctx % 2
    owners = jnp.stack(
        [((z_index + step) % 4) * 2 + (core ^ flip) for step in STEPS for flip in (0, 1)]
    )
    places = positions[0].reshape(8, count)[owners].reshape(8 * count)
    length = 8 * count
    cosine_table, sine_table = rope_tables(places, head_size)
    column = jnp.broadcast_to(places[:, None], (length, 2 * count))
    row = places[None]
    gains = (query_gain[:, None], key_gain[:, None])
    tables = (cosine_table, sine_table, column, row)
    block = shape((count, q_width), BF16)
    low_rows, rows = shape((count, width), BF16), shape((count, width), F32)
    qkv_width = q_width + 2 * k_width

    first_scale = rms_scale(tokens)
    first_hat = tokens * first_scale
    first_normed = (first_hat * attn_gain).astype(BF16)
    gate_up = lax.all_gather(
        jnp.concatenate([own_columns(w_gate, ff_width, ctx), own_columns(w_up, ff_width, ctx)], axis=1),
        "fsdp",
        axis=0,
        tiled=True,
    )
    first_pieces = gather_ctx(first_normed)
    qkv_block = jnp.concatenate(
        [own_columns(w_query, q_width, ctx), own_columns(w_key, k_width, ctx), own_columns(w_value, k_width, ctx)],
        axis=1,
    )
    w_qkv = join_y(spread_y(pair_x(qkv_block)))
    out_pair = pair_x(w_out)
    cot = cotangent[0]
    first_pieces, w_qkv, tables, out_pair, cot, w_down = stage(first_pieces, w_qkv, tables, out_pair, cot, w_down)

    cots = all_to_all(jnp.broadcast_to(cot[None], (8, count, width)), "ctx")
    out_pairs = spread_y(out_pair)
    down_chunk = transpose_mesh(jnp.transpose(own_columns(w_down, width // 8, ctx)))
    qkv, lse, *mixed_blocks = call(
        attend_forward,
        [shape((qkv_width, length), F32), shape((8, length), F32)] + [block] * 8,
        (*first_pieces, w_qkv, *tables, *gains),
        4 * 10**9,
    )
    mixed_blocks, out_pairs, down_chunk = stage(mixed_blocks, out_pairs, down_chunk)

    own_blocks = exchange_ctx(mixed_blocks)
    own_blocks, down_chunk = stage(own_blocks, down_chunk)
    residual, second_normed = call(
        out_project,
        [rows, low_rows],
        (owners, *own_blocks, join_y(out_pairs), hidden_in[0], ffn_gain[None]),
        3 * 10**8,
        [pltpu.VMEM((count, width), BF16)],
        1,
    )

    second_pieces = gather_ctx(second_normed)
    down_t = join_y(spread_y(pair_x(down_chunk)))
    hidden, d_ffn, block_parts, d_send, *d_mine = call(
        ffn,
        [
            shape((length, ff_width), BF16),
            shape((length, 2 * ff_width), BF16),
            shape((8, count, width), BF16),
            shape((4, count, width), BF16),
        ]
        + [rows] * 4,
        (owners, *second_pieces, cots, gate_up, down_t),
        8 * 10**9,
        (),
        1,
    )

    d_moves = start_scatter_ctx(d_mine, swap_core(d_send))
    padded = -(-3 * ff_width // 128) * 128
    (ffn_partial,) = call(
        ffn_weights,
        [shape((8, count, padded), BF16)],
        (owners, *second_pieces, cots, hidden, d_ffn),
        4 * 10**9,
        [pltpu.VMEM((length, width), BF16)],
        1,
    )
    d_moves, ffn_partial = stage(d_moves, ffn_partial)
    ffn_sums = all_to_all(ffn_partial, "fsdp")
    block_sum = lax.psum_scatter(block_parts, "ctx", scatter_dimension=0, tiled=False)
    block_out = (residual + block_sum.astype(F32)).astype(BF16)
    d_resid, d_attn, ffn_gain_part, *d_blocks = call(
        resid_backward,
        [rows, low_rows, shape((1, width), F32)] + [block] * 8,
        (owners, *d_moves, residual, cot, ffn_gain[None], join_y(out_pairs)),
        3 * 10**8,
        [pltpu.VMEM((count, width), BF16)],
        1,
    )

    d_blocks = exchange_ctx(d_blocks)
    d_blocks, d_attn = stage(d_blocks, d_attn)

    d_pieces = gather_ctx(d_attn)
    q_gain_part, k_gain_part, d_qkv, d_first_parts = call(
        attend_backward,
        [
            shape((head_size, 1), F32),
            shape((head_size, 1), F32),
            shape((length, qkv_width), BF16),
            shape((8, count, width), BF16),
        ],
        (owners, *d_blocks, w_qkv, *tables, *gains, qkv, lse),
        8 * 10**9,
        [pltpu.VMEM((qkv_width, length), F32)],
        1,
    )
    d_first = lax.psum_scatter(d_first_parts, "ctx", scatter_dimension=0, tiled=False).astype(F32)
    (attn_partial,) = call(
        attend_weights,
        [shape((8, count, qkv_width + 128 + q_width), BF16)],
        (*first_pieces, *d_pieces, *mixed_blocks, d_qkv, w_qkv, attn_gain[None], ffn_gain_part, q_gain_part, k_gain_part),
        10**9,
        [pltpu.VMEM((length, width), BF16), pltpu.VMEM((length, q_width), BF16)],
    )

    attn_sums = all_to_all(attn_partial, "fsdp")
    own, down = call(
        sum_ffn, [shape((count, 2 * ff_width), BF16), shape((count, ff_width), BF16)], (ffn_sums,), 10**6
    )
    (joined,) = call(
        join_ffn,
        [shape((count, 3 * ff_width), BF16)],
        (own, swap_dp(own), transpose_mesh(down), transpose_mesh(down, 1)),
        10**6,
    )
    ffn_parts = gather_ctx(joined)
    own, out = call(
        sum_attn, [shape((count, qkv_width + 128), BF16), shape((count, q_width), BF16)], (attn_sums,), 10**6
    )
    (joined,) = call(
        join_attn,
        [shape((count, qkv_width + 128 + q_width), BF16)],
        (own, swap_dp(own), transpose_mesh(out), transpose_mesh(out, 1)),
        10**6,
    )
    attn_parts = gather_ctx(joined)
    d_from_first, _ = norm_back(d_first, first_hat, first_scale, attn_gain)
    grad_in = (d_resid + d_from_first).astype(BF16)
    grad_gate, grad_up, grad_down = call(
        assemble_ffn,
        [shape((count, 8 * ff_width), F32)] * 2 + [shape((ff_width, width), F32)],
        (owners, *ffn_parts),
        10**6,
        [pltpu.VMEM((8, count, 3 * ff_width), BF16)],
        1,
    )
    grad_query, grad_key, grad_value, grad_out, totals = call(
        assemble_attn,
        [shape((count, width), F32)] + [shape((count, 8 * k_width), F32)] * 2 + [shape((q_width, width), F32), shape((24, 128), F32)],
        (owners, *attn_parts),
        10**6,
        [pltpu.VMEM((8, count, qkv_width + 128 + q_width), BF16)],
        1,
    )
    totals = totals.reshape(-1)
    grad_attn_gain = totals[:width]
    grad_ffn_gain = totals[width : 2 * width]
    grad_query_gain = totals[2 * width : 2 * width + head_size]
    grad_key_gain = totals[2 * width + head_size : 2 * width + 2 * head_size]
    return (
        block_out[None],
        grad_in[None],
        grad_attn_gain,
        grad_query,
        grad_key,
        grad_value,
        grad_query_gain,
        grad_key_gain,
        grad_out,
        grad_ffn_gain,
        grad_gate,
        grad_up,
        grad_down,
    )


def solution(mesh):
    in_specs = (
        P(("dp", "fsdp"), "ctx", None),
        P(("dp", "fsdp"), None),
        P(("dp", "fsdp"), "ctx", None),
        P(),
        P("fsdp", None),
        P("fsdp", None),
        P("fsdp", None),
        P(),
        P(),
        P("fsdp", None),
        P(),
        P("fsdp", None),
        P("fsdp", None),
        P("fsdp", None),
    )
    out_specs = (
        P(("dp", "fsdp"), "ctx", None),
        P(("dp", "fsdp"), "ctx", None),
        P(),
        P("fsdp", None),
        P("fsdp", None),
        P("fsdp", None),
        P(),
        P(),
        P("fsdp", None),
        P(),
        P("fsdp", None),
        P("fsdp", None),
        P("fsdp", None),
    )
    return jax.shard_map(body, mesh=mesh, in_specs=in_specs, out_specs=out_specs, check_vma=False)
```

```python
import math

import jax
import jax.numpy as jnp
from jax import lax
from jax.experimental import pallas as pl
from jax.experimental.pallas import tpu as pltpu
from jax.sharding import PartitionSpec as P

NORM_EPSILON = 1e-05
ROPE_BASE = 1000000.0
MASKED_SCORE = -1e30
BF16 = jnp.bfloat16
F32 = jnp.float32
STEPS = (0, -1, 1, 2)


def rms_scale(values):
    return lax.rsqrt(jnp.mean(values * values, axis=-1, keepdims=True) + NORM_EPSILON)


def rope_tables(places, head_size):
    half_width = head_size // 2
    pair_index = jnp.arange(half_width, dtype=F32)
    frequency = ROPE_BASE ** (-2.0 * pair_index / head_size)
    angles = frequency[:, None] * places.astype(F32)[None, :]
    return jnp.cos(angles), jnp.sin(angles)


def call(kernel, out_shapes, scalars, fetched, args, flops, scratch=(), copies=0):
    vmem = pl.BlockSpec(memory_space=pltpu.VMEM)
    operands = (*scalars, *fetched, *args)
    out_bytes = sum(math.prod(o.shape) * o.dtype.itemsize for o in out_shapes)
    in_bytes = sum(math.prod(a.shape) * a.dtype.itemsize for a in operands)
    return pl.pallas_call(
        kernel,
        out_shape=out_shapes,
        in_specs=[pl.BlockSpec(memory_space=pltpu.SMEM)] * len(scalars)
        + [pl.BlockSpec(memory_space=pl.ANY)] * len(fetched)
        + [vmem] * len(args),
        out_specs=[vmem] * len(out_shapes),
        scratch_shapes=list(scratch) + ([pltpu.SemaphoreType.DMA((copies,))] if copies else []),
        compiler_params=pltpu.CompilerParams(vmem_limit_bytes=40 * 2**20),
        cost_estimate=pl.CostEstimate(flops=flops, bytes_accessed=in_bytes + out_bytes, transcendentals=0),
    )(*operands)


def shape(dims, kind):
    return jax.ShapeDtypeStruct(dims, kind)


def head_forward(values, gain, cosine, sine):
    scale = lax.rsqrt(jnp.mean(values * values, axis=0, keepdims=True) + NORM_EPSILON)
    hat = values * scale
    normed = hat * gain
    half = values.shape[0] // 2
    front, back = normed[:half], normed[half:]
    rotated = jnp.concatenate([front * cosine - back * sine, back * cosine + front * sine], axis=0)
    return scale, hat, rotated


def head_backward(grads, hat, scale, gain, cosine, sine):
    half = grads.shape[0] // 2
    front, back = grads[:half], grads[half:]
    d_normed = jnp.concatenate([front * cosine + back * sine, back * cosine - front * sine], axis=0)
    scaled = d_normed * gain
    inner = jnp.mean(hat * scaled, axis=0, keepdims=True)
    return scale * (scaled - hat * inner), jnp.sum(d_normed * hat, axis=1, keepdims=True)


def norm_back(d_normed, normed_hat, scale_values, gain_vector):
    scaled = d_normed * gain_vector
    inner = jnp.mean(normed_hat * scaled, axis=-1, keepdims=True)
    return (scale_values * (scaled - normed_hat * inner), d_normed * normed_hat)


def mm(left, right):
    return jnp.dot(left, right, preferred_element_type=F32)


def mm_t(left, right):
    return lax.dot_general(left, right, (((1,), (1,)), ((), ())), preferred_element_type=F32)


def outer_sum(left, right):
    return lax.dot_general(left, right, (((0,), (0,)), ((), ())), preferred_element_type=F32)


def swap_core(value):
    return lax.ppermute(value, "ctx", [(i, i ^ 1) for i in range(8)])


def move_z(value, step):
    return lax.ppermute(value, "ctx", [(i, (i + 2 * step) % 8) for i in range(8)])


def gather_ctx(block):
    pieces = []
    for step in STEPS:
        mine = block if step == 0 else move_z(block, -step)
        pieces += [mine, swap_core(mine)]
    return pieces


def start_scatter_ctx(mine, received):
    sums = [own + other.astype(F32) for own, other in zip(mine, received)]
    return [sums[0]] + [move_z(sums[slot].astype(BF16), STEPS[slot]) for slot in (3, 1, 2)]


def exchange_ctx(own, other):
    other = swap_core(other)
    out = [None] * 4
    for i, step in enumerate(STEPS):
        both = jnp.stack([own[i], other[i]])
        out[(0, 2, 1, 3)[i]] = move_z(both, step) if step else both
    return out


def stage(*values):
    return lax.optimization_barrier(values)


def transpose_mesh(value, flip=0):
    pairs = [
        ((d * 8 + c) * 8 + f, ((d ^ flip) * 8 + f) * 8 + c) for d in range(2) for c in range(8) for f in range(8)
    ]
    return lax.ppermute(value, ("dp", "ctx", "fsdp"), pairs)


def swap_dp(value):
    return lax.ppermute(value, "dp", [(0, 1), (1, 0)])


def move_y(value, step, flip=0):
    pairs = [(y * 2 + x, (y + step) % 4 * 2 + (x ^ flip)) for y in range(4) for x in range(2)]
    return lax.ppermute(value, "fsdp", pairs)


def pair_x(block):
    other = move_y(block, 0, 1)
    first = lax.axis_index("fsdp") % 2 == 0
    return jnp.concatenate([jnp.where(first, block, other), jnp.where(first, other, block)], axis=0)


def spread_y(pair):
    return [pair] + [move_y(pair, step) for step in (1, 3, 2)]


def fetch(pairs, sems, first=0):
    copies = [pltpu.make_async_copy(src, dst, sems.at[first + i]) for i, (src, dst) in enumerate(pairs)]
    for copy in copies:
        copy.start()
    return copies


def rows_of(pieces, ref):
    count = pieces[0].shape[0]
    return [(piece, ref.at[pl.ds(i * count, count)]) for i, piece in enumerate(pieces)]


def joined_y(place, pairs, ref):
    rows = pairs[0].shape[0]
    owners = [(place[0] + 4 - step) % 4 for step in (0, 1, 3, 2)]
    return [(pair, ref.at[pl.ds(pl.multiple_of(y * rows, rows), rows)]) for y, pair in zip(owners, pairs)]


def wait(copies):
    for copy in copies:
        copy.wait()


def all_to_all(blocks, axis):
    return lax.all_to_all(blocks, axis, split_axis=0, concat_axis=0, tiled=True)


def own_columns(weight, width, index):
    return lax.dynamic_slice_in_dim(weight, index * width, width, 1)


def attend_forward(*refs):
    place, pieces, w_pairs, refs = refs[0], refs[1:9], refs[9:13], refs[13:]
    cos_ref, sin_ref, column_ref, row_ref, q_gain, k_gain = refs[:6]
    qkv_ref, lse_ref, own_ref, other_ref, x_ref, w_qkv, sems = refs[6:]
    w_copies = fetch(joined_y(place, w_pairs, w_qkv), sems, 8)
    x_copies = fetch(rows_of(pieces, x_ref), sems)
    wait(w_copies)
    length = qkv_ref.shape[1]
    count = length // 8
    head = q_gain.shape[0]
    for pair in range(4):
        wait(x_copies[2 * pair : 2 * pair + 2])
        lanes = slice(pair * 2 * count, (pair + 1) * 2 * count)
        qkv_ref[:, lanes] = jnp.transpose(mm(x_ref[lanes], w_qkv[...]))
    cosine, sine = cos_ref[...], sin_ref[...]
    queries = [
        head_forward(qkv_ref[h * head : (h + 1) * head], q_gain[...], cosine, sine)[2].astype(BF16) * BF16(head**-0.5)
        for h in range(2)
    ]
    key = jnp.transpose(head_forward(qkv_ref[2 * head : 3 * head], k_gain[...], cosine, sine)[2]).astype(BF16)
    value = qkv_ref[3 * head :].astype(BF16)
    width = column_ref.shape[1]
    for tile in range(length // width):
        lanes = slice(tile * width, (tile + 1) * width)
        allowed = column_ref[...] <= row_ref[:, lanes]
        outs = []
        for h in range(2):
            scores = jnp.where(allowed, mm(key, queries[h][:, lanes]), MASKED_SCORE)
            top = jnp.max(scores, axis=0, keepdims=True)
            weights = jnp.exp(scores - top)
            total = jnp.sum(weights, axis=0, keepdims=True)
            lse_ref[h : h + 1, lanes] = top + jnp.log(total)
            outs.append(mm(value, (weights * (1.0 / total)).astype(BF16)))
        mixed = jnp.transpose(jnp.concatenate(outs, axis=0)).astype(BF16)
        own_ref[tile] = mixed[:count]
        other_ref[tile] = mixed[count:]


def out_project(place, order, *refs):
    out_pairs, blocks, (tokens, gain, resid_ref, normed_ref, w_out, mixed_ref, sems) = refs[:4], refs[4:8], refs[8:]
    copies = fetch(joined_y(place, out_pairs, w_out), sems)
    count = blocks[0].shape[2]
    for i in range(8):
        lanes = pl.ds(pl.multiple_of(order[i] * count, count), count)
        mixed_ref[:, lanes] = blocks[i // 2][i % 2]
    wait(copies)
    resid = tokens[...].astype(F32) + mm(mixed_ref[...], w_out[...])
    resid_ref[...] = resid
    normed_ref[...] = (resid * rms_scale(resid) * gain[...]).astype(BF16)


def resid_backward(place, order, *refs):
    out_pairs, refs = refs[:4], refs[4:]
    total, move_a, move_b, move_c, resid_ref, cot_ref, gain_ref = refs[:7]
    d_resid_ref, d_attn_ref, gain_part_ref, own_ref, other_ref, w_out, d_mixed_ref, sems = refs[7:]
    copies = fetch(joined_y(place, out_pairs, w_out), sems)
    d_second = total[...] + move_a[...].astype(F32) + move_b[...].astype(F32) + move_c[...].astype(F32)
    resid = resid_ref[...]
    scale = rms_scale(resid)
    d_from, gain_part = norm_back(d_second, resid * scale, scale, gain_ref[...])
    gain_part_ref[...] = jnp.sum(gain_part, axis=0, keepdims=True)
    d_resid = cot_ref[...].astype(F32) + d_from
    d_resid_ref[...] = d_resid
    d_attn = d_resid.astype(BF16)
    d_attn_ref[...] = d_attn
    wait(copies)
    d_mixed_ref[...] = mm_t(d_attn, w_out[...]).astype(BF16)
    count = own_ref.shape[2]
    for i in range(8):
        lanes = pl.ds(pl.multiple_of(order[i] * count, count), count)
        (own_ref, other_ref)[i % 2][i // 2] = d_mixed_ref[:, lanes]


def attend_backward(*refs):
    place, order, w_pairs, d_blocks, refs = refs[0], refs[1], refs[2:6], refs[6:10], refs[10:]
    cos_ref, sin_ref, column_ref, row_ref, q_gain, k_gain, qkv_ref, lse_ref = refs[:8]
    q_gain_ref, k_gain_ref, d_low_ref, d_first_ref, d_qkv_ref, w_qkv, sems = refs[8:]
    copies = fetch(joined_y(place, w_pairs, w_qkv), sems)
    length = qkv_ref.shape[1]
    head = q_gain.shape[0]
    count = length // 8
    cosine, sine = cos_ref[...], sin_ref[...]
    scales, hats, queries = [], [], []
    for h in range(2):
        scale, hat, rotated = head_forward(qkv_ref[h * head : (h + 1) * head], q_gain[...], cosine, sine)
        scales.append(scale)
        hats.append(hat)
        queries.append(rotated.astype(BF16) * BF16(head**-0.5))
    k_scale, k_hat, rotated = head_forward(qkv_ref[2 * head : 3 * head], k_gain[...], cosine, sine)
    key_rows = rotated.astype(BF16)
    key = jnp.transpose(rotated).astype(BF16)
    value = jnp.transpose(qkv_ref[3 * head :]).astype(BF16)
    width = column_ref.shape[1]
    d_key = jnp.zeros((length, head), F32)
    d_value = jnp.zeros((length, head), F32)
    for tile in range(length // width):
        lanes = slice(tile * width, (tile + 1) * width)
        allowed = column_ref[...] <= row_ref[:, lanes]
        d_mixed = jnp.concatenate([d_blocks[tile][0], d_blocks[tile][1]], axis=0)
        d_mixed = jnp.transpose(d_mixed.astype(F32)).astype(BF16)
        for h in range(2):
            rows = slice(h * head, (h + 1) * head)
            query = queries[h][:, lanes]
            probs = jnp.where(allowed, jnp.exp(mm(key, query) - lse_ref[h : h + 1, lanes]), 0.0)
            d_probs = mm(value, d_mixed[rows])
            inner = jnp.sum(probs * d_probs, axis=0, keepdims=True)
            d_scores = (probs * (d_probs - inner)).astype(BF16)
            d_value += mm_t(probs.astype(BF16), d_mixed[rows])
            d_key += mm_t(d_scores, query)
            d_qkv_ref[rows, lanes] = mm(key_rows, d_scores) * head**-0.5
    for h in range(2):
        rows = slice(h * head, (h + 1) * head)
        d_query, gain_part = head_backward(d_qkv_ref[rows], hats[h], scales[h], q_gain[...], cosine, sine)
        d_qkv_ref[rows] = d_query
        if h == 0:
            q_gain_ref[...] = gain_part
        else:
            q_gain_ref[...] += gain_part
    d_keys, gain_part = head_backward(jnp.transpose(d_key), k_hat, k_scale, k_gain[...], cosine, sine)
    k_gain_ref[...] = gain_part
    d_qkv_ref[2 * head : 3 * head] = d_keys
    d_qkv_ref[3 * head :] = jnp.transpose(d_value)
    wait(copies)
    for tile in range(4):
        lanes = slice(tile * 2 * count, (tile + 1) * 2 * count)
        d_qkv = jnp.transpose(d_qkv_ref[:, lanes]).astype(BF16)
        d_low_ref[lanes] = d_qkv
        d_first = mm_t(d_qkv, w_qkv[...])
        d_first_ref[order[2 * tile]] = d_first[:count].astype(BF16)
        d_first_ref[order[2 * tile + 1]] = d_first[count:].astype(BF16)


def attend_weights(*refs):
    place, pieces, d_pieces, own, other, w_pairs = refs[0], refs[1:9], refs[9:17], refs[17], refs[18], refs[19:23]
    d_low, attn_gain, ffn_part, q_part, k_part = refs[23:28]
    out_ref, x_ref, d_ref, mixed_ref, d_low_ref, w_qkv, sems = refs[28:]
    count = pieces[0].shape[0]
    width = d_low_ref.shape[1]
    mixed = []
    for i in range(4):
        mixed += [(own.at[i], mixed_ref.at[pl.ds(2 * i * count, count)])]
        mixed += [(other.at[i], mixed_ref.at[pl.ds((2 * i + 1) * count, count)])]
    copies = fetch([(d_low, d_low_ref), *rows_of(pieces, x_ref), *joined_y(place, w_pairs, w_qkv)], sems)
    more = fetch([*mixed, *rows_of(d_pieces, d_ref)], sems, len(copies))
    wait(copies)
    grad_qkv = outer_sum(d_low_ref[...], x_ref[...])
    attn_part = jnp.sum(grad_qkv * jnp.transpose(w_qkv[...].astype(F32)), axis=0, keepdims=True) / attn_gain[...]
    grad_qkv = jnp.transpose(grad_qkv).astype(BF16)
    wait(more)
    grad_out = jnp.transpose(outer_sum(mixed_ref[...], d_ref[...])).astype(BF16)
    lines = [part[:, i * 128 : (i + 1) * 128] for part in (attn_part, ffn_part[...]) for i in range(8)]
    lines.append(jnp.concatenate([jnp.transpose(q_part[...]), jnp.transpose(k_part[...])], axis=1))
    gains = jnp.concatenate(lines + [jnp.zeros((7, 128), F32)], axis=0)
    high = gains.astype(BF16)
    low = (gains - high.astype(F32)).astype(BF16)
    gains = jnp.concatenate([high, low, jnp.zeros((count - 48, 128), BF16)], axis=0)
    for i in range(8):
        rows = slice(i * count, (i + 1) * count)
        out_ref[i, :, :width] = grad_qkv[rows]
        out_ref[i, :, width : width + 128] = gains
        out_ref[i, :, width + 128 :] = grad_out[rows]


def ffn(*refs):
    place, order, seconds, cots, weights, down_pairs = refs[0], refs[1], refs[2:10], refs[10], refs[11], refs[12:16]
    hidden_ref, d_ffn_ref, block_ref, d_send = refs[16:20]
    d_mine, (x_ref, cot_ref, gate_up, down, sems) = refs[20:24], refs[24:]
    copies = fetch([(weights, gate_up), *joined_y(place, down_pairs, down)], sems)
    loads = rows_of(seconds, x_ref) + rows_of([cots.at[order[i]] for i in range(8)], cot_ref)
    loads = fetch([loads[8 * j + 2 * g + i] for g in (3, 1, 2, 0) for j in (0, 1) for i in (0, 1)], sems, 5)
    wait(copies)
    width = hidden_ref.shape[1]
    count = seconds[0].shape[0]
    for group in (3, 1, 2, 0):
        rows = slice(2 * group * count, 2 * (group + 1) * count)
        wait(loads[:4])
        loads = loads[4:]
        x, cot = x_ref[rows], cot_ref[rows]
        both = mm(x, gate_up[...])
        gate, up = both[:, :width], both[:, width:]
        sigmoid = 1.0 / (1.0 + jnp.exp(-gate))
        act = gate * sigmoid
        hidden = (act * up).astype(BF16)
        hidden_ref[rows] = hidden
        d_hidden = mm(cot, down[...])
        d_gate = d_hidden * up * sigmoid * (1.0 + gate * (1.0 - sigmoid))
        d_ffn = jnp.concatenate([d_gate, d_hidden * act], axis=1).astype(BF16)
        d_ffn_ref[rows] = d_ffn
        d_second = mm_t(d_ffn, gate_up[...])
        d_mine[group][...] = d_second[:count]
        d_send[group] = d_second[count:].astype(BF16)
        out = mm_t(hidden, down[...])
        block_ref[order[2 * group]] = out[:count].astype(BF16)
        block_ref[order[2 * group + 1]] = out[count:].astype(BF16)


def ffn_weights(*refs):
    order, seconds, cots, hidden, d_ffn = refs[0], refs[1:9], *refs[9:12]
    out_ref, x_ref, cot_ref, hidden_ref, d_ffn_ref, sems = refs[12:]
    count = seconds[0].shape[0]
    copies = fetch([(d_ffn, d_ffn_ref), *rows_of(seconds, x_ref)], sems)
    more = fetch([(hidden, hidden_ref), *rows_of([cots.at[order[i]] for i in range(8)], cot_ref)], sems, 9)
    for left_ref, right_ref, columns in ((x_ref, d_ffn_ref, 0), (cot_ref, hidden_ref, d_ffn_ref.shape[1])):
        wait(more if columns else copies)
        width = right_ref.shape[1]
        for pair in range(4):
            both = outer_sum(left_ref[:, 2 * pair * count : 2 * (pair + 1) * count], right_ref[...]).astype(BF16)
            out_ref[2 * pair, :, columns : columns + width] = both[:count]
            out_ref[2 * pair + 1, :, columns : columns + width] = both[count:]
    used = d_ffn_ref.shape[1] + hidden_ref.shape[1]
    out_ref[:, :, used:] = jnp.zeros((8, count, out_ref.shape[2] - used), BF16)


def sum_ffn(parts, gate_up_ref, down_ref):
    width = gate_up_ref.shape[1]
    total = sum(parts[i].astype(F32) for i in range(8)).astype(BF16)
    gate_up_ref[...] = total[:, :width]
    down_ref[...] = total[:, width : width + down_ref.shape[1]]


def sum_attn(parts, first_ref, out_ref):
    count = out_ref.shape[0]
    width = first_ref.shape[1] - 128
    total = sum(parts[i].astype(F32) for i in range(8))
    first_ref[:, :width] = total[:, :width].astype(BF16)
    pack_gains(first_ref, width, total[:24, width : width + 128] + total[24:48, width : width + 128])
    out_ref[...] = total[:, width + 128 :].astype(BF16)


def pack_gains(ref, width, gains):
    high = gains.astype(BF16)
    low = (gains - high.astype(F32)).astype(BF16)
    rest = jnp.zeros((ref.shape[0] - 48, 128), BF16)
    ref[:, width : width + 128] = jnp.concatenate([high, low, rest], axis=0)


def join_ffn(own, other, down, down_other, out_ref):
    width = own.shape[1]
    out_ref[:, :width] = (own[...].astype(F32) + other[...].astype(F32)).astype(BF16)
    out_ref[:, width:] = (down[...].astype(F32) + down_other[...].astype(F32)).astype(BF16)


def join_attn(own, other, out, out_other, out_ref):
    width = own.shape[1] - 128
    total = own[...].astype(F32) + other[...].astype(F32)
    out_ref[:, :width] = total[:, :width].astype(BF16)
    pack_gains(out_ref, width, total[:24, width:] + total[24:48, width:])
    out_ref[:, width + 128 :] = (out[...].astype(F32) + out_other[...].astype(F32)).astype(BF16)


def assemble_ffn(*refs):
    order, pieces, (gate_ref, up_ref, down_ref, held, sems) = refs[0], refs[1:9], refs[9:]
    width = down_ref.shape[0]
    count = pieces[0].shape[0]
    wait(fetch([(pieces[i], held.at[order[i]]) for i in range(8)], sems))
    for owner in range(8):
        columns = slice(owner * width, (owner + 1) * width)
        gate_ref[:, columns] = held[owner, :, :width].astype(F32)
        up_ref[:, columns] = held[owner, :, width : 2 * width].astype(F32)
        down = held[owner, :, 2 * width :].astype(F32)
        down_ref[:, owner * count : (owner + 1) * count] = jnp.transpose(down)


def assemble_attn(*refs):
    order, pieces, (query_ref, key_ref, value_ref, out_ref, gains_ref, held, sems) = refs[0], refs[1:9], refs[9:]
    count = pieces[0].shape[0]
    half = count // 2
    wait(fetch([(pieces[i], held.at[order[i]]) for i in range(8)], sems))
    gains = jnp.zeros(gains_ref.shape, F32)
    for owner in range(8):
        columns = slice(owner * count, (owner + 1) * count)
        narrow = slice(owner * half, (owner + 1) * half)
        part = held[owner].astype(F32)
        query_ref[:, columns] = part[:, :count]
        key_ref[:, narrow] = part[:, count : count + half]
        value_ref[:, narrow] = part[:, count + half : 2 * count]
        out_ref[:, columns] = jnp.transpose(part[:, 3 * count :])
        gains += part[:24, 2 * count : 3 * count] + part[24:48, 2 * count : 3 * count]
    gains_ref[...] = gains


def body(
    hidden_in,
    positions,
    cotangent,
    attn_gain,
    w_query,
    w_key,
    w_value,
    query_gain,
    key_gain,
    w_out,
    ffn_gain,
    w_gate,
    w_up,
    w_down,
):
    ctx = lax.axis_index("ctx")
    tokens = hidden_in[0].astype(F32)
    count, width = tokens.shape
    head_size = query_gain.shape[0]
    q_width = w_query.shape[1] // 8
    k_width = w_key.shape[1] // 8
    ff_width = w_gate.shape[1] // 8

    z_index, core = ctx // 2, ctx % 2
    owners = jnp.stack(
        [((z_index + step) % 4) * 2 + (core ^ flip) for step in STEPS for flip in (0, 1)]
    )
    places = positions[0].reshape(8, count)[owners].reshape(8 * count)
    length = 8 * count
    cosine_table, sine_table = rope_tables(places, head_size)
    column = jnp.broadcast_to(places[:, None], (length, 2 * count))
    row = places[None]
    gains = (query_gain[:, None], key_gain[:, None])
    tables = (cosine_table, sine_table, column, row)
    block = shape((count, q_width), BF16)
    low_rows, rows = shape((count, width), BF16), shape((count, width), F32)
    qkv_width = q_width + 2 * k_width

    place = jnp.stack([lax.axis_index("fsdp") // 2, lax.axis_index("fsdp") % 2])
    wide, head_rows = pltpu.VMEM((length, width), BF16), pltpu.VMEM((length, qkv_width), BF16)

    first_scale = rms_scale(tokens)
    first_hat = tokens * first_scale
    first_normed = (first_hat * attn_gain).astype(BF16)
    first_pieces = gather_ctx(first_normed)
    qkv_block = jnp.concatenate(
        [own_columns(w_query, q_width, ctx), own_columns(w_key, k_width, ctx), own_columns(w_value, k_width, ctx)],
        axis=1,
    )
    qkv_pairs = spread_y(pair_x(qkv_block))
    out_pair = pair_x(w_out)
    cot = cotangent[0]
    cot_copies = jnp.broadcast_to(cot[None], (8, count, width))
    down_chunk = jnp.transpose(own_columns(w_down, width // 8, ctx))
    gate_up_block = jnp.concatenate([own_columns(w_gate, ff_width, ctx), own_columns(w_up, ff_width, ctx)], axis=1)
    first_pieces, qkv_pairs, tables, out_pair, cot_copies, down_chunk, gate_up_block = stage(
        first_pieces, qkv_pairs, tables, out_pair, cot_copies, down_chunk, gate_up_block
    )

    gate_up = lax.all_gather(gate_up_block, "fsdp", axis=0, tiled=True)
    cots = all_to_all(cot_copies, "ctx")
    out_pairs = spread_y(out_pair)
    down_chunk = transpose_mesh(down_chunk)
    qkv, lse, own, other = call(
        attend_forward,
        [shape((qkv_width, length), F32), shape((8, length), F32)] + [shape((4, count, q_width), BF16)] * 2,
        (place,),
        (*first_pieces, *qkv_pairs),
        (*tables, *gains),
        4 * 10**9,
        [wide, pltpu.VMEM((width, qkv_width), BF16)],
        12,
    )
    own, other, out_pairs, down_chunk = stage(own, other, out_pairs, down_chunk)

    mixed_blocks = exchange_ctx(own, other)
    mixed_blocks, down_chunk = stage(mixed_blocks, down_chunk)
    square = pltpu.VMEM((width, width), BF16)
    residual, second_normed = call(
        out_project,
        [rows, low_rows],
        (place, owners),
        out_pairs,
        (*mixed_blocks, hidden_in[0], ffn_gain[None]),
        3 * 10**8,
        [square, pltpu.VMEM((count, width), BF16)],
        4,
    )

    second_pieces = gather_ctx(second_normed)
    down_pairs = spread_y(pair_x(down_chunk))
    hidden_shape, d_ffn_shape = shape((length, ff_width), BF16), shape((length, 2 * ff_width), BF16)
    hidden, d_ffn, block_parts, d_send, *d_mine = call(
        ffn,
        [hidden_shape, d_ffn_shape, shape((8, count, width), BF16), shape((4, count, width), BF16)] + [rows] * 4,
        (place, owners),
        (*second_pieces, cots, gate_up, *down_pairs),
        (),
        8 * 10**9,
        [wide, wide, pltpu.VMEM((width, 2 * ff_width), BF16), pltpu.VMEM((width, ff_width), BF16)],
        21,
    )

    d_moves = start_scatter_ctx(d_mine, swap_core(d_send))
    padded = -(-3 * ff_width // 128) * 128
    (ffn_partial,) = call(
        ffn_weights,
        [shape((8, count, padded), BF16)],
        (owners,),
        (*second_pieces, cots, hidden, d_ffn),
        (),
        4 * 10**9,
        [wide, wide, pltpu.VMEM((length, ff_width), BF16), pltpu.VMEM((length, 2 * ff_width), BF16)],
        18,
    )
    d_moves, ffn_partial = stage(d_moves, ffn_partial)
    ffn_sums = all_to_all(ffn_partial, "fsdp")
    block_sum = lax.psum_scatter(block_parts, "ctx", scatter_dimension=0, tiled=False)
    block_out = (residual + block_sum.astype(F32)).astype(BF16)
    d_resid, d_attn, ffn_gain_part, *d_blocks = call(
        resid_backward,
        [rows, low_rows, shape((1, width), F32)] + [shape((4, count, q_width), BF16)] * 2,
        (place, owners),
        out_pairs,
        (*d_moves, residual, cot, ffn_gain[None]),
        3 * 10**8,
        [square, pltpu.VMEM((count, width), BF16)],
        4,
    )

    d_blocks = exchange_ctx(*d_blocks)
    d_blocks, d_attn = stage(d_blocks, d_attn)

    d_pieces = gather_ctx(d_attn)
    q_gain_part, k_gain_part, d_qkv, d_first_parts = call(
        attend_backward,
        [
            shape((head_size, 1), F32),
            shape((head_size, 1), F32),
            shape((length, qkv_width), BF16),
            shape((8, count, width), BF16),
        ],
        (place, owners),
        qkv_pairs,
        (*d_blocks, *tables, *gains, qkv, lse),
        8 * 10**9,
        [pltpu.VMEM((qkv_width, length), F32), pltpu.VMEM((width, qkv_width), BF16)],
        4,
    )
    d_qkv, d_pieces, ffn_sums = stage(d_qkv, d_pieces, ffn_sums)
    d_first = lax.psum_scatter(d_first_parts, "ctx", scatter_dimension=0, tiled=False).astype(F32)
    (attn_partial,) = call(
        attend_weights,
        [shape((8, count, qkv_width + 128 + q_width), BF16)],
        (place,),
        (*first_pieces, *d_pieces, own, other, *qkv_pairs, d_qkv),
        (attn_gain[None], ffn_gain_part, q_gain_part, k_gain_part),
        10**9,
        [wide, wide, pltpu.VMEM((length, q_width), BF16), head_rows, pltpu.VMEM((width, qkv_width), BF16)],
        29,
    )

    attn_sums = all_to_all(attn_partial, "fsdp")
    half, down = call(
        sum_ffn, [shape((count, 2 * ff_width), BF16), shape((count, ff_width), BF16)], (), (), (ffn_sums,), 10**6
    )
    (joined,) = call(
        join_ffn,
        [shape((count, 3 * ff_width), BF16)],
        (),
        (),
        (half, swap_dp(half), transpose_mesh(down), transpose_mesh(down, 1)),
        10**6,
    )
    ffn_parts = gather_ctx(joined)
    half, out = call(
        sum_attn, [shape((count, qkv_width + 128), BF16), shape((count, q_width), BF16)], (), (), (attn_sums,), 10**6
    )
    (joined,) = call(
        join_attn,
        [shape((count, qkv_width + 128 + q_width), BF16)],
        (),
        (),
        (half, swap_dp(half), transpose_mesh(out), transpose_mesh(out, 1)),
        10**6,
    )
    attn_parts = gather_ctx(joined)
    d_from_first, _ = norm_back(d_first, first_hat, first_scale, attn_gain)
    grad_in = (d_resid + d_from_first).astype(BF16)
    grad_gate, grad_up, grad_down = call(
        assemble_ffn,
        [shape((count, 8 * ff_width), F32)] * 2 + [shape((ff_width, width), F32)],
        (owners,),
        ffn_parts,
        (),
        10**6,
        [pltpu.VMEM((8, count, 3 * ff_width), BF16)],
        8,
    )
    grad_query, grad_key, grad_value, grad_out, totals = call(
        assemble_attn,
        [shape((count, width), F32)] + [shape((count, 8 * k_width), F32)] * 2 + [shape((q_width, width), F32), shape((24, 128), F32)],
        (owners,),
        attn_parts,
        (),
        10**6,
        [pltpu.VMEM((8, count, qkv_width + 128 + q_width), BF16)],
        8,
    )
    totals = totals.reshape(-1)
    grad_attn_gain = totals[:width]
    grad_ffn_gain = totals[width : 2 * width]
    grad_query_gain = totals[2 * width : 2 * width + head_size]
    grad_key_gain = totals[2 * width + head_size : 2 * width + 2 * head_size]
    return (
        block_out[None],
        grad_in[None],
        grad_attn_gain,
        grad_query,
        grad_key,
        grad_value,
        grad_query_gain,
        grad_key_gain,
        grad_out,
        grad_ffn_gain,
        grad_gate,
        grad_up,
        grad_down,
    )


def solution(mesh):
    in_specs = (
        P(("dp", "fsdp"), "ctx", None),
        P(("dp", "fsdp"), None),
        P(("dp", "fsdp"), "ctx", None),
        P(),
        P("fsdp", None),
        P("fsdp", None),
        P("fsdp", None),
        P(),
        P(),
        P("fsdp", None),
        P(),
        P("fsdp", None),
        P("fsdp", None),
        P("fsdp", None),
    )
    out_specs = (
        P(("dp", "fsdp"), "ctx", None),
        P(("dp", "fsdp"), "ctx", None),
        P(),
        P("fsdp", None),
        P("fsdp", None),
        P("fsdp", None),
        P(),
        P(),
        P("fsdp", None),
        P(),
        P("fsdp", None),
        P("fsdp", None),
        P("fsdp", None),
    )
    return jax.shard_map(body, mesh=mesh, in_specs=in_specs, out_specs=out_specs, check_vma=False)
```

```python
import math

import jax
import jax.numpy as jnp
from jax import lax
from jax.experimental import pallas as pl
from jax.experimental.pallas import tpu as pltpu
from jax.sharding import PartitionSpec as P

NORM_EPSILON = 1e-05
ROPE_BASE = 1000000.0
MASKED_SCORE = -1e30
BF16 = jnp.bfloat16
F32 = jnp.float32
STEPS = (0, -1, 1, 2)


def rms_scale(values):
    return lax.rsqrt(jnp.mean(values * values, axis=-1, keepdims=True) + NORM_EPSILON)


def rope_tables(places, head_size):
    half_width = head_size // 2
    pair_index = jnp.arange(half_width, dtype=F32)
    frequency = ROPE_BASE ** (-2.0 * pair_index / head_size)
    angles = frequency[:, None] * places.astype(F32)[None, :]
    return jnp.cos(angles), jnp.sin(angles)


def call(kernel, out_shapes, scalars, fetched, args, flops, scratch=(), copies=0):
    vmem = pl.BlockSpec(memory_space=pltpu.VMEM)
    operands = (*scalars, *fetched, *args)
    out_bytes = sum(math.prod(o.shape) * o.dtype.itemsize for o in out_shapes)
    in_bytes = sum(math.prod(a.shape) * a.dtype.itemsize for a in operands)
    return pl.pallas_call(
        kernel,
        out_shape=out_shapes,
        in_specs=[pl.BlockSpec(memory_space=pltpu.SMEM)] * len(scalars)
        + [pl.BlockSpec(memory_space=pl.ANY)] * len(fetched)
        + [vmem] * len(args),
        out_specs=[vmem] * len(out_shapes),
        scratch_shapes=list(scratch) + ([pltpu.SemaphoreType.DMA((copies,))] if copies else []),
        compiler_params=pltpu.CompilerParams(vmem_limit_bytes=60 * 2**20),
        cost_estimate=pl.CostEstimate(flops=flops, bytes_accessed=in_bytes + out_bytes, transcendentals=0),
    )(*operands)


def shape(dims, kind):
    return jax.ShapeDtypeStruct(dims, kind)


def head_forward(values, gain, cosine, sine):
    scale = lax.rsqrt(jnp.mean(values * values, axis=0, keepdims=True) + NORM_EPSILON)
    hat = values * scale
    normed = hat * gain
    half = values.shape[0] // 2
    front, back = normed[:half], normed[half:]
    rotated = jnp.concatenate([front * cosine - back * sine, back * cosine + front * sine], axis=0)
    return scale, hat, rotated


def head_backward(grads, hat, scale, gain, cosine, sine):
    half = grads.shape[0] // 2
    front, back = grads[:half], grads[half:]
    d_normed = jnp.concatenate([front * cosine + back * sine, back * cosine - front * sine], axis=0)
    scaled = d_normed * gain
    inner = jnp.mean(hat * scaled, axis=0, keepdims=True)
    return scale * (scaled - hat * inner), jnp.sum(d_normed * hat, axis=1, keepdims=True)


def norm_back(d_normed, normed_hat, scale_values, gain_vector):
    scaled = d_normed * gain_vector
    inner = jnp.mean(normed_hat * scaled, axis=-1, keepdims=True)
    return (scale_values * (scaled - normed_hat * inner), d_normed * normed_hat)


def mm(left, right):
    return jnp.dot(left, right, preferred_element_type=F32)


def mm_t(left, right):
    return lax.dot_general(left, right, (((1,), (1,)), ((), ())), preferred_element_type=F32)


def outer_sum(left, right):
    return lax.dot_general(left, right, (((0,), (0,)), ((), ())), preferred_element_type=F32)


def swap_core(value):
    return lax.ppermute(value, "ctx", [(i, i ^ 1) for i in range(8)])


def move_z(value, step):
    return lax.ppermute(value, "ctx", [(i, (i + 2 * step) % 8) for i in range(8)])


def gather_ctx(block):
    pieces = []
    for step in STEPS:
        mine = block if step == 0 else move_z(block, -step)
        pieces += [mine, swap_core(mine)]
    return pieces


def start_scatter_ctx(mine, received):
    sums = [own + other.astype(F32) for own, other in zip(mine, received)]
    return [sums[0]] + [move_z(sums[slot].astype(BF16), STEPS[slot]) for slot in (3, 1, 2)]


def exchange_ctx(own, other):
    other = swap_core(other)
    out = [None] * 4
    for i, step in enumerate(STEPS):
        both = jnp.stack([own[i], other[i]])
        out[(0, 2, 1, 3)[i]] = move_z(both, step) if step else both
    return out


def stage(*values):
    return lax.optimization_barrier(values)


def transpose_mesh(value, flip=0):
    pairs = [
        ((d * 8 + c) * 8 + f, ((d ^ flip) * 8 + f) * 8 + c) for d in range(2) for c in range(8) for f in range(8)
    ]
    return lax.ppermute(value, ("dp", "ctx", "fsdp"), pairs)


def swap_dp(value):
    return lax.ppermute(value, "dp", [(0, 1), (1, 0)])


def move_y(value, step, flip=0):
    pairs = [(y * 2 + x, (y + step) % 4 * 2 + (x ^ flip)) for y in range(4) for x in range(2)]
    return lax.ppermute(value, "fsdp", pairs)


def pair_x(block):
    other = move_y(block, 0, 1)
    first = lax.axis_index("fsdp") % 2 == 0
    return jnp.concatenate([jnp.where(first, block, other), jnp.where(first, other, block)], axis=0)


def spread_y(pair):
    return [pair] + [move_y(pair, step) for step in (1, 3, 2)]


def fetch(pairs, sems, first=0):
    copies = [pltpu.make_async_copy(src, dst, sems.at[first + i]) for i, (src, dst) in enumerate(pairs)]
    for copy in copies:
        copy.start()
    return copies


def rows_of(pieces, ref):
    count = pieces[0].shape[0]
    return [(piece, ref.at[pl.ds(i * count, count)]) for i, piece in enumerate(pieces)]


def joined_y(place, pairs, ref):
    rows = pairs[0].shape[0]
    owners = [(place[0] + 4 - step) % 4 for step in (0, 1, 3, 2)]
    return [(pair, ref.at[pl.ds(pl.multiple_of(y * rows, rows), rows)]) for y, pair in zip(owners, pairs)]


def wait(copies):
    for copy in copies:
        copy.wait()


def all_to_all(blocks, axis):
    return lax.all_to_all(blocks, axis, split_axis=0, concat_axis=0, tiled=True)


def own_columns(weight, width, index):
    return lax.dynamic_slice_in_dim(weight, index * width, width, 1)


def attend_forward(*refs):
    pieces, w_whole, refs = refs[:8], refs[8], refs[9:]
    cos_ref, sin_ref, column_ref, row_ref, q_gain, k_gain = refs[:6]
    qkv_ref, lse_ref, own_ref, other_ref, x_ref, w_qkv, sems = refs[6:]
    w_copies = fetch([(w_whole, w_qkv)], sems, 8)
    x_copies = fetch(rows_of(pieces, x_ref), sems)
    wait(w_copies)
    length = qkv_ref.shape[1]
    count = length // 8
    head = q_gain.shape[0]
    for pair in range(4):
        wait(x_copies[2 * pair : 2 * pair + 2])
        lanes = slice(pair * 2 * count, (pair + 1) * 2 * count)
        qkv_ref[:, lanes] = jnp.transpose(mm(x_ref[lanes], w_qkv[...]))
    cosine, sine = cos_ref[...], sin_ref[...]
    queries = [
        head_forward(qkv_ref[h * head : (h + 1) * head], q_gain[...], cosine, sine)[2].astype(BF16) * BF16(head**-0.5)
        for h in range(2)
    ]
    key = jnp.transpose(head_forward(qkv_ref[2 * head : 3 * head], k_gain[...], cosine, sine)[2]).astype(BF16)
    value = qkv_ref[3 * head :].astype(BF16)
    width = column_ref.shape[1]
    for tile in range(length // width):
        lanes = slice(tile * width, (tile + 1) * width)
        allowed = column_ref[...] <= row_ref[:, lanes]
        outs = []
        for h in range(2):
            scores = jnp.where(allowed, mm(key, queries[h][:, lanes]), MASKED_SCORE)
            top = jnp.max(scores, axis=0, keepdims=True)
            weights = jnp.exp(scores - top)
            total = jnp.sum(weights, axis=0, keepdims=True)
            lse_ref[h : h + 1, lanes] = top + jnp.log(total)
            outs.append(mm(value, (weights * (1.0 / total)).astype(BF16)))
        mixed = jnp.transpose(jnp.concatenate(outs, axis=0)).astype(BF16)
        own_ref[tile] = mixed[:count]
        other_ref[tile] = mixed[count:]


def out_project(place, order, *refs):
    out_pairs, blocks, (tokens, gain, resid_ref, normed_ref, w_out, mixed_ref, sems) = refs[:4], refs[4:8], refs[8:]
    copies = fetch(joined_y(place, out_pairs, w_out), sems)
    count = blocks[0].shape[2]
    for i in range(8):
        lanes = pl.ds(pl.multiple_of(order[i] * count, count), count)
        mixed_ref[:, lanes] = blocks[i // 2][i % 2]
    wait(copies)
    resid = tokens[...].astype(F32) + mm(mixed_ref[...], w_out[...])
    resid_ref[...] = resid
    normed_ref[...] = (resid * rms_scale(resid) * gain[...]).astype(BF16)


def resid_backward(place, order, *refs):
    out_pairs, refs = refs[:4], refs[4:]
    total, move_a, move_b, move_c, resid_ref, cot_ref, gain_ref = refs[:7]
    d_resid_ref, d_attn_ref, gain_part_ref, own_ref, other_ref, w_out, d_mixed_ref, sems = refs[7:]
    copies = fetch(joined_y(place, out_pairs, w_out), sems)
    d_second = total[...] + move_a[...].astype(F32) + move_b[...].astype(F32) + move_c[...].astype(F32)
    resid = resid_ref[...]
    scale = rms_scale(resid)
    d_from, gain_part = norm_back(d_second, resid * scale, scale, gain_ref[...])
    gain_part_ref[...] = jnp.sum(gain_part, axis=0, keepdims=True)
    d_resid = cot_ref[...].astype(F32) + d_from
    d_resid_ref[...] = d_resid
    d_attn = d_resid.astype(BF16)
    d_attn_ref[...] = d_attn
    wait(copies)
    d_mixed_ref[...] = mm_t(d_attn, w_out[...]).astype(BF16)
    count = own_ref.shape[2]
    for i in range(8):
        lanes = pl.ds(pl.multiple_of(order[i] * count, count), count)
        (own_ref, other_ref)[i % 2][i // 2] = d_mixed_ref[:, lanes]


def attend_backward(*refs):
    order, w_whole, d_blocks, refs = refs[0], refs[1], refs[2:6], refs[6:]
    cos_ref, sin_ref, column_ref, row_ref, q_gain, k_gain, qkv_ref, lse_ref = refs[:8]
    q_gain_ref, k_gain_ref, d_low_ref, d_first_ref, d_qkv_ref, w_qkv, sems = refs[8:]
    copies = fetch([(w_whole, w_qkv)], sems)
    length = qkv_ref.shape[1]
    head = q_gain.shape[0]
    count = length // 8
    cosine, sine = cos_ref[...], sin_ref[...]
    scales, hats, queries = [], [], []
    for h in range(2):
        scale, hat, rotated = head_forward(qkv_ref[h * head : (h + 1) * head], q_gain[...], cosine, sine)
        scales.append(scale)
        hats.append(hat)
        queries.append(rotated.astype(BF16) * BF16(head**-0.5))
    k_scale, k_hat, rotated = head_forward(qkv_ref[2 * head : 3 * head], k_gain[...], cosine, sine)
    key_rows = rotated.astype(BF16)
    key = jnp.transpose(rotated).astype(BF16)
    value = jnp.transpose(qkv_ref[3 * head :]).astype(BF16)
    width = column_ref.shape[1]
    d_key = jnp.zeros((length, head), F32)
    d_value = jnp.zeros((length, head), F32)
    for tile in range(length // width):
        lanes = slice(tile * width, (tile + 1) * width)
        allowed = column_ref[...] <= row_ref[:, lanes]
        d_mixed = jnp.concatenate([d_blocks[tile][0], d_blocks[tile][1]], axis=0)
        d_mixed = jnp.transpose(d_mixed.astype(F32)).astype(BF16)
        for h in range(2):
            rows = slice(h * head, (h + 1) * head)
            query = queries[h][:, lanes]
            probs = jnp.where(allowed, jnp.exp(mm(key, query) - lse_ref[h : h + 1, lanes]), 0.0)
            d_probs = mm(value, d_mixed[rows])
            inner = jnp.sum(probs * d_probs, axis=0, keepdims=True)
            d_scores = (probs * (d_probs - inner)).astype(BF16)
            d_value += mm_t(probs.astype(BF16), d_mixed[rows])
            d_key += mm_t(d_scores, query)
            d_qkv_ref[rows, lanes] = mm(key_rows, d_scores) * head**-0.5
    for h in range(2):
        rows = slice(h * head, (h + 1) * head)
        d_query, gain_part = head_backward(d_qkv_ref[rows], hats[h], scales[h], q_gain[...], cosine, sine)
        d_qkv_ref[rows] = d_query
        if h == 0:
            q_gain_ref[...] = gain_part
        else:
            q_gain_ref[...] += gain_part
    d_keys, gain_part = head_backward(jnp.transpose(d_key), k_hat, k_scale, k_gain[...], cosine, sine)
    k_gain_ref[...] = gain_part
    d_qkv_ref[2 * head : 3 * head] = d_keys
    d_qkv_ref[3 * head :] = jnp.transpose(d_value)
    wait(copies)
    for tile in range(4):
        lanes = slice(tile * 2 * count, (tile + 1) * 2 * count)
        d_qkv = jnp.transpose(d_qkv_ref[:, lanes]).astype(BF16)
        d_low_ref[lanes] = d_qkv
        d_first = mm_t(d_qkv, w_qkv[...])
        d_first_ref[order[2 * tile]] = d_first[:count].astype(BF16)
        d_first_ref[order[2 * tile + 1]] = d_first[count:].astype(BF16)


def attend_weights(*refs):
    pieces, d_pieces, own, other, w_whole = refs[:8], refs[8:16], *refs[16:19]
    d_low, attn_gain, ffn_part, q_part, k_part = refs[19:24]
    out_ref, x_ref, d_ref, mixed_ref, d_low_ref, w_qkv, sems = refs[24:]
    count = pieces[0].shape[0]
    width = d_low_ref.shape[1]
    mixed = []
    for i in range(4):
        mixed += [(own.at[i], mixed_ref.at[pl.ds(2 * i * count, count)])]
        mixed += [(other.at[i], mixed_ref.at[pl.ds((2 * i + 1) * count, count)])]
    copies = fetch([(d_low, d_low_ref), *rows_of(pieces, x_ref), (w_whole, w_qkv)], sems)
    more = fetch([*mixed, *rows_of(d_pieces, d_ref)], sems, len(copies))
    wait(copies)
    grad_qkv = outer_sum(d_low_ref[...], x_ref[...])
    attn_part = jnp.sum(grad_qkv * jnp.transpose(w_qkv[...].astype(F32)), axis=0, keepdims=True) / attn_gain[...]
    grad_qkv = jnp.transpose(grad_qkv).astype(BF16)
    wait(more)
    grad_out = jnp.transpose(outer_sum(mixed_ref[...], d_ref[...])).astype(BF16)
    lines = [part[:, i * 128 : (i + 1) * 128] for part in (attn_part, ffn_part[...]) for i in range(8)]
    lines.append(jnp.concatenate([jnp.transpose(q_part[...]), jnp.transpose(k_part[...])], axis=1))
    gains = jnp.concatenate(lines + [jnp.zeros((7, 128), F32)], axis=0)
    high = gains.astype(BF16)
    low = (gains - high.astype(F32)).astype(BF16)
    gains = jnp.concatenate([high, low, jnp.zeros((count - 48, 128), BF16)], axis=0)
    for i in range(8):
        rows = slice(i * count, (i + 1) * count)
        out_ref[i, :, :width] = grad_qkv[rows]
        out_ref[i, :, width : width + 128] = gains
        out_ref[i, :, width + 128 :] = grad_out[rows]


def ffn(*refs):
    order, seconds, cots, weights = refs[0], refs[1:9], refs[9], refs[10]
    hidden_ref, d_ffn_ref, block_ref, d_send = refs[11:15]
    d_mine, (x_ref, cot_ref, w_ref, sems) = refs[15:19], refs[19:]
    copies = fetch([(weights, w_ref)], sems)
    loads = rows_of(seconds, x_ref) + rows_of([cots.at[order[i]] for i in range(8)], cot_ref)
    loads = fetch([loads[8 * j + 2 * g + i] for g in (3, 1, 2, 0) for j in (0, 1) for i in (0, 1)], sems, 1)
    wait(copies)
    width = hidden_ref.shape[1]
    count = seconds[0].shape[0]
    for group in (3, 1, 2, 0):
        rows = slice(2 * group * count, 2 * (group + 1) * count)
        wait(loads[:4])
        loads = loads[4:]
        x, cot = x_ref[rows], cot_ref[rows]
        both = mm(x, w_ref[:, : 2 * width])
        gate, up = both[:, :width], both[:, width:]
        sigmoid = 1.0 / (1.0 + jnp.exp(-gate))
        act = gate * sigmoid
        hidden = (act * up).astype(BF16)
        hidden_ref[rows] = hidden
        d_hidden = mm(cot, w_ref[:, 2 * width :])
        d_gate = d_hidden * up * sigmoid * (1.0 + gate * (1.0 - sigmoid))
        d_ffn = jnp.concatenate([d_gate, d_hidden * act], axis=1).astype(BF16)
        d_ffn_ref[rows] = d_ffn
        d_second = mm_t(d_ffn, w_ref[:, : 2 * width])
        d_mine[group][...] = d_second[:count]
        d_send[group] = d_second[count:].astype(BF16)
        out = mm_t(hidden, w_ref[:, 2 * width :])
        block_ref[order[2 * group]] = out[:count].astype(BF16)
        block_ref[order[2 * group + 1]] = out[count:].astype(BF16)


def ffn_weights(*refs):
    order, seconds, cots, hidden, d_ffn = refs[0], refs[1:9], *refs[9:12]
    out_ref, x_ref, cot_ref, hidden_ref, d_ffn_ref, sems = refs[12:]
    count = seconds[0].shape[0]
    copies = fetch([(d_ffn, d_ffn_ref), *rows_of(seconds, x_ref)], sems)
    more = fetch([(hidden, hidden_ref), *rows_of([cots.at[order[i]] for i in range(8)], cot_ref)], sems, 9)
    for left_ref, right_ref, columns in ((x_ref, d_ffn_ref, 0), (cot_ref, hidden_ref, d_ffn_ref.shape[1])):
        wait(more if columns else copies)
        width = right_ref.shape[1]
        for pair in range(4):
            both = outer_sum(left_ref[:, 2 * pair * count : 2 * (pair + 1) * count], right_ref[...]).astype(BF16)
            out_ref[2 * pair, :, columns : columns + width] = both[:count]
            out_ref[2 * pair + 1, :, columns : columns + width] = both[count:]
    used = d_ffn_ref.shape[1] + hidden_ref.shape[1]
    out_ref[:, :, used:] = jnp.zeros((8, count, out_ref.shape[2] - used), BF16)


def sum_ffn(parts, gate_up_ref, down_ref):
    width = gate_up_ref.shape[1]
    total = sum(parts[i].astype(F32) for i in range(8)).astype(BF16)
    gate_up_ref[...] = total[:, :width]
    down_ref[...] = total[:, width : width + down_ref.shape[1]]


def sum_attn(parts, first_ref, out_ref):
    count = out_ref.shape[0]
    width = first_ref.shape[1] - 128
    total = sum(parts[i].astype(F32) for i in range(8))
    first_ref[:, :width] = total[:, :width].astype(BF16)
    pack_gains(first_ref, width, total[:24, width : width + 128] + total[24:48, width : width + 128])
    out_ref[...] = total[:, width + 128 :].astype(BF16)


def pack_gains(ref, width, gains):
    high = gains.astype(BF16)
    low = (gains - high.astype(F32)).astype(BF16)
    rest = jnp.zeros((ref.shape[0] - 48, 128), BF16)
    ref[:, width : width + 128] = jnp.concatenate([high, low, rest], axis=0)


def join_ffn(own, other, down, down_other, out_ref):
    width = own.shape[1]
    out_ref[:, :width] = (own[...].astype(F32) + other[...].astype(F32)).astype(BF16)
    out_ref[:, width:] = (down[...].astype(F32) + down_other[...].astype(F32)).astype(BF16)


def join_attn(own, other, out, out_other, out_ref):
    width = own.shape[1] - 128
    total = own[...].astype(F32) + other[...].astype(F32)
    out_ref[:, :width] = total[:, :width].astype(BF16)
    pack_gains(out_ref, width, total[:24, width:] + total[24:48, width:])
    out_ref[:, width + 128 :] = (out[...].astype(F32) + out_other[...].astype(F32)).astype(BF16)


def assemble_ffn(*refs):
    order, pieces, (gate_ref, up_ref, down_ref, held, sems) = refs[0], refs[1:9], refs[9:]
    width = down_ref.shape[0]
    count = pieces[0].shape[0]
    wait(fetch([(pieces[i], held.at[order[i]]) for i in range(8)], sems))
    for owner in range(8):
        columns = slice(owner * width, (owner + 1) * width)
        gate_ref[:, columns] = held[owner, :, :width].astype(F32)
        up_ref[:, columns] = held[owner, :, width : 2 * width].astype(F32)
        down = held[owner, :, 2 * width :].astype(F32)
        down_ref[:, owner * count : (owner + 1) * count] = jnp.transpose(down)


def assemble_attn(*refs):
    order, pieces, (query_ref, key_ref, value_ref, out_ref, gains_ref, held, sems) = refs[0], refs[1:9], refs[9:]
    count = pieces[0].shape[0]
    half = count // 2
    wait(fetch([(pieces[i], held.at[order[i]]) for i in range(8)], sems))
    gains = jnp.zeros(gains_ref.shape, F32)
    for owner in range(8):
        columns = slice(owner * count, (owner + 1) * count)
        narrow = slice(owner * half, (owner + 1) * half)
        part = held[owner].astype(F32)
        query_ref[:, columns] = part[:, :count]
        key_ref[:, narrow] = part[:, count : count + half]
        value_ref[:, narrow] = part[:, count + half : 2 * count]
        out_ref[:, columns] = jnp.transpose(part[:, 3 * count :])
        gains += part[:24, 2 * count : 3 * count] + part[24:48, 2 * count : 3 * count]
    gains_ref[...] = gains


def body(
    hidden_in,
    positions,
    cotangent,
    attn_gain,
    w_query,
    w_key,
    w_value,
    query_gain,
    key_gain,
    w_out,
    ffn_gain,
    w_gate,
    w_up,
    w_down,
):
    ctx = lax.axis_index("ctx")
    tokens = hidden_in[0].astype(F32)
    count, width = tokens.shape
    head_size = query_gain.shape[0]
    q_width = w_query.shape[1] // 8
    k_width = w_key.shape[1] // 8
    ff_width = w_gate.shape[1] // 8

    z_index, core = ctx // 2, ctx % 2
    owners = jnp.stack(
        [((z_index + step) % 4) * 2 + (core ^ flip) for step in STEPS for flip in (0, 1)]
    )
    places = positions[0].reshape(8, count)[owners].reshape(8 * count)
    length = 8 * count
    cosine_table, sine_table = rope_tables(places, head_size)
    column = jnp.broadcast_to(places[:, None], (length, 2 * count))
    row = places[None]
    gains = (query_gain[:, None], key_gain[:, None])
    tables = (cosine_table, sine_table, column, row)
    block = shape((count, q_width), BF16)
    low_rows, rows = shape((count, width), BF16), shape((count, width), F32)
    qkv_width = q_width + 2 * k_width

    place = jnp.stack([lax.axis_index("fsdp") // 2, lax.axis_index("fsdp") % 2])
    wide, head_rows = pltpu.VMEM((length, width), BF16), pltpu.VMEM((length, qkv_width), BF16)

    first_scale = rms_scale(tokens)
    first_hat = tokens * first_scale
    first_normed = (first_hat * attn_gain).astype(BF16)
    first_pieces = gather_ctx(first_normed)
    qkv_block = jnp.concatenate(
        [own_columns(w_query, q_width, ctx), own_columns(w_key, k_width, ctx), own_columns(w_value, k_width, ctx)],
        axis=1,
    )
    w_qkv = all_to_all(jnp.broadcast_to(qkv_block[None], (8, *qkv_block.shape)), "fsdp").reshape(width, qkv_width)
    out_pair = pair_x(w_out)
    cot = cotangent[0]
    cot_copies = jnp.broadcast_to(cot[None], (8, count, width))
    down_chunk = transpose_mesh(jnp.transpose(own_columns(w_down, width // 8, ctx)))
    ffn_block = jnp.concatenate(
        [own_columns(w_gate, ff_width, ctx), own_columns(w_up, ff_width, ctx), down_chunk], axis=1
    )
    ffn_block, w_qkv = stage(ffn_block, w_qkv)
    ffn_rows = lax.all_gather(ffn_block, "fsdp", axis=0, tiled=True)
    first_pieces, w_qkv, tables, out_pair, cot_copies = stage(first_pieces, w_qkv, tables, out_pair, cot_copies)

    cots = all_to_all(cot_copies, "ctx")
    out_pairs = spread_y(out_pair)
    qkv, lse, own, other = call(
        attend_forward,
        [shape((qkv_width, length), F32), shape((8, length), F32)] + [shape((4, count, q_width), BF16)] * 2,
        (),
        (*first_pieces, w_qkv),
        (*tables, *gains),
        4 * 10**9,
        [wide, pltpu.VMEM((width, qkv_width), BF16)],
        9,
    )

    mixed_blocks = exchange_ctx(own, other)
    mixed_blocks, out_pairs = stage(mixed_blocks, out_pairs)
    square = pltpu.VMEM((width, width), BF16)
    residual, second_normed = call(
        out_project,
        [rows, low_rows],
        (place, owners),
        out_pairs,
        (*mixed_blocks, hidden_in[0], ffn_gain[None]),
        3 * 10**8,
        [square, pltpu.VMEM((count, width), BF16)],
        4,
    )

    second_pieces = gather_ctx(second_normed)
    hidden_shape, d_ffn_shape = shape((length, ff_width), BF16), shape((length, 2 * ff_width), BF16)
    hidden, d_ffn, block_parts, d_send, *d_mine = call(
        ffn,
        [hidden_shape, d_ffn_shape, shape((8, count, width), BF16), shape((4, count, width), BF16)] + [rows] * 4,
        (owners,),
        (*second_pieces, cots, ffn_rows),
        (),
        8 * 10**9,
        [wide, wide, pltpu.VMEM((width, 3 * ff_width), BF16)],
        17,
    )

    d_moves = start_scatter_ctx(d_mine, swap_core(d_send))
    padded = -(-3 * ff_width // 128) * 128
    (ffn_partial,) = call(
        ffn_weights,
        [shape((8, count, padded), BF16)],
        (owners,),
        (*second_pieces, cots, hidden, d_ffn),
        (),
        4 * 10**9,
        [wide, wide, pltpu.VMEM((length, ff_width), BF16), pltpu.VMEM((length, 2 * ff_width), BF16)],
        18,
    )
    ffn_sums = all_to_all(ffn_partial, "fsdp")
    d_moves, _ = stage(d_moves, ffn_partial)
    block_sum = lax.psum_scatter(block_parts, "ctx", scatter_dimension=0, tiled=False)
    block_out = (residual + block_sum.astype(F32)).astype(BF16)
    d_resid, d_attn, ffn_gain_part, *d_blocks = call(
        resid_backward,
        [rows, low_rows, shape((1, width), F32)] + [shape((4, count, q_width), BF16)] * 2,
        (place, owners),
        out_pairs,
        (*d_moves, residual, cot, ffn_gain[None]),
        3 * 10**8,
        [square, pltpu.VMEM((count, width), BF16)],
        4,
    )

    d_blocks = exchange_ctx(*d_blocks)
    d_blocks, d_attn = stage(d_blocks, d_attn)

    d_pieces = gather_ctx(d_attn)
    q_gain_part, k_gain_part, d_qkv, d_first_parts = call(
        attend_backward,
        [
            shape((head_size, 1), F32),
            shape((head_size, 1), F32),
            shape((length, qkv_width), BF16),
            shape((8, count, width), BF16),
        ],
        (owners,),
        (w_qkv,),
        (*d_blocks, *tables, *gains, qkv, lse),
        8 * 10**9,
        [pltpu.VMEM((qkv_width, length), F32), pltpu.VMEM((width, qkv_width), BF16)],
        1,
    )
    half, down = call(
        sum_ffn, [shape((count, 2 * ff_width), BF16), shape((count, ff_width), BF16)], (), (), (ffn_sums,), 10**6
    )
    d_qkv, d_pieces, half, down = stage(d_qkv, d_pieces, half, down)
    ffn_steps = (half, swap_dp(half), transpose_mesh(down), transpose_mesh(down, 1))
    d_first = lax.psum_scatter(d_first_parts, "ctx", scatter_dimension=0, tiled=False).astype(F32)
    (attn_partial,) = call(
        attend_weights,
        [shape((8, count, qkv_width + 128 + q_width), BF16)],
        (),
        (*first_pieces, *d_pieces, own, other, w_qkv, d_qkv),
        (attn_gain[None], ffn_gain_part, q_gain_part, k_gain_part),
        10**9,
        [wide, wide, pltpu.VMEM((length, q_width), BF16), head_rows, pltpu.VMEM((width, qkv_width), BF16)],
        26,
    )
    attn_partial, ffn_steps = stage(attn_partial, ffn_steps)

    attn_sums = all_to_all(attn_partial, "fsdp")
    (joined,) = call(
        join_ffn,
        [shape((count, 3 * ff_width), BF16)],
        (),
        (),
        ffn_steps,
        10**6,
    )
    ffn_parts = gather_ctx(joined)
    half, out = call(
        sum_attn, [shape((count, qkv_width + 128), BF16), shape((count, q_width), BF16)], (), (), (attn_sums,), 10**6
    )
    (joined,) = call(
        join_attn,
        [shape((count, qkv_width + 128 + q_width), BF16)],
        (),
        (),
        (half, swap_dp(half), transpose_mesh(out), transpose_mesh(out, 1)),
        10**6,
    )
    attn_parts = gather_ctx(joined)
    d_from_first, _ = norm_back(d_first, first_hat, first_scale, attn_gain)
    grad_in = (d_resid + d_from_first).astype(BF16)
    grad_gate, grad_up, grad_down = call(
        assemble_ffn,
        [shape((count, 8 * ff_width), F32)] * 2 + [shape((ff_width, width), F32)],
        (owners,),
        ffn_parts,
        (),
        10**6,
        [pltpu.VMEM((8, count, 3 * ff_width), BF16)],
        8,
    )
    grad_query, grad_key, grad_value, grad_out, totals = call(
        assemble_attn,
        [shape((count, width), F32)] + [shape((count, 8 * k_width), F32)] * 2 + [shape((q_width, width), F32), shape((24, 128), F32)],
        (owners,),
        attn_parts,
        (),
        10**6,
        [pltpu.VMEM((8, count, qkv_width + 128 + q_width), BF16)],
        8,
    )
    totals = totals.reshape(-1)
    grad_attn_gain = totals[:width]
    grad_ffn_gain = totals[width : 2 * width]
    grad_query_gain = totals[2 * width : 2 * width + head_size]
    grad_key_gain = totals[2 * width + head_size : 2 * width + 2 * head_size]
    return (
        block_out[None],
        grad_in[None],
        grad_attn_gain,
        grad_query,
        grad_key,
        grad_value,
        grad_query_gain,
        grad_key_gain,
        grad_out,
        grad_ffn_gain,
        grad_gate,
        grad_up,
        grad_down,
    )


def solution(mesh):
    in_specs = (
        P(("dp", "fsdp"), "ctx", None),
        P(("dp", "fsdp"), None),
        P(("dp", "fsdp"), "ctx", None),
        P(),
        P("fsdp", None),
        P("fsdp", None),
        P("fsdp", None),
        P(),
        P(),
        P("fsdp", None),
        P(),
        P("fsdp", None),
        P("fsdp", None),
        P("fsdp", None),
    )
    out_specs = (
        P(("dp", "fsdp"), "ctx", None),
        P(("dp", "fsdp"), "ctx", None),
        P(),
        P("fsdp", None),
        P("fsdp", None),
        P("fsdp", None),
        P(),
        P(),
        P("fsdp", None),
        P(),
        P("fsdp", None),
        P("fsdp", None),
        P("fsdp", None),
    )
    return jax.shard_map(body, mesh=mesh, in_specs=in_specs, out_specs=out_specs, check_vma=False)
```

```python
import math

import jax
import jax.numpy as jnp
from jax import lax
from jax.experimental import pallas as pl
from jax.experimental.pallas import tpu as pltpu
from jax.sharding import PartitionSpec as P

NORM_EPSILON = 1e-05
ROPE_BASE = 1000000.0
MASKED_SCORE = -1e30
BF16 = jnp.bfloat16
F32 = jnp.float32
STEPS = (0, -1, 1, 2)


def rms_scale(values):
    return lax.rsqrt(jnp.mean(values * values, axis=-1, keepdims=True) + NORM_EPSILON)


def rope_tables(places, head_size):
    half_width = head_size // 2
    pair_index = jnp.arange(half_width, dtype=F32)
    frequency = ROPE_BASE ** (-2.0 * pair_index / head_size)
    angles = frequency[:, None] * places.astype(F32)[None, :]
    return jnp.cos(angles), jnp.sin(angles)


def call(kernel, out_shapes, scalars, fetched, args, flops, scratch=(), copies=0):
    vmem = pl.BlockSpec(memory_space=pltpu.VMEM)
    operands = (*scalars, *fetched, *args)
    out_bytes = sum(math.prod(o.shape) * o.dtype.itemsize for o in out_shapes)
    in_bytes = sum(math.prod(a.shape) * a.dtype.itemsize for a in operands)
    return pl.pallas_call(
        kernel,
        out_shape=out_shapes,
        in_specs=[pl.BlockSpec(memory_space=pltpu.SMEM)] * len(scalars)
        + [pl.BlockSpec(memory_space=pl.ANY)] * len(fetched)
        + [vmem] * len(args),
        out_specs=[vmem] * len(out_shapes),
        scratch_shapes=list(scratch) + ([pltpu.SemaphoreType.DMA((copies,))] if copies else []),
        compiler_params=pltpu.CompilerParams(vmem_limit_bytes=60 * 2**20),
        cost_estimate=pl.CostEstimate(flops=flops, bytes_accessed=in_bytes + out_bytes, transcendentals=0),
    )(*operands)


def shape(dims, kind):
    return jax.ShapeDtypeStruct(dims, kind)


def head_forward(values, gain, cosine, sine):
    scale = lax.rsqrt(jnp.mean(values * values, axis=0, keepdims=True) + NORM_EPSILON)
    hat = values * scale
    normed = hat * gain
    half = values.shape[0] // 2
    front, back = normed[:half], normed[half:]
    rotated = jnp.concatenate([front * cosine - back * sine, back * cosine + front * sine], axis=0)
    return scale, hat, rotated


def head_backward(grads, hat, scale, gain, cosine, sine):
    half = grads.shape[0] // 2
    front, back = grads[:half], grads[half:]
    d_normed = jnp.concatenate([front * cosine + back * sine, back * cosine - front * sine], axis=0)
    scaled = d_normed * gain
    inner = jnp.mean(hat * scaled, axis=0, keepdims=True)
    return scale * (scaled - hat * inner), jnp.sum(d_normed * hat, axis=1, keepdims=True)


def norm_back(d_normed, normed_hat, scale_values, gain_vector):
    scaled = d_normed * gain_vector
    inner = jnp.mean(normed_hat * scaled, axis=-1, keepdims=True)
    return (scale_values * (scaled - normed_hat * inner), d_normed * normed_hat)


def mm(left, right):
    return jnp.dot(left, right, preferred_element_type=F32)


def mm_t(left, right):
    return lax.dot_general(left, right, (((1,), (1,)), ((), ())), preferred_element_type=F32)


def outer_sum(left, right):
    return lax.dot_general(left, right, (((0,), (0,)), ((), ())), preferred_element_type=F32)


def swap_core(value):
    return lax.ppermute(value, "ctx", [(i, i ^ 1) for i in range(8)])


def move_z(value, step):
    return lax.ppermute(value, "ctx", [(i, (i + 2 * step) % 8) for i in range(8)])


def move_pieces(block):
    return [move_z(block, -step) if step else block for step in STEPS]


def swap_pieces(moved):
    pieces = []
    for piece in moved:
        pieces += [piece, swap_core(piece)]
    return pieces


def gather_ctx(block):
    return swap_pieces(move_pieces(block))


def start_scatter_ctx(mine, received):
    sums = [own + other.astype(F32) for own, other in zip(mine, received)]
    return [sums[0]] + [move_z(sums[slot].astype(BF16), STEPS[slot]) for slot in (3, 1, 2)]


def exchange_ctx(own, other):
    other = swap_core(other)
    out = [None] * 4
    for i, step in enumerate(STEPS):
        both = jnp.stack([own[i], other[i]])
        out[(0, 2, 1, 3)[i]] = move_z(both, step) if step else both
    return out


def stage(*values):
    return lax.optimization_barrier(values)


def transpose_mesh(value, flip=0):
    pairs = [
        ((d * 8 + c) * 8 + f, ((d ^ flip) * 8 + f) * 8 + c) for d in range(2) for c in range(8) for f in range(8)
    ]
    return lax.ppermute(value, ("dp", "ctx", "fsdp"), pairs)


def swap_dp(value):
    return lax.ppermute(value, "dp", [(0, 1), (1, 0)])


def move_y(value, step, flip=0):
    pairs = [(y * 2 + x, (y + step) % 4 * 2 + (x ^ flip)) for y in range(4) for x in range(2)]
    return lax.ppermute(value, "fsdp", pairs)


def pair_x(block):
    other = move_y(block, 0, 1)
    first = lax.axis_index("fsdp") % 2 == 0
    return jnp.concatenate([jnp.where(first, block, other), jnp.where(first, other, block)], axis=0)


def spread_y(pair):
    return [pair] + [move_y(pair, step) for step in (1, 3, 2)]


def fetch(pairs, sems, first=0):
    copies = [pltpu.make_async_copy(src, dst, sems.at[first + i]) for i, (src, dst) in enumerate(pairs)]
    for copy in copies:
        copy.start()
    return copies


def rows_of(pieces, ref):
    count = pieces[0].shape[0]
    return [(piece, ref.at[pl.ds(i * count, count)]) for i, piece in enumerate(pieces)]


def joined_y(place, pairs, ref):
    rows = pairs[0].shape[0]
    owners = [(place[0] + 4 - step) % 4 for step in (0, 1, 3, 2)]
    return [(pair, ref.at[pl.ds(pl.multiple_of(y * rows, rows), rows)]) for y, pair in zip(owners, pairs)]


def wait(copies):
    for copy in copies:
        copy.wait()


def all_to_all(blocks, axis):
    return lax.all_to_all(blocks, axis, split_axis=0, concat_axis=0, tiled=True)


def own_columns(weight, width, index):
    return lax.dynamic_slice_in_dim(weight, index * width, width, 1)


def attend_forward(*refs):
    pieces, w_whole, refs = refs[:8], refs[8], refs[9:]
    cos_ref, sin_ref, column_ref, row_ref, q_gain, k_gain = refs[:6]
    qkv_ref, lse_ref, own_ref, other_ref, x_ref, w_qkv, sems = refs[6:]
    w_copies = fetch([(w_whole, w_qkv)], sems, 8)
    x_copies = fetch(rows_of(pieces, x_ref), sems)
    wait(w_copies)
    length = qkv_ref.shape[1]
    count = length // 8
    head = q_gain.shape[0]
    for pair in range(4):
        wait(x_copies[2 * pair : 2 * pair + 2])
        lanes = slice(pair * 2 * count, (pair + 1) * 2 * count)
        qkv_ref[:, lanes] = jnp.transpose(mm(x_ref[lanes], w_qkv[...]))
    cosine, sine = cos_ref[...], sin_ref[...]
    queries = [
        head_forward(qkv_ref[h * head : (h + 1) * head], q_gain[...], cosine, sine)[2].astype(BF16) * BF16(head**-0.5)
        for h in range(2)
    ]
    key = jnp.transpose(head_forward(qkv_ref[2 * head : 3 * head], k_gain[...], cosine, sine)[2]).astype(BF16)
    value = qkv_ref[3 * head :].astype(BF16)
    width = column_ref.shape[1]
    for tile in range(length // width):
        lanes = slice(tile * width, (tile + 1) * width)
        allowed = column_ref[...] <= row_ref[:, lanes]
        outs = []
        for h in range(2):
            scores = jnp.where(allowed, mm(key, queries[h][:, lanes]), MASKED_SCORE)
            top = jnp.max(scores, axis=0, keepdims=True)
            weights = jnp.exp(scores - top)
            total = jnp.sum(weights, axis=0, keepdims=True)
            lse_ref[h : h + 1, lanes] = top + jnp.log(total)
            outs.append(mm(value, (weights * (1.0 / total)).astype(BF16)))
        mixed = jnp.transpose(jnp.concatenate(outs, axis=0)).astype(BF16)
        own_ref[tile] = mixed[:count]
        other_ref[tile] = mixed[count:]


def out_project(place, order, *refs):
    out_pairs, blocks, (tokens, gain, resid_ref, normed_ref, w_out, mixed_ref, sems) = refs[:4], refs[4:8], refs[8:]
    copies = fetch(joined_y(place, out_pairs, w_out), sems)
    count = blocks[0].shape[2]
    for i in range(8):
        lanes = pl.ds(pl.multiple_of(order[i] * count, count), count)
        mixed_ref[:, lanes] = blocks[i // 2][i % 2]
    wait(copies)
    resid = tokens[...].astype(F32) + mm(mixed_ref[...], w_out[...])
    resid_ref[...] = resid
    normed_ref[...] = (resid * rms_scale(resid) * gain[...]).astype(BF16)


def resid_backward(place, order, *refs):
    out_pairs, refs = refs[:4], refs[4:]
    total, move_a, move_b, move_c, resid_ref, cot_ref, gain_ref = refs[:7]
    d_resid_ref, d_attn_ref, gain_part_ref, own_ref, other_ref, w_out, d_mixed_ref, sems = refs[7:]
    copies = fetch(joined_y(place, out_pairs, w_out), sems)
    d_second = total[...] + move_a[...].astype(F32) + move_b[...].astype(F32) + move_c[...].astype(F32)
    resid = resid_ref[...]
    scale = rms_scale(resid)
    d_from, gain_part = norm_back(d_second, resid * scale, scale, gain_ref[...])
    gain_part_ref[...] = jnp.sum(gain_part, axis=0, keepdims=True)
    d_resid = cot_ref[...].astype(F32) + d_from
    d_resid_ref[...] = d_resid
    d_attn = d_resid.astype(BF16)
    d_attn_ref[...] = d_attn
    wait(copies)
    d_mixed_ref[...] = mm_t(d_attn, w_out[...]).astype(BF16)
    count = own_ref.shape[2]
    for i in range(8):
        lanes = pl.ds(pl.multiple_of(order[i] * count, count), count)
        (own_ref, other_ref)[i % 2][i // 2] = d_mixed_ref[:, lanes]


def attend_backward(*refs):
    order, w_whole, d_blocks, refs = refs[0], refs[1], refs[2:6], refs[6:]
    cos_ref, sin_ref, column_ref, row_ref, q_gain, k_gain, qkv_ref, lse_ref = refs[:8]
    q_gain_ref, k_gain_ref, d_low_ref, d_first_ref, d_qkv_ref, w_qkv, sems = refs[8:]
    copies = fetch([(w_whole, w_qkv)], sems)
    length = qkv_ref.shape[1]
    head = q_gain.shape[0]
    count = length // 8
    cosine, sine = cos_ref[...], sin_ref[...]
    scales, hats, queries = [], [], []
    for h in range(2):
        scale, hat, rotated = head_forward(qkv_ref[h * head : (h + 1) * head], q_gain[...], cosine, sine)
        scales.append(scale)
        hats.append(hat)
        queries.append(rotated.astype(BF16) * BF16(head**-0.5))
    k_scale, k_hat, rotated = head_forward(qkv_ref[2 * head : 3 * head], k_gain[...], cosine, sine)
    key_rows = rotated.astype(BF16)
    key = jnp.transpose(rotated).astype(BF16)
    value = jnp.transpose(qkv_ref[3 * head :]).astype(BF16)
    width = column_ref.shape[1]
    d_key = jnp.zeros((length, head), F32)
    d_value = jnp.zeros((length, head), F32)
    for tile in range(length // width):
        lanes = slice(tile * width, (tile + 1) * width)
        allowed = column_ref[...] <= row_ref[:, lanes]
        d_mixed = jnp.concatenate([d_blocks[tile][0], d_blocks[tile][1]], axis=0)
        d_mixed = jnp.transpose(d_mixed.astype(F32)).astype(BF16)
        for h in range(2):
            rows = slice(h * head, (h + 1) * head)
            query = queries[h][:, lanes]
            probs = jnp.where(allowed, jnp.exp(mm(key, query) - lse_ref[h : h + 1, lanes]), 0.0)
            d_probs = mm(value, d_mixed[rows])
            inner = jnp.sum(probs * d_probs, axis=0, keepdims=True)
            d_scores = (probs * (d_probs - inner)).astype(BF16)
            d_value += mm_t(probs.astype(BF16), d_mixed[rows])
            d_key += mm_t(d_scores, query)
            d_qkv_ref[rows, lanes] = mm(key_rows, d_scores) * head**-0.5
    for h in range(2):
        rows = slice(h * head, (h + 1) * head)
        d_query, gain_part = head_backward(d_qkv_ref[rows], hats[h], scales[h], q_gain[...], cosine, sine)
        d_qkv_ref[rows] = d_query
        if h == 0:
            q_gain_ref[...] = gain_part
        else:
            q_gain_ref[...] += gain_part
    d_keys, gain_part = head_backward(jnp.transpose(d_key), k_hat, k_scale, k_gain[...], cosine, sine)
    k_gain_ref[...] = gain_part
    d_qkv_ref[2 * head : 3 * head] = d_keys
    d_qkv_ref[3 * head :] = jnp.transpose(d_value)
    wait(copies)
    for tile in range(4):
        lanes = slice(tile * 2 * count, (tile + 1) * 2 * count)
        d_qkv = jnp.transpose(d_qkv_ref[:, lanes]).astype(BF16)
        d_low_ref[lanes] = d_qkv
        d_first = mm_t(d_qkv, w_qkv[...])
        d_first_ref[order[2 * tile]] = d_first[:count].astype(BF16)
        d_first_ref[order[2 * tile + 1]] = d_first[count:].astype(BF16)


def attend_weights(*refs):
    pieces, d_pieces, own, other, w_whole = refs[:8], refs[8:16], *refs[16:19]
    d_low, attn_gain, ffn_part, q_part, k_part = refs[19:24]
    out_ref, x_ref, d_ref, mixed_ref, d_low_ref, w_qkv, sems = refs[24:]
    count = pieces[0].shape[0]
    width = d_low_ref.shape[1]
    mixed = []
    for i in range(4):
        mixed += [(own.at[i], mixed_ref.at[pl.ds(2 * i * count, count)])]
        mixed += [(other.at[i], mixed_ref.at[pl.ds((2 * i + 1) * count, count)])]
    copies = fetch([(d_low, d_low_ref), *rows_of(pieces, x_ref), (w_whole, w_qkv)], sems)
    more = fetch([*mixed, *rows_of(d_pieces, d_ref)], sems, len(copies))
    wait(copies)
    grad_qkv = outer_sum(d_low_ref[...], x_ref[...])
    attn_part = jnp.sum(grad_qkv * jnp.transpose(w_qkv[...].astype(F32)), axis=0, keepdims=True) / attn_gain[...]
    grad_qkv = jnp.transpose(grad_qkv).astype(BF16)
    wait(more)
    grad_out = jnp.transpose(outer_sum(mixed_ref[...], d_ref[...])).astype(BF16)
    lines = [part[:, i * 128 : (i + 1) * 128] for part in (attn_part, ffn_part[...]) for i in range(8)]
    lines.append(jnp.concatenate([jnp.transpose(q_part[...]), jnp.transpose(k_part[...])], axis=1))
    gains = jnp.concatenate(lines + [jnp.zeros((7, 128), F32)], axis=0)
    high = gains.astype(BF16)
    low = (gains - high.astype(F32)).astype(BF16)
    gains = jnp.concatenate([high, low, jnp.zeros((count - 48, 128), BF16)], axis=0)
    for i in range(8):
        rows = slice(i * count, (i + 1) * count)
        out_ref[i, :, :width] = grad_qkv[rows]
        out_ref[i, :, width : width + 128] = gains
        out_ref[i, :, width + 128 :] = grad_out[rows]


def ffn(*refs):
    order, seconds, cots, weights = refs[0], refs[1:9], refs[9], refs[10]
    hidden_ref, d_ffn_ref, block_ref, d_send = refs[11:15]
    d_mine, (x_ref, cot_ref, w_ref, sems) = refs[15:19], refs[19:]
    copies = fetch([(weights, w_ref)], sems)
    loads = rows_of(seconds, x_ref) + rows_of([cots.at[order[i]] for i in range(8)], cot_ref)
    loads = fetch([loads[8 * j + 2 * g + i] for g in (3, 1, 2, 0) for j in (0, 1) for i in (0, 1)], sems, 1)
    wait(copies)
    width = hidden_ref.shape[1]
    count = seconds[0].shape[0]
    for group in (3, 1, 2, 0):
        rows = slice(2 * group * count, 2 * (group + 1) * count)
        wait(loads[:4])
        loads = loads[4:]
        x, cot = x_ref[rows], cot_ref[rows]
        both = mm(x, w_ref[:, : 2 * width])
        gate, up = both[:, :width], both[:, width:]
        sigmoid = 1.0 / (1.0 + jnp.exp(-gate))
        act = gate * sigmoid
        hidden = (act * up).astype(BF16)
        hidden_ref[rows] = hidden
        d_hidden = mm(cot, w_ref[:, 2 * width :])
        d_gate = d_hidden * up * sigmoid * (1.0 + gate * (1.0 - sigmoid))
        d_ffn = jnp.concatenate([d_gate, d_hidden * act], axis=1).astype(BF16)
        d_ffn_ref[rows] = d_ffn
        d_second = mm_t(d_ffn, w_ref[:, : 2 * width])
        d_mine[group][...] = d_second[:count]
        d_send[group] = d_second[count:].astype(BF16)
        out = mm_t(hidden, w_ref[:, 2 * width :])
        block_ref[order[2 * group]] = out[:count].astype(BF16)
        block_ref[order[2 * group + 1]] = out[count:].astype(BF16)


def ffn_weights(*refs):
    order, seconds, cots, hidden, d_ffn = refs[0], refs[1:9], *refs[9:12]
    out_ref, x_ref, cot_ref, hidden_ref, d_ffn_ref, sems = refs[12:]
    count = seconds[0].shape[0]
    copies = fetch([(d_ffn, d_ffn_ref), *rows_of(seconds, x_ref)], sems)
    more = fetch([(hidden, hidden_ref), *rows_of([cots.at[order[i]] for i in range(8)], cot_ref)], sems, 9)
    for left_ref, right_ref, columns in ((x_ref, d_ffn_ref, 0), (cot_ref, hidden_ref, d_ffn_ref.shape[1])):
        wait(more if columns else copies)
        width = right_ref.shape[1]
        for pair in range(4):
            both = outer_sum(left_ref[:, 2 * pair * count : 2 * (pair + 1) * count], right_ref[...]).astype(BF16)
            out_ref[2 * pair, :, columns : columns + width] = both[:count]
            out_ref[2 * pair + 1, :, columns : columns + width] = both[count:]
    used = d_ffn_ref.shape[1] + hidden_ref.shape[1]
    out_ref[:, :, used:] = jnp.zeros((8, count, out_ref.shape[2] - used), BF16)


def sum_ffn(parts, gate_up_ref, down_ref):
    width = gate_up_ref.shape[1]
    total = sum(parts[i].astype(F32) for i in range(8)).astype(BF16)
    gate_up_ref[...] = total[:, :width]
    down_ref[...] = total[:, width : width + down_ref.shape[1]]


def sum_attn(parts, first_ref, out_ref):
    count = out_ref.shape[0]
    width = first_ref.shape[1] - 128
    total = sum(parts[i].astype(F32) for i in range(8))
    first_ref[:, :width] = total[:, :width].astype(BF16)
    pack_gains(first_ref, width, total[:24, width : width + 128] + total[24:48, width : width + 128])
    out_ref[...] = total[:, width + 128 :].astype(BF16)


def pack_gains(ref, width, gains):
    high = gains.astype(BF16)
    low = (gains - high.astype(F32)).astype(BF16)
    rest = jnp.zeros((ref.shape[0] - 48, 128), BF16)
    ref[:, width : width + 128] = jnp.concatenate([high, low, rest], axis=0)


def join_ffn(own, other, down, down_other, out_ref):
    width = own.shape[1]
    out_ref[:, :width] = (own[...].astype(F32) + other[...].astype(F32)).astype(BF16)
    out_ref[:, width:] = (down[...].astype(F32) + down_other[...].astype(F32)).astype(BF16)


def join_attn(own, other, out, out_other, out_ref):
    width = own.shape[1] - 128
    total = own[...].astype(F32) + other[...].astype(F32)
    out_ref[:, :width] = total[:, :width].astype(BF16)
    pack_gains(out_ref, width, total[:24, width:] + total[24:48, width:])
    out_ref[:, width + 128 :] = (out[...].astype(F32) + out_other[...].astype(F32)).astype(BF16)


def assemble_ffn(*refs):
    order, pieces, (gate_ref, up_ref, down_ref, held, sems) = refs[0], refs[1:9], refs[9:]
    width = down_ref.shape[0]
    count = pieces[0].shape[0]
    wait(fetch([(pieces[i], held.at[order[i]]) for i in range(8)], sems))
    for owner in range(8):
        columns = slice(owner * width, (owner + 1) * width)
        gate_ref[:, columns] = held[owner, :, :width].astype(F32)
        up_ref[:, columns] = held[owner, :, width : 2 * width].astype(F32)
        down = held[owner, :, 2 * width :].astype(F32)
        down_ref[:, owner * count : (owner + 1) * count] = jnp.transpose(down)


def assemble_attn(*refs):
    order, pieces, (query_ref, key_ref, value_ref, out_ref, gains_ref, held, sems) = refs[0], refs[1:9], refs[9:]
    count = pieces[0].shape[0]
    half = count // 2
    wait(fetch([(pieces[i], held.at[order[i]]) for i in range(8)], sems))
    gains = jnp.zeros(gains_ref.shape, F32)
    for owner in range(8):
        columns = slice(owner * count, (owner + 1) * count)
        narrow = slice(owner * half, (owner + 1) * half)
        part = held[owner].astype(F32)
        query_ref[:, columns] = part[:, :count]
        key_ref[:, narrow] = part[:, count : count + half]
        value_ref[:, narrow] = part[:, count + half : 2 * count]
        out_ref[:, columns] = jnp.transpose(part[:, 3 * count :])
        gains += part[:24, 2 * count : 3 * count] + part[24:48, 2 * count : 3 * count]
    gains_ref[...] = gains


def body(
    hidden_in,
    positions,
    cotangent,
    attn_gain,
    w_query,
    w_key,
    w_value,
    query_gain,
    key_gain,
    w_out,
    ffn_gain,
    w_gate,
    w_up,
    w_down,
):
    ctx = lax.axis_index("ctx")
    tokens = hidden_in[0].astype(F32)
    count, width = tokens.shape
    head_size = query_gain.shape[0]
    q_width = w_query.shape[1] // 8
    k_width = w_key.shape[1] // 8
    ff_width = w_gate.shape[1] // 8

    z_index, core = ctx // 2, ctx % 2
    owners = jnp.stack(
        [((z_index + step) % 4) * 2 + (core ^ flip) for step in STEPS for flip in (0, 1)]
    )
    places = positions[0].reshape(8, count)[owners].reshape(8 * count)
    length = 8 * count
    cosine_table, sine_table = rope_tables(places, head_size)
    column = jnp.broadcast_to(places[:, None], (length, 2 * count))
    row = places[None]
    gains = (query_gain[:, None], key_gain[:, None])
    tables = (cosine_table, sine_table, column, row)
    block = shape((count, q_width), BF16)
    low_rows, rows = shape((count, width), BF16), shape((count, width), F32)
    qkv_width = q_width + 2 * k_width

    place = jnp.stack([lax.axis_index("fsdp") // 2, lax.axis_index("fsdp") % 2])
    wide, head_rows = pltpu.VMEM((length, width), BF16), pltpu.VMEM((length, qkv_width), BF16)

    first_scale = rms_scale(tokens)
    first_hat = tokens * first_scale
    first_normed = (first_hat * attn_gain).astype(BF16)
    first_moved = move_pieces(first_normed)
    qkv_block = jnp.concatenate(
        [own_columns(w_query, q_width, ctx), own_columns(w_key, k_width, ctx), own_columns(w_value, k_width, ctx)],
        axis=1,
    )
    w_qkv = all_to_all(jnp.broadcast_to(qkv_block[None], (8, *qkv_block.shape)), "fsdp").reshape(width, qkv_width)
    out_pair = pair_x(w_out)
    cot = cotangent[0]
    cot_copies = jnp.broadcast_to(cot[None], (8, count, width))
    down_chunk = transpose_mesh(jnp.transpose(own_columns(w_down, width // 8, ctx)))
    ffn_block = jnp.concatenate(
        [own_columns(w_gate, ff_width, ctx), own_columns(w_up, ff_width, ctx), down_chunk], axis=1
    )
    ffn_block, w_qkv, first_moved, cot_copies = stage(ffn_block, w_qkv, first_moved, cot_copies)
    ffn_rows = lax.all_gather(ffn_block, "fsdp", axis=0, tiled=True)
    cots = all_to_all(cot_copies, "ctx")
    first_pieces = swap_pieces(first_moved)
    first_pieces, w_qkv, tables, out_pair = stage(first_pieces, w_qkv, tables, out_pair)

    out_pairs = spread_y(out_pair)
    qkv, lse, own, other = call(
        attend_forward,
        [shape((qkv_width, length), F32), shape((8, length), F32)] + [shape((4, count, q_width), BF16)] * 2,
        (),
        (*first_pieces, w_qkv),
        (*tables, *gains),
        4 * 10**9,
        [wide, pltpu.VMEM((width, qkv_width), BF16)],
        9,
    )

    mixed_blocks = exchange_ctx(own, other)
    mixed_blocks, out_pairs, cots = stage(mixed_blocks, out_pairs, cots)
    square = pltpu.VMEM((width, width), BF16)
    residual, second_normed = call(
        out_project,
        [rows, low_rows],
        (place, owners),
        out_pairs,
        (*mixed_blocks, hidden_in[0], ffn_gain[None]),
        3 * 10**8,
        [square, pltpu.VMEM((count, width), BF16)],
        4,
    )

    second_pieces = gather_ctx(second_normed)
    hidden_shape, d_ffn_shape = shape((length, ff_width), BF16), shape((length, 2 * ff_width), BF16)
    hidden, d_ffn, block_parts, d_send, *d_mine = call(
        ffn,
        [hidden_shape, d_ffn_shape, shape((8, count, width), BF16), shape((4, count, width), BF16)] + [rows] * 4,
        (owners,),
        (*second_pieces, cots, ffn_rows),
        (),
        8 * 10**9,
        [wide, wide, pltpu.VMEM((width, 3 * ff_width), BF16)],
        17,
    )

    d_moves = start_scatter_ctx(d_mine, swap_core(d_send))
    padded = -(-3 * ff_width // 128) * 128
    (ffn_partial,) = call(
        ffn_weights,
        [shape((8, count, padded), BF16)],
        (owners,),
        (*second_pieces, cots, hidden, d_ffn),
        (),
        4 * 10**9,
        [wide, wide, pltpu.VMEM((length, ff_width), BF16), pltpu.VMEM((length, 2 * ff_width), BF16)],
        18,
    )
    ffn_sums = all_to_all(ffn_partial, "fsdp")
    d_moves, _ = stage(d_moves, ffn_partial)
    block_sum = lax.psum_scatter(block_parts, "ctx", scatter_dimension=0, tiled=False)
    block_out = (residual + block_sum.astype(F32)).astype(BF16)
    d_resid, d_attn, ffn_gain_part, *d_blocks = call(
        resid_backward,
        [rows, low_rows, shape((1, width), F32)] + [shape((4, count, q_width), BF16)] * 2,
        (place, owners),
        out_pairs,
        (*d_moves, residual, cot, ffn_gain[None]),
        3 * 10**8,
        [square, pltpu.VMEM((count, width), BF16)],
        4,
    )

    d_blocks = exchange_ctx(*d_blocks)
    d_blocks, d_attn = stage(d_blocks, d_attn)

    d_moved = move_pieces(d_attn)
    q_gain_part, k_gain_part, d_qkv, d_first_parts = call(
        attend_backward,
        [
            shape((head_size, 1), F32),
            shape((head_size, 1), F32),
            shape((length, qkv_width), BF16),
            shape((8, count, width), BF16),
        ],
        (owners,),
        (w_qkv,),
        (*d_blocks, *tables, *gains, qkv, lse),
        8 * 10**9,
        [pltpu.VMEM((qkv_width, length), F32), pltpu.VMEM((width, qkv_width), BF16)],
        1,
    )
    d_qkv, d_first_parts, d_moved = stage(d_qkv, d_first_parts, d_moved)
    d_pieces = swap_pieces(d_moved)
    half, down = call(
        sum_ffn, [shape((count, 2 * ff_width), BF16), shape((count, ff_width), BF16)], (), (), (ffn_sums,), 10**6
    )
    d_qkv, d_pieces, half, down = stage(d_qkv, d_pieces, half, down)
    ffn_steps = (half, swap_dp(half), transpose_mesh(down), transpose_mesh(down, 1))
    d_first = lax.psum_scatter(d_first_parts, "ctx", scatter_dimension=0, tiled=False).astype(F32)
    (attn_partial,) = call(
        attend_weights,
        [shape((8, count, qkv_width + 128 + q_width), BF16)],
        (),
        (*first_pieces, *d_pieces, own, other, w_qkv, d_qkv),
        (attn_gain[None], ffn_gain_part, q_gain_part, k_gain_part),
        10**9,
        [wide, wide, pltpu.VMEM((length, q_width), BF16), head_rows, pltpu.VMEM((width, qkv_width), BF16)],
        26,
    )
    (joined,) = call(join_ffn, [shape((count, 3 * ff_width), BF16)], (), (), ffn_steps, 10**6)
    attn_partial, joined = stage(attn_partial, joined)

    ffn_moved = move_pieces(joined)
    attn_sums = all_to_all(attn_partial, "fsdp")
    d_from_first, _ = norm_back(d_first, first_hat, first_scale, attn_gain)
    grad_in = (d_resid + d_from_first).astype(BF16)
    attn_sums, ffn_moved, grad_in, block_out = stage(attn_sums, ffn_moved, grad_in, block_out)
    half, out = call(
        sum_attn, [shape((count, qkv_width + 128), BF16), shape((count, q_width), BF16)], (), (), (attn_sums,), 10**6
    )
    attn_steps = (half, swap_dp(half), transpose_mesh(out), transpose_mesh(out, 1))
    (joined,) = call(
        join_attn, [shape((count, qkv_width + 128 + q_width), BF16)], (), (), attn_steps, 10**6
    )
    attn_moved = move_pieces(joined)
    grads_ffn = call(
        assemble_ffn,
        [shape((count, 8 * ff_width), F32)] * 2 + [shape((ff_width, width), F32)],
        (owners,),
        swap_pieces(ffn_moved),
        (),
        10**6,
        [pltpu.VMEM((8, count, 3 * ff_width), BF16)],
        8,
    )
    attn_moved, grads_ffn = stage(attn_moved, grads_ffn)
    grad_gate, grad_up, grad_down = grads_ffn
    grad_query, grad_key, grad_value, grad_out, totals = call(
        assemble_attn,
        [shape((count, width), F32)]
        + [shape((count, 8 * k_width), F32)] * 2
        + [shape((q_width, width), F32), shape((24, 128), F32)],
        (owners,),
        swap_pieces(attn_moved),
        (),
        10**6,
        [pltpu.VMEM((8, count, qkv_width + 128 + q_width), BF16)],
        8,
    )
    totals = totals.reshape(-1)
    grad_attn_gain = totals[:width]
    grad_ffn_gain = totals[width : 2 * width]
    grad_query_gain = totals[2 * width : 2 * width + head_size]
    grad_key_gain = totals[2 * width + head_size : 2 * width + 2 * head_size]
    return (
        block_out[None],
        grad_in[None],
        grad_attn_gain,
        grad_query,
        grad_key,
        grad_value,
        grad_query_gain,
        grad_key_gain,
        grad_out,
        grad_ffn_gain,
        grad_gate,
        grad_up,
        grad_down,
    )


def solution(mesh):
    in_specs = (
        P(("dp", "fsdp"), "ctx", None),
        P(("dp", "fsdp"), None),
        P(("dp", "fsdp"), "ctx", None),
        P(),
        P("fsdp", None),
        P("fsdp", None),
        P("fsdp", None),
        P(),
        P(),
        P("fsdp", None),
        P(),
        P("fsdp", None),
        P("fsdp", None),
        P("fsdp", None),
    )
    out_specs = (
        P(("dp", "fsdp"), "ctx", None),
        P(("dp", "fsdp"), "ctx", None),
        P(),
        P("fsdp", None),
        P("fsdp", None),
        P("fsdp", None),
        P(),
        P(),
        P("fsdp", None),
        P(),
        P("fsdp", None),
        P("fsdp", None),
        P("fsdp", None),
    )
    return jax.shard_map(body, mesh=mesh, in_specs=in_specs, out_specs=out_specs, check_vma=False)
```

```python
import math

import jax
import jax.numpy as jnp
from jax import lax
from jax.experimental import pallas as pl
from jax.experimental.pallas import tpu as pltpu
from jax.sharding import PartitionSpec as P

NORM_EPSILON = 1e-05
ROPE_BASE = 1000000.0
MASKED_SCORE = -1e30
BF16 = jnp.bfloat16
F32 = jnp.float32
STEPS = (0, -1, 1, 2)


def rms_scale(values):
    return lax.rsqrt(jnp.mean(values * values, axis=-1, keepdims=True) + NORM_EPSILON)


def rope_tables(places, head_size):
    half_width = head_size // 2
    pair_index = jnp.arange(half_width, dtype=F32)
    frequency = ROPE_BASE ** (-2.0 * pair_index / head_size)
    angles = frequency[:, None] * places.astype(F32)[None, :]
    return jnp.cos(angles), jnp.sin(angles)


def call(kernel, out_shapes, scalars, fetched, args, flops, scratch=(), copies=0):
    vmem = pl.BlockSpec(memory_space=pltpu.VMEM)
    operands = (*scalars, *fetched, *args)
    out_bytes = sum(math.prod(o.shape) * o.dtype.itemsize for o in out_shapes)
    in_bytes = sum(math.prod(a.shape) * a.dtype.itemsize for a in operands)
    return pl.pallas_call(
        kernel,
        out_shape=out_shapes,
        in_specs=[pl.BlockSpec(memory_space=pltpu.SMEM)] * len(scalars)
        + [pl.BlockSpec(memory_space=pl.ANY)] * len(fetched)
        + [vmem] * len(args),
        out_specs=[vmem] * len(out_shapes),
        scratch_shapes=list(scratch) + ([pltpu.SemaphoreType.DMA((copies,))] if copies else []),
        compiler_params=pltpu.CompilerParams(vmem_limit_bytes=60 * 2**20),
        cost_estimate=pl.CostEstimate(flops=flops, bytes_accessed=in_bytes + out_bytes, transcendentals=0),
    )(*operands)


def shape(dims, kind):
    return jax.ShapeDtypeStruct(dims, kind)


def head_forward(values, gain, cosine, sine):
    scale = lax.rsqrt(jnp.mean(values * values, axis=0, keepdims=True) + NORM_EPSILON)
    hat = values * scale
    normed = hat * gain
    half = values.shape[0] // 2
    front, back = normed[:half], normed[half:]
    rotated = jnp.concatenate([front * cosine - back * sine, back * cosine + front * sine], axis=0)
    return scale, hat, rotated


def head_backward(grads, hat, scale, gain, cosine, sine):
    half = grads.shape[0] // 2
    front, back = grads[:half], grads[half:]
    d_normed = jnp.concatenate([front * cosine + back * sine, back * cosine - front * sine], axis=0)
    scaled = d_normed * gain
    inner = jnp.mean(hat * scaled, axis=0, keepdims=True)
    return scale * (scaled - hat * inner), jnp.sum(d_normed * hat, axis=1, keepdims=True)


def norm_back(d_normed, normed_hat, scale_values, gain_vector):
    scaled = d_normed * gain_vector
    inner = jnp.mean(normed_hat * scaled, axis=-1, keepdims=True)
    return (scale_values * (scaled - normed_hat * inner), d_normed * normed_hat)


def mm(left, right):
    return jnp.dot(left, right, preferred_element_type=F32)


def mm_t(left, right):
    return lax.dot_general(left, right, (((1,), (1,)), ((), ())), preferred_element_type=F32)


def outer_sum(left, right):
    return lax.dot_general(left, right, (((0,), (0,)), ((), ())), preferred_element_type=F32)


def swap_core(value):
    return lax.ppermute(value, "ctx", [(i, i ^ 1) for i in range(8)])


def move_z(value, step):
    return lax.ppermute(value, "ctx", [(i, (i + 2 * step) % 8) for i in range(8)])


def move_pieces(block):
    return [move_z(block, -step) if step else block for step in STEPS]


def swap_pieces(moved):
    pieces = []
    for piece in moved:
        pieces += [piece, swap_core(piece)]
    return pieces


def gather_ctx(block):
    return swap_pieces(move_pieces(block))


def start_scatter_ctx(mine, received):
    sums = [own + other.astype(F32) for own, other in zip(mine, received)]
    return [sums[0]] + [move_z(sums[slot].astype(BF16), STEPS[slot]) for slot in (3, 1, 2)]


def exchange_ctx(own, other):
    other = swap_core(other)
    out = [None] * 4
    for i, step in enumerate(STEPS):
        both = jnp.stack([own[i], other[i]])
        out[(0, 2, 1, 3)[i]] = move_z(both, step) if step else both
    return out


def stage(*values):
    return lax.optimization_barrier(values)


def transpose_mesh(value, flip=0):
    pairs = [
        ((d * 8 + c) * 8 + f, ((d ^ flip) * 8 + f) * 8 + c) for d in range(2) for c in range(8) for f in range(8)
    ]
    return lax.ppermute(value, ("dp", "ctx", "fsdp"), pairs)


def swap_dp(value):
    return lax.ppermute(value, "dp", [(0, 1), (1, 0)])


def move_y(value, step, flip=0):
    pairs = [(y * 2 + x, (y + step) % 4 * 2 + (x ^ flip)) for y in range(4) for x in range(2)]
    return lax.ppermute(value, "fsdp", pairs)


def pair_x(block):
    other = move_y(block, 0, 1)
    first = lax.axis_index("fsdp") % 2 == 0
    return jnp.concatenate([jnp.where(first, block, other), jnp.where(first, other, block)], axis=0)


def spread_y(pair):
    return [pair] + [move_y(pair, step) for step in (1, 3, 2)]


def fetch(pairs, sems, first=0):
    copies = [pltpu.make_async_copy(src, dst, sems.at[first + i]) for i, (src, dst) in enumerate(pairs)]
    for copy in copies:
        copy.start()
    return copies


def rows_of(pieces, ref):
    count = pieces[0].shape[0]
    return [(piece, ref.at[pl.ds(i * count, count)]) for i, piece in enumerate(pieces)]


def joined_y(place, pairs, ref):
    rows = pairs[0].shape[0]
    owners = [(place[0] + 4 - step) % 4 for step in (0, 1, 3, 2)]
    return [(pair, ref.at[pl.ds(pl.multiple_of(y * rows, rows), rows)]) for y, pair in zip(owners, pairs)]


def wait(copies):
    for copy in copies:
        copy.wait()


def all_to_all(blocks, axis):
    return lax.all_to_all(blocks, axis, split_axis=0, concat_axis=0, tiled=True)


def own_columns(weight, width, index):
    return lax.dynamic_slice_in_dim(weight, index * width, width, 1)


def attend_forward(*refs):
    pieces, w_whole, refs = refs[:8], refs[8], refs[9:]
    cos_ref, sin_ref, column_ref, row_ref, q_gain, k_gain = refs[:6]
    qkv_ref, lse_ref, own_ref, other_ref, x_ref, w_qkv, sems = refs[6:]
    w_copies = fetch([(w_whole, w_qkv)], sems, 8)
    x_copies = fetch(rows_of(pieces, x_ref), sems)
    wait(w_copies)
    length = qkv_ref.shape[1]
    count = length // 8
    head = q_gain.shape[0]
    for pair in range(4):
        wait(x_copies[2 * pair : 2 * pair + 2])
        lanes = slice(pair * 2 * count, (pair + 1) * 2 * count)
        qkv_ref[:, lanes] = jnp.transpose(mm(x_ref[lanes], w_qkv[...]))
    cosine, sine = cos_ref[...], sin_ref[...]
    queries = [
        head_forward(qkv_ref[h * head : (h + 1) * head], q_gain[...], cosine, sine)[2].astype(BF16) * BF16(head**-0.5)
        for h in range(2)
    ]
    key = jnp.transpose(head_forward(qkv_ref[2 * head : 3 * head], k_gain[...], cosine, sine)[2]).astype(BF16)
    value = qkv_ref[3 * head :].astype(BF16)
    width = column_ref.shape[1]
    for tile in range(length // width):
        lanes = slice(tile * width, (tile + 1) * width)
        allowed = column_ref[...] <= row_ref[:, lanes]
        outs = []
        for h in range(2):
            scores = jnp.where(allowed, mm(key, queries[h][:, lanes]), MASKED_SCORE)
            top = jnp.max(scores, axis=0, keepdims=True)
            weights = jnp.exp(scores - top)
            total = jnp.sum(weights, axis=0, keepdims=True)
            lse_ref[h : h + 1, lanes] = top + jnp.log(total)
            outs.append(mm(value, (weights * (1.0 / total)).astype(BF16)))
        mixed = jnp.transpose(jnp.concatenate(outs, axis=0)).astype(BF16)
        own_ref[tile] = mixed[:count]
        other_ref[tile] = mixed[count:]


def out_project(place, order, *refs):
    out_pairs, blocks, (tokens, gain, resid_ref, normed_ref, w_out, mixed_ref, sems) = refs[:4], refs[4:8], refs[8:]
    copies = fetch(joined_y(place, out_pairs, w_out), sems)
    count = blocks[0].shape[2]
    for i in range(8):
        lanes = pl.ds(pl.multiple_of(order[i] * count, count), count)
        mixed_ref[:, lanes] = blocks[i // 2][i % 2]
    wait(copies)
    resid = tokens[...].astype(F32) + mm(mixed_ref[...], w_out[...])
    resid_ref[...] = resid
    normed_ref[...] = (resid * rms_scale(resid) * gain[...]).astype(BF16)


def resid_backward(place, order, *refs):
    out_pairs, refs = refs[:4], refs[4:]
    total, move_a, move_b, move_c, resid_ref, cot_ref, gain_ref = refs[:7]
    d_resid_ref, d_attn_ref, gain_part_ref, own_ref, other_ref, w_out, d_mixed_ref, sems = refs[7:]
    copies = fetch(joined_y(place, out_pairs, w_out), sems)
    d_second = total[...] + move_a[...].astype(F32) + move_b[...].astype(F32) + move_c[...].astype(F32)
    resid = resid_ref[...]
    scale = rms_scale(resid)
    d_from, gain_part = norm_back(d_second, resid * scale, scale, gain_ref[...])
    gain_part_ref[...] = jnp.sum(gain_part, axis=0, keepdims=True)
    d_resid = cot_ref[...].astype(F32) + d_from
    d_resid_ref[...] = d_resid
    d_attn = d_resid.astype(BF16)
    d_attn_ref[...] = d_attn
    wait(copies)
    d_mixed_ref[...] = mm_t(d_attn, w_out[...]).astype(BF16)
    count = own_ref.shape[2]
    for i in range(8):
        lanes = pl.ds(pl.multiple_of(order[i] * count, count), count)
        (own_ref, other_ref)[i % 2][i // 2] = d_mixed_ref[:, lanes]


def attend_backward(*refs):
    order, w_whole, d_blocks, refs = refs[0], refs[1], refs[2:6], refs[6:]
    cos_ref, sin_ref, column_ref, row_ref, q_gain, k_gain, qkv_ref, lse_ref = refs[:8]
    q_gain_ref, k_gain_ref, d_low_ref, d_first_ref, d_qkv_ref, w_qkv, sems = refs[8:]
    copies = fetch([(w_whole, w_qkv)], sems)
    length = qkv_ref.shape[1]
    head = q_gain.shape[0]
    count = length // 8
    cosine, sine = cos_ref[...], sin_ref[...]
    scales, hats, queries = [], [], []
    for h in range(2):
        scale, hat, rotated = head_forward(qkv_ref[h * head : (h + 1) * head], q_gain[...], cosine, sine)
        scales.append(scale)
        hats.append(hat)
        queries.append(rotated.astype(BF16) * BF16(head**-0.5))
    k_scale, k_hat, rotated = head_forward(qkv_ref[2 * head : 3 * head], k_gain[...], cosine, sine)
    key_rows = rotated.astype(BF16)
    key = jnp.transpose(rotated).astype(BF16)
    value = jnp.transpose(qkv_ref[3 * head :]).astype(BF16)
    width = column_ref.shape[1]
    d_key = jnp.zeros((length, head), F32)
    d_value = jnp.zeros((length, head), F32)
    for tile in range(length // width):
        lanes = slice(tile * width, (tile + 1) * width)
        allowed = column_ref[...] <= row_ref[:, lanes]
        d_mixed = jnp.concatenate([d_blocks[tile][0], d_blocks[tile][1]], axis=0)
        d_mixed = jnp.transpose(d_mixed.astype(F32)).astype(BF16)
        for h in range(2):
            rows = slice(h * head, (h + 1) * head)
            query = queries[h][:, lanes]
            probs = jnp.where(allowed, jnp.exp(mm(key, query) - lse_ref[h : h + 1, lanes]), 0.0)
            d_probs = mm(value, d_mixed[rows])
            inner = jnp.sum(probs * d_probs, axis=0, keepdims=True)
            d_scores = (probs * (d_probs - inner)).astype(BF16)
            d_value += mm_t(probs.astype(BF16), d_mixed[rows])
            d_key += mm_t(d_scores, query)
            d_qkv_ref[rows, lanes] = mm(key_rows, d_scores) * head**-0.5
    for h in range(2):
        rows = slice(h * head, (h + 1) * head)
        d_query, gain_part = head_backward(d_qkv_ref[rows], hats[h], scales[h], q_gain[...], cosine, sine)
        d_qkv_ref[rows] = d_query
        if h == 0:
            q_gain_ref[...] = gain_part
        else:
            q_gain_ref[...] += gain_part
    d_keys, gain_part = head_backward(jnp.transpose(d_key), k_hat, k_scale, k_gain[...], cosine, sine)
    k_gain_ref[...] = gain_part
    d_qkv_ref[2 * head : 3 * head] = d_keys
    d_qkv_ref[3 * head :] = jnp.transpose(d_value)
    wait(copies)
    for tile in range(4):
        lanes = slice(tile * 2 * count, (tile + 1) * 2 * count)
        d_qkv = jnp.transpose(d_qkv_ref[:, lanes]).astype(BF16)
        d_low_ref[lanes] = d_qkv
        d_first = mm_t(d_qkv, w_qkv[...])
        d_first_ref[order[2 * tile]] = d_first[:count].astype(BF16)
        d_first_ref[order[2 * tile + 1]] = d_first[count:].astype(BF16)


def attend_weights(*refs):
    pieces, d_pieces, own, other, w_whole = refs[:8], refs[8:16], *refs[16:19]
    d_low, attn_gain, ffn_part, q_part, k_part = refs[19:24]
    out_ref, x_ref, d_ref, mixed_ref, d_low_ref, w_qkv, sems = refs[24:]
    count = pieces[0].shape[0]
    width = d_low_ref.shape[1]
    mixed = []
    for i in range(4):
        mixed += [(own.at[i], mixed_ref.at[pl.ds(2 * i * count, count)])]
        mixed += [(other.at[i], mixed_ref.at[pl.ds((2 * i + 1) * count, count)])]
    copies = fetch([(d_low, d_low_ref), *rows_of(pieces, x_ref), (w_whole, w_qkv)], sems)
    more = fetch([*mixed, *rows_of(d_pieces, d_ref)], sems, len(copies))
    wait(copies)
    grad_qkv = outer_sum(d_low_ref[...], x_ref[...])
    attn_part = jnp.sum(grad_qkv * jnp.transpose(w_qkv[...].astype(F32)), axis=0, keepdims=True) / attn_gain[...]
    grad_qkv = jnp.transpose(grad_qkv).astype(BF16)
    wait(more)
    grad_out = jnp.transpose(outer_sum(mixed_ref[...], d_ref[...])).astype(BF16)
    lines = [part[:, i * 128 : (i + 1) * 128] for part in (attn_part, ffn_part[...]) for i in range(8)]
    lines.append(jnp.concatenate([jnp.transpose(q_part[...]), jnp.transpose(k_part[...])], axis=1))
    gains = jnp.concatenate(lines + [jnp.zeros((7, 128), F32)], axis=0)
    high = gains.astype(BF16)
    low = (gains - high.astype(F32)).astype(BF16)
    gains = jnp.concatenate([high, low, jnp.zeros((count - 48, 128), BF16)], axis=0)
    for i in range(8):
        rows = slice(i * count, (i + 1) * count)
        out_ref[i, :, :width] = grad_qkv[rows]
        out_ref[i, :, width : width + 128] = gains
        out_ref[i, :, width + 128 :] = grad_out[rows]


def ffn(*refs):
    order, seconds, cots, weights = refs[0], refs[1:9], refs[9], refs[10]
    hidden_ref, d_ffn_ref, block_ref, d_send = refs[11:15]
    d_mine, (x_ref, cot_ref, w_ref, sems) = refs[15:19], refs[19:]
    copies = fetch([(weights, w_ref)], sems)
    loads = rows_of(seconds, x_ref) + rows_of([cots.at[order[i]] for i in range(8)], cot_ref)
    loads = fetch([loads[8 * j + 2 * g + i] for g in (3, 1, 2, 0) for j in (0, 1) for i in (0, 1)], sems, 1)
    wait(copies)
    width = hidden_ref.shape[1]
    count = seconds[0].shape[0]
    for group in (3, 1, 2, 0):
        rows = slice(2 * group * count, 2 * (group + 1) * count)
        wait(loads[:4])
        loads = loads[4:]
        x, cot = x_ref[rows], cot_ref[rows]
        both = mm(x, w_ref[:, : 2 * width])
        gate, up = both[:, :width], both[:, width:]
        sigmoid = 1.0 / (1.0 + jnp.exp(-gate))
        act = gate * sigmoid
        hidden = (act * up).astype(BF16)
        hidden_ref[rows] = hidden
        d_hidden = mm(cot, w_ref[:, 2 * width :])
        d_gate = d_hidden * up * sigmoid * (1.0 + gate * (1.0 - sigmoid))
        d_ffn = jnp.concatenate([d_gate, d_hidden * act], axis=1).astype(BF16)
        d_ffn_ref[rows] = d_ffn
        d_second = mm_t(d_ffn, w_ref[:, : 2 * width])
        d_mine[group][...] = d_second[:count]
        d_send[group] = d_second[count:].astype(BF16)
        out = mm_t(hidden, w_ref[:, 2 * width :])
        block_ref[order[2 * group]] = out[:count].astype(BF16)
        block_ref[order[2 * group + 1]] = out[count:].astype(BF16)


def ffn_weights(*refs):
    order, seconds, cots, hidden, d_ffn = refs[0], refs[1:9], *refs[9:12]
    out_ref, x_ref, cot_ref, hidden_ref, d_ffn_ref, sems = refs[12:]
    count = seconds[0].shape[0]
    copies = fetch([(d_ffn, d_ffn_ref), *rows_of(seconds, x_ref)], sems)
    more = fetch([(hidden, hidden_ref), *rows_of([cots.at[order[i]] for i in range(8)], cot_ref)], sems, 9)
    for left_ref, right_ref, columns in ((x_ref, d_ffn_ref, 0), (cot_ref, hidden_ref, d_ffn_ref.shape[1])):
        wait(more if columns else copies)
        width = right_ref.shape[1]
        for pair in range(4):
            both = outer_sum(left_ref[:, 2 * pair * count : 2 * (pair + 1) * count], right_ref[...]).astype(BF16)
            out_ref[2 * pair, :, columns : columns + width] = both[:count]
            out_ref[2 * pair + 1, :, columns : columns + width] = both[count:]
    used = d_ffn_ref.shape[1] + hidden_ref.shape[1]
    out_ref[:, :, used:] = jnp.zeros((8, count, out_ref.shape[2] - used), BF16)


def sum_ffn(parts, gate_up_ref, down_ref):
    width = gate_up_ref.shape[1]
    total = sum(parts[i].astype(F32) for i in range(8)).astype(BF16)
    gate_up_ref[...] = total[:, :width]
    down_ref[...] = total[:, width : width + down_ref.shape[1]]


def sum_attn(parts, first_ref, out_ref):
    count = out_ref.shape[0]
    width = first_ref.shape[1] - 128
    total = sum(parts[i].astype(F32) for i in range(8))
    first_ref[:, :width] = total[:, :width].astype(BF16)
    pack_gains(first_ref, width, total[:24, width : width + 128] + total[24:48, width : width + 128])
    out_ref[...] = total[:, width + 128 :].astype(BF16)


def pack_gains(ref, width, gains):
    high = gains.astype(BF16)
    low = (gains - high.astype(F32)).astype(BF16)
    rest = jnp.zeros((ref.shape[0] - 48, 128), BF16)
    ref[:, width : width + 128] = jnp.concatenate([high, low, rest], axis=0)


def join_ffn(own, other, down, down_other, out_ref):
    width = own.shape[1]
    out_ref[:, :width] = (own[...].astype(F32) + other[...].astype(F32)).astype(BF16)
    out_ref[:, width:] = (down[...].astype(F32) + down_other[...].astype(F32)).astype(BF16)


def join_attn(own, other, out, out_other, out_ref):
    width = own.shape[1] - 128
    total = own[...].astype(F32) + other[...].astype(F32)
    out_ref[:, :width] = total[:, :width].astype(BF16)
    pack_gains(out_ref, width, total[:24, width:] + total[24:48, width:])
    out_ref[:, width + 128 :] = (out[...].astype(F32) + out_other[...].astype(F32)).astype(BF16)


def assemble_ffn(*refs):
    order, pieces, (gate_ref, up_ref, down_ref, held, sems) = refs[0], refs[1:9], refs[9:]
    width = down_ref.shape[0]
    count = pieces[0].shape[0]
    wait(fetch([(pieces[i], held.at[order[i]]) for i in range(8)], sems))
    for owner in range(8):
        columns = slice(owner * width, (owner + 1) * width)
        gate_ref[:, columns] = held[owner, :, :width].astype(F32)
        up_ref[:, columns] = held[owner, :, width : 2 * width].astype(F32)
        down = held[owner, :, 2 * width :].astype(F32)
        down_ref[:, owner * count : (owner + 1) * count] = jnp.transpose(down)


def assemble_attn(*refs):
    order, pieces, (query_ref, key_ref, value_ref, out_ref, gains_ref, held, sems) = refs[0], refs[1:9], refs[9:]
    count = pieces[0].shape[0]
    half = count // 2
    wait(fetch([(pieces[i], held.at[order[i]]) for i in range(8)], sems))
    gains = jnp.zeros(gains_ref.shape, F32)
    for owner in range(8):
        columns = slice(owner * count, (owner + 1) * count)
        narrow = slice(owner * half, (owner + 1) * half)
        part = held[owner].astype(F32)
        query_ref[:, columns] = part[:, :count]
        key_ref[:, narrow] = part[:, count : count + half]
        value_ref[:, narrow] = part[:, count + half : 2 * count]
        out_ref[:, columns] = jnp.transpose(part[:, 3 * count :])
        gains += part[:24, 2 * count : 3 * count] + part[24:48, 2 * count : 3 * count]
    gains_ref[...] = gains


def body(
    hidden_in,
    positions,
    cotangent,
    attn_gain,
    w_query,
    w_key,
    w_value,
    query_gain,
    key_gain,
    w_out,
    ffn_gain,
    w_gate,
    w_up,
    w_down,
):
    ctx = lax.axis_index("ctx")
    tokens = hidden_in[0].astype(F32)
    count, width = tokens.shape
    head_size = query_gain.shape[0]
    q_width = w_query.shape[1] // 8
    k_width = w_key.shape[1] // 8
    ff_width = w_gate.shape[1] // 8

    z_index, core = ctx // 2, ctx % 2
    owners = jnp.stack(
        [((z_index + step) % 4) * 2 + (core ^ flip) for step in STEPS for flip in (0, 1)]
    )
    places = positions[0].reshape(8, count)[owners].reshape(8 * count)
    length = 8 * count
    cosine_table, sine_table = rope_tables(places, head_size)
    column = jnp.broadcast_to(places[:, None], (length, 2 * count))
    row = places[None]
    gains = (query_gain[:, None], key_gain[:, None])
    tables = (cosine_table, sine_table, column, row)
    block = shape((count, q_width), BF16)
    low_rows, rows = shape((count, width), BF16), shape((count, width), F32)
    qkv_width = q_width + 2 * k_width

    place = jnp.stack([lax.axis_index("fsdp") // 2, lax.axis_index("fsdp") % 2])
    wide, head_rows = pltpu.VMEM((length, width), BF16), pltpu.VMEM((length, qkv_width), BF16)

    first_scale = rms_scale(tokens)
    first_hat = tokens * first_scale
    first_normed = (first_hat * attn_gain).astype(BF16)
    first_moved = move_pieces(first_normed)
    qkv_block = jnp.concatenate(
        [own_columns(w_query, q_width, ctx), own_columns(w_key, k_width, ctx), own_columns(w_value, k_width, ctx)],
        axis=1,
    )
    w_qkv = all_to_all(jnp.broadcast_to(qkv_block[None], (8, *qkv_block.shape)), "fsdp").reshape(width, qkv_width)
    out_pair = pair_x(w_out)
    cot = cotangent[0]
    cot_copies = jnp.broadcast_to(cot[None], (8, count, width))
    down_chunk = transpose_mesh(jnp.transpose(own_columns(w_down, width // 8, ctx)))
    ffn_block = jnp.concatenate(
        [own_columns(w_gate, ff_width, ctx), own_columns(w_up, ff_width, ctx), down_chunk], axis=1
    )
    ffn_rows = lax.all_gather(ffn_block, "fsdp", axis=0, tiled=True)
    w_qkv, first_moved, cot_copies = stage(w_qkv, first_moved, cot_copies)
    cots = all_to_all(cot_copies, "ctx")
    first_pieces = swap_pieces(first_moved)
    first_pieces, w_qkv, tables, out_pair = stage(first_pieces, w_qkv, tables, out_pair)

    out_pairs = spread_y(out_pair)
    qkv, lse, own, other = call(
        attend_forward,
        [shape((qkv_width, length), F32), shape((8, length), F32)] + [shape((4, count, q_width), BF16)] * 2,
        (),
        (*first_pieces, w_qkv),
        (*tables, *gains),
        4 * 10**9,
        [wide, pltpu.VMEM((width, qkv_width), BF16)],
        9,
    )

    mixed_blocks = exchange_ctx(own, other)
    mixed_blocks, out_pairs, cots = stage(mixed_blocks, out_pairs, cots)
    square = pltpu.VMEM((width, width), BF16)
    residual, second_normed = call(
        out_project,
        [rows, low_rows],
        (place, owners),
        out_pairs,
        (*mixed_blocks, hidden_in[0], ffn_gain[None]),
        3 * 10**8,
        [square, pltpu.VMEM((count, width), BF16)],
        4,
    )

    second_pieces = gather_ctx(second_normed)
    hidden_shape, d_ffn_shape = shape((length, ff_width), BF16), shape((length, 2 * ff_width), BF16)
    hidden, d_ffn, block_parts, d_send, *d_mine = call(
        ffn,
        [hidden_shape, d_ffn_shape, shape((8, count, width), BF16), shape((4, count, width), BF16)] + [rows] * 4,
        (owners,),
        (*second_pieces, cots, ffn_rows),
        (),
        8 * 10**9,
        [wide, wide, pltpu.VMEM((width, 3 * ff_width), BF16)],
        17,
    )

    d_moves = start_scatter_ctx(d_mine, swap_core(d_send))
    padded = -(-3 * ff_width // 128) * 128
    (ffn_partial,) = call(
        ffn_weights,
        [shape((8, count, padded), BF16)],
        (owners,),
        (*second_pieces, cots, hidden, d_ffn),
        (),
        4 * 10**9,
        [wide, wide, pltpu.VMEM((length, ff_width), BF16), pltpu.VMEM((length, 2 * ff_width), BF16)],
        18,
    )
    ffn_sums = all_to_all(ffn_partial, "fsdp")
    d_moves, _ = stage(d_moves, ffn_partial)
    block_sum = lax.psum_scatter(block_parts, "ctx", scatter_dimension=0, tiled=False)
    block_out = (residual + block_sum.astype(F32)).astype(BF16)
    d_resid, d_attn, ffn_gain_part, *d_blocks = call(
        resid_backward,
        [rows, low_rows, shape((1, width), F32)] + [shape((4, count, q_width), BF16)] * 2,
        (place, owners),
        out_pairs,
        (*d_moves, residual, cot, ffn_gain[None]),
        3 * 10**8,
        [square, pltpu.VMEM((count, width), BF16)],
        4,
    )

    d_blocks = exchange_ctx(*d_blocks)
    d_blocks, d_attn = stage(d_blocks, d_attn)

    d_pieces = gather_ctx(d_attn)
    q_gain_part, k_gain_part, d_qkv, d_first_parts = call(
        attend_backward,
        [
            shape((head_size, 1), F32),
            shape((head_size, 1), F32),
            shape((length, qkv_width), BF16),
            shape((8, count, width), BF16),
        ],
        (owners,),
        (w_qkv,),
        (*d_blocks, *tables, *gains, qkv, lse),
        8 * 10**9,
        [pltpu.VMEM((qkv_width, length), F32), pltpu.VMEM((width, qkv_width), BF16)],
        1,
    )
    half, down = call(
        sum_ffn, [shape((count, 2 * ff_width), BF16), shape((count, ff_width), BF16)], (), (), (ffn_sums,), 10**6
    )
    d_qkv, d_pieces, half, down = stage(d_qkv, d_pieces, half, down)
    ffn_steps = (half, swap_dp(half), transpose_mesh(down), transpose_mesh(down, 1))
    d_first = lax.psum_scatter(d_first_parts, "ctx", scatter_dimension=0, tiled=False).astype(F32)
    (attn_partial,) = call(
        attend_weights,
        [shape((8, count, qkv_width + 128 + q_width), BF16)],
        (),
        (*first_pieces, *d_pieces, own, other, w_qkv, d_qkv),
        (attn_gain[None], ffn_gain_part, q_gain_part, k_gain_part),
        10**9,
        [wide, wide, pltpu.VMEM((length, q_width), BF16), head_rows, pltpu.VMEM((width, qkv_width), BF16)],
        26,
    )
    (joined,) = call(join_ffn, [shape((count, 3 * ff_width), BF16)], (), (), ffn_steps, 10**6)
    attn_partial, joined = stage(attn_partial, joined)

    ffn_moved = move_pieces(joined)
    attn_sums = all_to_all(attn_partial, "fsdp")
    d_from_first, _ = norm_back(d_first, first_hat, first_scale, attn_gain)
    grad_in = (d_resid + d_from_first).astype(BF16)
    attn_sums, grad_in, block_out = stage(attn_sums, grad_in, block_out)
    half, out = call(
        sum_attn, [shape((count, qkv_width + 128), BF16), shape((count, q_width), BF16)], (), (), (attn_sums,), 10**6
    )
    attn_steps = (half, swap_dp(half), transpose_mesh(out), transpose_mesh(out, 1))
    (joined,) = call(
        join_attn, [shape((count, qkv_width + 128 + q_width), BF16)], (), (), attn_steps, 10**6
    )
    joined, ffn_moved = stage(joined, ffn_moved)
    attn_moved = move_pieces(joined)
    grads_ffn = call(
        assemble_ffn,
        [shape((count, 8 * ff_width), F32)] * 2 + [shape((ff_width, width), F32)],
        (owners,),
        swap_pieces(ffn_moved),
        (),
        10**6,
        [pltpu.VMEM((8, count, 3 * ff_width), BF16)],
        8,
    )
    attn_moved, grads_ffn = stage(attn_moved, grads_ffn)
    grad_gate, grad_up, grad_down = grads_ffn
    grad_query, grad_key, grad_value, grad_out, totals = call(
        assemble_attn,
        [shape((count, width), F32)]
        + [shape((count, 8 * k_width), F32)] * 2
        + [shape((q_width, width), F32), shape((24, 128), F32)],
        (owners,),
        swap_pieces(attn_moved),
        (),
        10**6,
        [pltpu.VMEM((8, count, qkv_width + 128 + q_width), BF16)],
        8,
    )
    totals = totals.reshape(-1)
    grad_attn_gain = totals[:width]
    grad_ffn_gain = totals[width : 2 * width]
    grad_query_gain = totals[2 * width : 2 * width + head_size]
    grad_key_gain = totals[2 * width + head_size : 2 * width + 2 * head_size]
    return (
        block_out[None],
        grad_in[None],
        grad_attn_gain,
        grad_query,
        grad_key,
        grad_value,
        grad_query_gain,
        grad_key_gain,
        grad_out,
        grad_ffn_gain,
        grad_gate,
        grad_up,
        grad_down,
    )


def solution(mesh):
    in_specs = (
        P(("dp", "fsdp"), "ctx", None),
        P(("dp", "fsdp"), None),
        P(("dp", "fsdp"), "ctx", None),
        P(),
        P("fsdp", None),
        P("fsdp", None),
        P("fsdp", None),
        P(),
        P(),
        P("fsdp", None),
        P(),
        P("fsdp", None),
        P("fsdp", None),
        P("fsdp", None),
    )
    out_specs = (
        P(("dp", "fsdp"), "ctx", None),
        P(("dp", "fsdp"), "ctx", None),
        P(),
        P("fsdp", None),
        P("fsdp", None),
        P("fsdp", None),
        P(),
        P(),
        P("fsdp", None),
        P(),
        P("fsdp", None),
        P("fsdp", None),
        P("fsdp", None),
    )
    return jax.shard_map(body, mesh=mesh, in_specs=in_specs, out_specs=out_specs, check_vma=False)
```

```python
import math

import jax
import jax.numpy as jnp
from jax import lax
from jax.experimental import pallas as pl
from jax.experimental.pallas import tpu as pltpu
from jax.sharding import PartitionSpec as P

NORM_EPSILON = 1e-05
ROPE_BASE = 1000000.0
MASKED_SCORE = -1e30
BF16 = jnp.bfloat16
F32 = jnp.float32
STEPS = (0, -1, 1, 2)


def rms_scale(values):
    return lax.rsqrt(jnp.mean(values * values, axis=-1, keepdims=True) + NORM_EPSILON)


def rope_tables(places, head_size):
    half_width = head_size // 2
    pair_index = jnp.arange(half_width, dtype=F32)
    frequency = ROPE_BASE ** (-2.0 * pair_index / head_size)
    angles = frequency[:, None] * places.astype(F32)[None, :]
    return jnp.cos(angles), jnp.sin(angles)


def call(kernel, out_shapes, scalars, fetched, args, flops, scratch=(), copies=0):
    vmem = pl.BlockSpec(memory_space=pltpu.VMEM)
    operands = (*scalars, *fetched, *args)
    out_bytes = sum(math.prod(o.shape) * o.dtype.itemsize for o in out_shapes)
    in_bytes = sum(math.prod(a.shape) * a.dtype.itemsize for a in operands)
    return pl.pallas_call(
        kernel,
        out_shape=out_shapes,
        in_specs=[pl.BlockSpec(memory_space=pltpu.SMEM)] * len(scalars)
        + [pl.BlockSpec(memory_space=pl.ANY)] * len(fetched)
        + [vmem] * len(args),
        out_specs=[vmem] * len(out_shapes),
        scratch_shapes=list(scratch) + ([pltpu.SemaphoreType.DMA((copies,))] if copies else []),
        compiler_params=pltpu.CompilerParams(vmem_limit_bytes=60 * 2**20),
        cost_estimate=pl.CostEstimate(flops=flops, bytes_accessed=in_bytes + out_bytes, transcendentals=0),
    )(*operands)


def shape(dims, kind):
    return jax.ShapeDtypeStruct(dims, kind)


def head_forward(values, gain, cosine, sine):
    scale = lax.rsqrt(jnp.mean(values * values, axis=0, keepdims=True) + NORM_EPSILON)
    hat = values * scale
    normed = hat * gain
    half = values.shape[0] // 2
    front, back = normed[:half], normed[half:]
    rotated = jnp.concatenate([front * cosine - back * sine, back * cosine + front * sine], axis=0)
    return scale, hat, rotated


def head_backward(grads, hat, scale, gain, cosine, sine):
    half = grads.shape[0] // 2
    front, back = grads[:half], grads[half:]
    d_normed = jnp.concatenate([front * cosine + back * sine, back * cosine - front * sine], axis=0)
    scaled = d_normed * gain
    inner = jnp.mean(hat * scaled, axis=0, keepdims=True)
    return scale * (scaled - hat * inner), jnp.sum(d_normed * hat, axis=1, keepdims=True)


def norm_back(d_normed, normed_hat, scale_values, gain_vector):
    scaled = d_normed * gain_vector
    inner = jnp.mean(normed_hat * scaled, axis=-1, keepdims=True)
    return (scale_values * (scaled - normed_hat * inner), d_normed * normed_hat)


def mm(left, right):
    return jnp.dot(left, right, preferred_element_type=F32)


def mm_t(left, right):
    return lax.dot_general(left, right, (((1,), (1,)), ((), ())), preferred_element_type=F32)


def outer_sum(left, right):
    return lax.dot_general(left, right, (((0,), (0,)), ((), ())), preferred_element_type=F32)


def swap_core(value):
    return lax.ppermute(value, "ctx", [(i, i ^ 1) for i in range(8)])


def move_z(value, step):
    return lax.ppermute(value, "ctx", [(i, (i + 2 * step) % 8) for i in range(8)])


def gather_ctx(block):
    pieces = []
    for step in STEPS:
        mine = block if step == 0 else move_z(block, -step)
        pieces += [mine, swap_core(mine)]
    return pieces


def swap_pieces(moved):
    pieces = []
    for piece in moved:
        pieces += [piece, swap_core(piece)]
    return pieces


def start_scatter_ctx(mine, received):
    sums = [own + other.astype(F32) for own, other in zip(mine, received)]
    return [sums[0]] + [move_z(sums[slot].astype(BF16), STEPS[slot]) for slot in (3, 1, 2)]


def exchange_ctx(own, other):
    other = swap_core(other)
    out = [None] * 4
    for i, step in enumerate(STEPS):
        both = jnp.stack([own[i], other[i]])
        out[(0, 2, 1, 3)[i]] = move_z(both, step) if step else both
    return out


def stage(*values):
    return lax.optimization_barrier(values)


def transpose_mesh(value, flip=0):
    pairs = [
        ((d * 8 + c) * 8 + f, ((d ^ flip) * 8 + f) * 8 + c) for d in range(2) for c in range(8) for f in range(8)
    ]
    return lax.ppermute(value, ("dp", "ctx", "fsdp"), pairs)


def swap_dp(value):
    return lax.ppermute(value, "dp", [(0, 1), (1, 0)])


def move_y(value, step, flip=0):
    pairs = [(y * 2 + x, (y + step) % 4 * 2 + (x ^ flip)) for y in range(4) for x in range(2)]
    return lax.ppermute(value, "fsdp", pairs)


def pair_x(block):
    other = move_y(block, 0, 1)
    first = lax.axis_index("fsdp") % 2 == 0
    return jnp.concatenate([jnp.where(first, block, other), jnp.where(first, other, block)], axis=0)


def spread_y(pair):
    return [pair] + [move_y(pair, step) for step in (1, 3, 2)]


def fetch(pairs, sems, first=0):
    copies = [pltpu.make_async_copy(src, dst, sems.at[first + i]) for i, (src, dst) in enumerate(pairs)]
    for copy in copies:
        copy.start()
    return copies


def rows_of(pieces, ref):
    count = pieces[0].shape[0]
    return [(piece, ref.at[pl.ds(i * count, count)]) for i, piece in enumerate(pieces)]


def joined_y(place, pairs, ref):
    rows = pairs[0].shape[0]
    owners = [(place[0] + 4 - step) % 4 for step in (0, 1, 3, 2)]
    return [(pair, ref.at[pl.ds(pl.multiple_of(y * rows, rows), rows)]) for y, pair in zip(owners, pairs)]


def wait(copies):
    for copy in copies:
        copy.wait()


def all_to_all(blocks, axis):
    return lax.all_to_all(blocks, axis, split_axis=0, concat_axis=0, tiled=True)


def own_columns(weight, width, index):
    return lax.dynamic_slice_in_dim(weight, index * width, width, 1)


def attend_forward(*refs):
    pieces, w_whole, refs = refs[:8], refs[8], refs[9:]
    cos_ref, sin_ref, column_ref, row_ref, q_gain, k_gain = refs[:6]
    qkv_ref, lse_ref, own_ref, other_ref, x_ref, w_qkv, sems = refs[6:]
    w_copies = fetch([(w_whole, w_qkv)], sems, 8)
    x_copies = fetch(rows_of(pieces, x_ref), sems)
    wait(w_copies)
    length = qkv_ref.shape[1]
    count = length // 8
    head = q_gain.shape[0]
    for pair in range(4):
        wait(x_copies[2 * pair : 2 * pair + 2])
        lanes = slice(pair * 2 * count, (pair + 1) * 2 * count)
        qkv_ref[:, lanes] = jnp.transpose(mm(x_ref[lanes], w_qkv[...]))
    cosine, sine = cos_ref[...], sin_ref[...]
    queries = [
        head_forward(qkv_ref[h * head : (h + 1) * head], q_gain[...], cosine, sine)[2].astype(BF16) * BF16(head**-0.5)
        for h in range(2)
    ]
    key = jnp.transpose(head_forward(qkv_ref[2 * head : 3 * head], k_gain[...], cosine, sine)[2]).astype(BF16)
    value = qkv_ref[3 * head :].astype(BF16)
    width = column_ref.shape[1]
    for tile in range(length // width):
        lanes = slice(tile * width, (tile + 1) * width)
        allowed = column_ref[...] <= row_ref[:, lanes]
        outs = []
        for h in range(2):
            scores = jnp.where(allowed, mm(key, queries[h][:, lanes]), MASKED_SCORE)
            top = jnp.max(scores, axis=0, keepdims=True)
            weights = jnp.exp(scores - top)
            total = jnp.sum(weights, axis=0, keepdims=True)
            lse_ref[h : h + 1, lanes] = top + jnp.log(total)
            outs.append(mm(value, (weights * (1.0 / total)).astype(BF16)))
        mixed = jnp.transpose(jnp.concatenate(outs, axis=0)).astype(BF16)
        own_ref[tile] = mixed[:count]
        other_ref[tile] = mixed[count:]


def out_project(place, order, *refs):
    out_pairs, blocks, (tokens, gain, resid_ref, normed_ref, w_out, mixed_ref, sems) = refs[:4], refs[4:8], refs[8:]
    copies = fetch(joined_y(place, out_pairs, w_out), sems)
    count = blocks[0].shape[2]
    for i in range(8):
        lanes = pl.ds(pl.multiple_of(order[i] * count, count), count)
        mixed_ref[:, lanes] = blocks[i // 2][i % 2]
    wait(copies)
    resid = tokens[...].astype(F32) + mm(mixed_ref[...], w_out[...])
    resid_ref[...] = resid
    normed_ref[...] = (resid * rms_scale(resid) * gain[...]).astype(BF16)


def resid_backward(place, order, *refs):
    out_pairs, refs = refs[:4], refs[4:]
    total, move_a, move_b, move_c, resid_ref, cot_ref, gain_ref = refs[:7]
    d_resid_ref, d_attn_ref, gain_part_ref, own_ref, other_ref, w_out, d_mixed_ref, sems = refs[7:]
    copies = fetch(joined_y(place, out_pairs, w_out), sems)
    d_second = total[...] + move_a[...].astype(F32) + move_b[...].astype(F32) + move_c[...].astype(F32)
    resid = resid_ref[...]
    scale = rms_scale(resid)
    d_from, gain_part = norm_back(d_second, resid * scale, scale, gain_ref[...])
    gain_part_ref[...] = jnp.sum(gain_part, axis=0, keepdims=True)
    d_resid = cot_ref[...].astype(F32) + d_from
    d_resid_ref[...] = d_resid
    d_attn = d_resid.astype(BF16)
    d_attn_ref[...] = d_attn
    wait(copies)
    d_mixed_ref[...] = mm_t(d_attn, w_out[...]).astype(BF16)
    count = own_ref.shape[2]
    for i in range(8):
        lanes = pl.ds(pl.multiple_of(order[i] * count, count), count)
        (own_ref, other_ref)[i % 2][i // 2] = d_mixed_ref[:, lanes]


def attend_backward(*refs):
    order, w_whole, d_blocks, refs = refs[0], refs[1], refs[2:6], refs[6:]
    cos_ref, sin_ref, column_ref, row_ref, q_gain, k_gain, qkv_ref, lse_ref = refs[:8]
    q_gain_ref, k_gain_ref, d_low_ref, d_first_ref, d_qkv_ref, w_qkv, sems = refs[8:]
    copies = fetch([(w_whole, w_qkv)], sems)
    length = qkv_ref.shape[1]
    head = q_gain.shape[0]
    count = length // 8
    cosine, sine = cos_ref[...], sin_ref[...]
    scales, hats, queries = [], [], []
    for h in range(2):
        scale, hat, rotated = head_forward(qkv_ref[h * head : (h + 1) * head], q_gain[...], cosine, sine)
        scales.append(scale)
        hats.append(hat)
        queries.append(rotated.astype(BF16) * BF16(head**-0.5))
    k_scale, k_hat, rotated = head_forward(qkv_ref[2 * head : 3 * head], k_gain[...], cosine, sine)
    key_rows = rotated.astype(BF16)
    key = jnp.transpose(rotated).astype(BF16)
    value = jnp.transpose(qkv_ref[3 * head :]).astype(BF16)
    width = column_ref.shape[1]
    d_key = jnp.zeros((length, head), F32)
    d_value = jnp.zeros((length, head), F32)
    for tile in range(length // width):
        lanes = slice(tile * width, (tile + 1) * width)
        allowed = column_ref[...] <= row_ref[:, lanes]
        d_mixed = jnp.concatenate([d_blocks[tile][0], d_blocks[tile][1]], axis=0)
        d_mixed = jnp.transpose(d_mixed.astype(F32)).astype(BF16)
        for h in range(2):
            rows = slice(h * head, (h + 1) * head)
            query = queries[h][:, lanes]
            probs = jnp.where(allowed, jnp.exp(mm(key, query) - lse_ref[h : h + 1, lanes]), 0.0)
            d_probs = mm(value, d_mixed[rows])
            inner = jnp.sum(probs * d_probs, axis=0, keepdims=True)
            d_scores = (probs * (d_probs - inner)).astype(BF16)
            d_value += mm_t(probs.astype(BF16), d_mixed[rows])
            d_key += mm_t(d_scores, query)
            d_qkv_ref[rows, lanes] = mm(key_rows, d_scores) * head**-0.5
    for h in range(2):
        rows = slice(h * head, (h + 1) * head)
        d_query, gain_part = head_backward(d_qkv_ref[rows], hats[h], scales[h], q_gain[...], cosine, sine)
        d_qkv_ref[rows] = d_query
        if h == 0:
            q_gain_ref[...] = gain_part
        else:
            q_gain_ref[...] += gain_part
    d_keys, gain_part = head_backward(jnp.transpose(d_key), k_hat, k_scale, k_gain[...], cosine, sine)
    k_gain_ref[...] = gain_part
    d_qkv_ref[2 * head : 3 * head] = d_keys
    d_qkv_ref[3 * head :] = jnp.transpose(d_value)
    wait(copies)
    for tile in range(4):
        lanes = slice(tile * 2 * count, (tile + 1) * 2 * count)
        d_qkv = jnp.transpose(d_qkv_ref[:, lanes]).astype(BF16)
        d_low_ref[lanes] = d_qkv
        d_first = mm_t(d_qkv, w_qkv[...])
        d_first_ref[order[2 * tile]] = d_first[:count].astype(BF16)
        d_first_ref[order[2 * tile + 1]] = d_first[count:].astype(BF16)


def attend_weights(*refs):
    pieces, d_pieces, own, other, w_whole = refs[:8], refs[8:16], *refs[16:19]
    d_low, attn_gain, ffn_part, q_part, k_part = refs[19:24]
    out_ref, x_ref, d_ref, mixed_ref, d_low_ref, w_qkv, sems = refs[24:]
    count = pieces[0].shape[0]
    width = d_low_ref.shape[1]
    mixed = []
    for i in range(4):
        mixed += [(own.at[i], mixed_ref.at[pl.ds(2 * i * count, count)])]
        mixed += [(other.at[i], mixed_ref.at[pl.ds((2 * i + 1) * count, count)])]
    copies = fetch([(d_low, d_low_ref), *rows_of(pieces, x_ref), (w_whole, w_qkv)], sems)
    more = fetch([*mixed, *rows_of(d_pieces, d_ref)], sems, len(copies))
    wait(copies)
    grad_qkv = outer_sum(d_low_ref[...], x_ref[...])
    attn_part = jnp.sum(grad_qkv * jnp.transpose(w_qkv[...].astype(F32)), axis=0, keepdims=True) / attn_gain[...]
    grad_qkv = jnp.transpose(grad_qkv).astype(BF16)
    wait(more)
    grad_out = jnp.transpose(outer_sum(mixed_ref[...], d_ref[...])).astype(BF16)
    lines = [part[:, i * 128 : (i + 1) * 128] for part in (attn_part, ffn_part[...]) for i in range(8)]
    lines.append(jnp.concatenate([jnp.transpose(q_part[...]), jnp.transpose(k_part[...])], axis=1))
    gains = jnp.concatenate(lines + [jnp.zeros((7, 128), F32)], axis=0)
    high = gains.astype(BF16)
    low = (gains - high.astype(F32)).astype(BF16)
    gains = jnp.concatenate([high, low, jnp.zeros((count - 48, 128), BF16)], axis=0)
    for i in range(8):
        rows = slice(i * count, (i + 1) * count)
        out_ref[i, :, :width] = grad_qkv[rows]
        out_ref[i, :, width : width + 128] = gains
        out_ref[i, :, width + 128 :] = grad_out[rows]


def ffn(*refs):
    order, seconds, cots, weights = refs[0], refs[1:9], refs[9], refs[10]
    hidden_ref, d_ffn_ref, block_ref, d_send = refs[11:15]
    d_mine, (x_ref, cot_ref, w_ref, sems) = refs[15:19], refs[19:]
    copies = fetch([(weights, w_ref)], sems)
    loads = rows_of(seconds, x_ref) + rows_of([cots.at[order[i]] for i in range(8)], cot_ref)
    loads = fetch([loads[8 * j + 2 * g + i] for g in (3, 1, 2, 0) for j in (0, 1) for i in (0, 1)], sems, 1)
    wait(copies)
    width = hidden_ref.shape[1]
    count = seconds[0].shape[0]
    for group in (3, 1, 2, 0):
        rows = slice(2 * group * count, 2 * (group + 1) * count)
        wait(loads[:4])
        loads = loads[4:]
        x, cot = x_ref[rows], cot_ref[rows]
        both = mm(x, w_ref[:, : 2 * width])
        gate, up = both[:, :width], both[:, width:]
        sigmoid = 1.0 / (1.0 + jnp.exp(-gate))
        act = gate * sigmoid
        hidden = (act * up).astype(BF16)
        hidden_ref[rows] = hidden
        d_hidden = mm(cot, w_ref[:, 2 * width :])
        d_gate = d_hidden * up * sigmoid * (1.0 + gate * (1.0 - sigmoid))
        d_ffn = jnp.concatenate([d_gate, d_hidden * act], axis=1).astype(BF16)
        d_ffn_ref[rows] = d_ffn
        d_second = mm_t(d_ffn, w_ref[:, : 2 * width])
        d_mine[group][...] = d_second[:count]
        d_send[group] = d_second[count:].astype(BF16)
        out = mm_t(hidden, w_ref[:, 2 * width :])
        block_ref[order[2 * group]] = out[:count].astype(BF16)
        block_ref[order[2 * group + 1]] = out[count:].astype(BF16)


def ffn_weights(*refs):
    order, seconds, cots, hidden, d_ffn = refs[0], refs[1:9], *refs[9:12]
    out_ref, x_ref, cot_ref, hidden_ref, d_ffn_ref, sems = refs[12:]
    count = seconds[0].shape[0]
    copies = fetch([(d_ffn, d_ffn_ref), *rows_of(seconds, x_ref)], sems)
    more = fetch([(hidden, hidden_ref), *rows_of([cots.at[order[i]] for i in range(8)], cot_ref)], sems, 9)
    for left_ref, right_ref, columns in ((x_ref, d_ffn_ref, 0), (cot_ref, hidden_ref, d_ffn_ref.shape[1])):
        wait(more if columns else copies)
        width = right_ref.shape[1]
        for pair in range(4):
            both = outer_sum(left_ref[:, 2 * pair * count : 2 * (pair + 1) * count], right_ref[...]).astype(BF16)
            out_ref[2 * pair, :, columns : columns + width] = both[:count]
            out_ref[2 * pair + 1, :, columns : columns + width] = both[count:]
    used = d_ffn_ref.shape[1] + hidden_ref.shape[1]
    out_ref[:, :, used:] = jnp.zeros((8, count, out_ref.shape[2] - used), BF16)


def sum_ffn(parts, gate_up_ref, down_ref):
    width = gate_up_ref.shape[1]
    total = sum(parts[i].astype(F32) for i in range(8)).astype(BF16)
    gate_up_ref[...] = total[:, :width]
    down_ref[...] = total[:, width : width + down_ref.shape[1]]


def sum_attn(parts, first_ref, out_ref):
    count = out_ref.shape[0]
    width = first_ref.shape[1] - 128
    total = sum(parts[i].astype(F32) for i in range(8))
    first_ref[:, :width] = total[:, :width].astype(BF16)
    pack_gains(first_ref, width, total[:24, width : width + 128] + total[24:48, width : width + 128])
    out_ref[...] = total[:, width + 128 :].astype(BF16)


def pack_gains(ref, width, gains):
    high = gains.astype(BF16)
    low = (gains - high.astype(F32)).astype(BF16)
    rest = jnp.zeros((ref.shape[0] - 48, 128), BF16)
    ref[:, width : width + 128] = jnp.concatenate([high, low, rest], axis=0)


def join_ffn(own, other, down, down_other, out_ref):
    width = own.shape[1]
    out_ref[:, :width] = (own[...].astype(F32) + other[...].astype(F32)).astype(BF16)
    out_ref[:, width:] = (down[...].astype(F32) + down_other[...].astype(F32)).astype(BF16)


def join_attn(own, other, out, out_other, out_ref):
    width = own.shape[1] - 128
    total = own[...].astype(F32) + other[...].astype(F32)
    out_ref[:, :width] = total[:, :width].astype(BF16)
    pack_gains(out_ref, width, total[:24, width:] + total[24:48, width:])
    out_ref[:, width + 128 :] = (out[...].astype(F32) + out_other[...].astype(F32)).astype(BF16)


def assemble_ffn(*refs):
    order, pieces, (gate_ref, up_ref, down_ref, held, sems) = refs[0], refs[1:9], refs[9:]
    width = down_ref.shape[0]
    count = pieces[0].shape[0]
    wait(fetch([(pieces[i], held.at[order[i]]) for i in range(8)], sems))
    for owner in range(8):
        columns = slice(owner * width, (owner + 1) * width)
        gate_ref[:, columns] = held[owner, :, :width].astype(F32)
        up_ref[:, columns] = held[owner, :, width : 2 * width].astype(F32)
        down = held[owner, :, 2 * width :].astype(F32)
        down_ref[:, owner * count : (owner + 1) * count] = jnp.transpose(down)


def assemble_attn(*refs):
    order, pieces, (query_ref, key_ref, value_ref, out_ref, gains_ref, held, sems) = refs[0], refs[1:9], refs[9:]
    count = pieces[0].shape[0]
    half = count // 2
    wait(fetch([(pieces[i], held.at[order[i]]) for i in range(8)], sems))
    gains = jnp.zeros(gains_ref.shape, F32)
    for owner in range(8):
        columns = slice(owner * count, (owner + 1) * count)
        narrow = slice(owner * half, (owner + 1) * half)
        part = held[owner].astype(F32)
        query_ref[:, columns] = part[:, :count]
        key_ref[:, narrow] = part[:, count : count + half]
        value_ref[:, narrow] = part[:, count + half : 2 * count]
        out_ref[:, columns] = jnp.transpose(part[:, 3 * count :])
        gains += part[:24, 2 * count : 3 * count] + part[24:48, 2 * count : 3 * count]
    gains_ref[...] = gains


def body(
    hidden_in,
    positions,
    cotangent,
    attn_gain,
    w_query,
    w_key,
    w_value,
    query_gain,
    key_gain,
    w_out,
    ffn_gain,
    w_gate,
    w_up,
    w_down,
):
    ctx = lax.axis_index("ctx")
    tokens = hidden_in[0].astype(F32)
    count, width = tokens.shape
    head_size = query_gain.shape[0]
    q_width = w_query.shape[1] // 8
    k_width = w_key.shape[1] // 8
    ff_width = w_gate.shape[1] // 8

    z_index, core = ctx // 2, ctx % 2
    owners = jnp.stack(
        [((z_index + step) % 4) * 2 + (core ^ flip) for step in STEPS for flip in (0, 1)]
    )
    places = positions[0].reshape(8, count)[owners].reshape(8 * count)
    length = 8 * count
    cosine_table, sine_table = rope_tables(places, head_size)
    column = jnp.broadcast_to(places[:, None], (length, 2 * count))
    row = places[None]
    gains = (query_gain[:, None], key_gain[:, None])
    tables = (cosine_table, sine_table, column, row)
    block = shape((count, q_width), BF16)
    low_rows, rows = shape((count, width), BF16), shape((count, width), F32)
    qkv_width = q_width + 2 * k_width

    place = jnp.stack([lax.axis_index("fsdp") // 2, lax.axis_index("fsdp") % 2])
    wide, head_rows = pltpu.VMEM((length, width), BF16), pltpu.VMEM((length, qkv_width), BF16)

    first_scale = rms_scale(tokens)
    first_hat = tokens * first_scale
    first_normed = (first_hat * attn_gain).astype(BF16)
    first_moved = [move_z(first_normed, -step) if step else first_normed for step in STEPS]
    qkv_block = jnp.concatenate(
        [own_columns(w_query, q_width, ctx), own_columns(w_key, k_width, ctx), own_columns(w_value, k_width, ctx)],
        axis=1,
    )
    w_qkv = all_to_all(jnp.broadcast_to(qkv_block[None], (8, *qkv_block.shape)), "fsdp").reshape(width, qkv_width)
    out_pair = pair_x(w_out)
    cot = cotangent[0]
    cot_copies = jnp.broadcast_to(cot[None], (8, count, width))
    down_chunk = transpose_mesh(jnp.transpose(own_columns(w_down, width // 8, ctx)))
    ffn_block = jnp.concatenate(
        [own_columns(w_gate, ff_width, ctx), own_columns(w_up, ff_width, ctx), down_chunk], axis=1
    )
    ffn_block, w_qkv = stage(ffn_block, w_qkv)
    ffn_rows = lax.all_gather(ffn_block, "fsdp", axis=0, tiled=True)
    w_qkv, first_moved, cot_copies = stage(w_qkv, first_moved, cot_copies)
    cots = all_to_all(cot_copies, "ctx")
    first_pieces = swap_pieces(first_moved)
    first_pieces, w_qkv, tables, out_pair = stage(first_pieces, w_qkv, tables, out_pair)

    out_pairs = spread_y(out_pair)
    qkv, lse, own, other = call(
        attend_forward,
        [shape((qkv_width, length), F32), shape((8, length), F32)] + [shape((4, count, q_width), BF16)] * 2,
        (),
        (*first_pieces, w_qkv),
        (*tables, *gains),
        4 * 10**9,
        [wide, pltpu.VMEM((width, qkv_width), BF16)],
        9,
    )

    mixed_blocks = exchange_ctx(own, other)
    mixed_blocks, out_pairs, cots = stage(mixed_blocks, out_pairs, cots)
    square = pltpu.VMEM((width, width), BF16)
    residual, second_normed = call(
        out_project,
        [rows, low_rows],
        (place, owners),
        out_pairs,
        (*mixed_blocks, hidden_in[0], ffn_gain[None]),
        3 * 10**8,
        [square, pltpu.VMEM((count, width), BF16)],
        4,
    )

    second_pieces = gather_ctx(second_normed)
    hidden_shape, d_ffn_shape = shape((length, ff_width), BF16), shape((length, 2 * ff_width), BF16)
    hidden, d_ffn, block_parts, d_send, *d_mine = call(
        ffn,
        [hidden_shape, d_ffn_shape, shape((8, count, width), BF16), shape((4, count, width), BF16)] + [rows] * 4,
        (owners,),
        (*second_pieces, cots, ffn_rows),
        (),
        8 * 10**9,
        [wide, wide, pltpu.VMEM((width, 3 * ff_width), BF16)],
        17,
    )

    d_moves = start_scatter_ctx(d_mine, swap_core(d_send))
    padded = -(-3 * ff_width // 128) * 128
    (ffn_partial,) = call(
        ffn_weights,
        [shape((8, count, padded), BF16)],
        (owners,),
        (*second_pieces, cots, hidden, d_ffn),
        (),
        4 * 10**9,
        [wide, wide, pltpu.VMEM((length, ff_width), BF16), pltpu.VMEM((length, 2 * ff_width), BF16)],
        18,
    )
    ffn_sums = all_to_all(ffn_partial, "fsdp")
    d_moves, _ = stage(d_moves, ffn_partial)
    block_sum = lax.psum_scatter(block_parts, "ctx", scatter_dimension=0, tiled=False)
    block_out = (residual + block_sum.astype(F32)).astype(BF16)
    d_resid, d_attn, ffn_gain_part, *d_blocks = call(
        resid_backward,
        [rows, low_rows, shape((1, width), F32)] + [shape((4, count, q_width), BF16)] * 2,
        (place, owners),
        out_pairs,
        (*d_moves, residual, cot, ffn_gain[None]),
        3 * 10**8,
        [square, pltpu.VMEM((count, width), BF16)],
        4,
    )

    d_blocks = exchange_ctx(*d_blocks)
    d_blocks, d_attn = stage(d_blocks, d_attn)

    d_pieces = gather_ctx(d_attn)
    q_gain_part, k_gain_part, d_qkv, d_first_parts = call(
        attend_backward,
        [
            shape((head_size, 1), F32),
            shape((head_size, 1), F32),
            shape((length, qkv_width), BF16),
            shape((8, count, width), BF16),
        ],
        (owners,),
        (w_qkv,),
        (*d_blocks, *tables, *gains, qkv, lse),
        8 * 10**9,
        [pltpu.VMEM((qkv_width, length), F32), pltpu.VMEM((width, qkv_width), BF16)],
        1,
    )
    half, down = call(
        sum_ffn, [shape((count, 2 * ff_width), BF16), shape((count, ff_width), BF16)], (), (), (ffn_sums,), 10**6
    )
    d_qkv, d_pieces, half, down = stage(d_qkv, d_pieces, half, down)
    ffn_steps = (half, swap_dp(half), transpose_mesh(down), transpose_mesh(down, 1))
    d_first = lax.psum_scatter(d_first_parts, "ctx", scatter_dimension=0, tiled=False).astype(F32)
    (attn_partial,) = call(
        attend_weights,
        [shape((8, count, qkv_width + 128 + q_width), BF16)],
        (),
        (*first_pieces, *d_pieces, own, other, w_qkv, d_qkv),
        (attn_gain[None], ffn_gain_part, q_gain_part, k_gain_part),
        10**9,
        [wide, wide, pltpu.VMEM((length, q_width), BF16), head_rows, pltpu.VMEM((width, qkv_width), BF16)],
        26,
    )
    attn_partial, ffn_steps = stage(attn_partial, ffn_steps)

    attn_sums = all_to_all(attn_partial, "fsdp")
    (joined,) = call(
        join_ffn,
        [shape((count, 3 * ff_width), BF16)],
        (),
        (),
        ffn_steps,
        10**6,
    )
    ffn_parts = gather_ctx(joined)
    half, out = call(
        sum_attn, [shape((count, qkv_width + 128), BF16), shape((count, q_width), BF16)], (), (), (attn_sums,), 10**6
    )
    (joined,) = call(
        join_attn,
        [shape((count, qkv_width + 128 + q_width), BF16)],
        (),
        (),
        (half, swap_dp(half), transpose_mesh(out), transpose_mesh(out, 1)),
        10**6,
    )
    attn_parts = gather_ctx(joined)
    d_from_first, _ = norm_back(d_first, first_hat, first_scale, attn_gain)
    grad_in = (d_resid + d_from_first).astype(BF16)
    grad_gate, grad_up, grad_down = call(
        assemble_ffn,
        [shape((count, 8 * ff_width), F32)] * 2 + [shape((ff_width, width), F32)],
        (owners,),
        ffn_parts,
        (),
        10**6,
        [pltpu.VMEM((8, count, 3 * ff_width), BF16)],
        8,
    )
    grad_query, grad_key, grad_value, grad_out, totals = call(
        assemble_attn,
        [shape((count, width), F32)] + [shape((count, 8 * k_width), F32)] * 2 + [shape((q_width, width), F32), shape((24, 128), F32)],
        (owners,),
        attn_parts,
        (),
        10**6,
        [pltpu.VMEM((8, count, qkv_width + 128 + q_width), BF16)],
        8,
    )
    totals = totals.reshape(-1)
    grad_attn_gain = totals[:width]
    grad_ffn_gain = totals[width : 2 * width]
    grad_query_gain = totals[2 * width : 2 * width + head_size]
    grad_key_gain = totals[2 * width + head_size : 2 * width + 2 * head_size]
    return (
        block_out[None],
        grad_in[None],
        grad_attn_gain,
        grad_query,
        grad_key,
        grad_value,
        grad_query_gain,
        grad_key_gain,
        grad_out,
        grad_ffn_gain,
        grad_gate,
        grad_up,
        grad_down,
    )


def solution(mesh):
    in_specs = (
        P(("dp", "fsdp"), "ctx", None),
        P(("dp", "fsdp"), None),
        P(("dp", "fsdp"), "ctx", None),
        P(),
        P("fsdp", None),
        P("fsdp", None),
        P("fsdp", None),
        P(),
        P(),
        P("fsdp", None),
        P(),
        P("fsdp", None),
        P("fsdp", None),
        P("fsdp", None),
    )
    out_specs = (
        P(("dp", "fsdp"), "ctx", None),
        P(("dp", "fsdp"), "ctx", None),
        P(),
        P("fsdp", None),
        P("fsdp", None),
        P("fsdp", None),
        P(),
        P(),
        P("fsdp", None),
        P(),
        P("fsdp", None),
        P("fsdp", None),
        P("fsdp", None),
    )
    return jax.shard_map(body, mesh=mesh, in_specs=in_specs, out_specs=out_specs, check_vma=False)
```
